512 devices in a mesh: ctx: 64 (over z, x, core), head: 8 (over y).
Axes of the slice: x: 4, y: 8, z: 8, core: 2. Of those that a mesh axis runs over, the one named last changes fastest.
Arguments:
- query_rows: bfloat16 [8192, 2048], P('ctx', 'head'), may hold values from -120 to 120
- key_rows: bfloat16 [8192, 2048], P('ctx', 'head'), may hold values from -4 to 4
- value_rows: bfloat16 [8192, 2048], P('ctx', 'head'), may hold values from -6 to 6
- reflect_dirs: bfloat16 [8192, 2048], P('ctx', 'head'), may hold values from -6 to 6
- reflect_rates: float32 [16, 8192], P('head', 'ctx'), may hold values from 0.02 to 1.98
- norm_gain: float32 [2048], P('head'), may hold values from 0.5 to 1.5
- doc_lengths: int32 [32], replicated, may hold values from 1 to 512, 8192 in all
- out_cotangent: bfloat16 [8192, 2048], P('ctx', 'head'), may hold values from -6 to 6
Outputs:
- normed_out: bfloat16 [8192, 2048], P('ctx', 'head')
- grad_query: bfloat16 [8192, 2048], P('ctx', 'head')
- grad_key: bfloat16 [8192, 2048], P('ctx', 'head')
- grad_value: bfloat16 [8192, 2048], P('ctx', 'head')
- grad_reflect: bfloat16 [8192, 2048], P('ctx', 'head')
- grad_rate: float32 [16, 8192], P('head', 'ctx')
- grad_gain: float32 [2048], P('head')
The draws below stay inside these ranges and needn't reach their ends.
Inputs may be any that keep to these rules, and one draw needn't show every extreme that they name: `doc_lengths`: every document has at most 512 tokens and one has exactly that many; the lengths sum to 8192.
All inputs are finite; a program needn't handle non-finite values.
Results may differ from the reference program's by a relative error of at most 0.018.
Values may be sent and summed in bfloat16 or wider, within the bound.
No kernel may reach another device: no remote copies, remote signals or barrier semaphores. Data moves between devices by JAX's collectives and lax.ppermute only.
A program may use at most 128 MiB of HBM per device.

```python
import math
import jax
import jax.numpy as jnp
import numpy as np
from jax import lax

DH = 128
TOK_DEV = 128
WIN = 4
HEADS = 16
TOKENS = 8192
DOCS = 32
N_CTX = 64


def shared_keys(key):
    return jax.random.truncated_normal(jax.random.fold_in(key, 101), -4.0, 4.0, (TOKENS, HEADS * DH), jnp.float32)


def draw_key_rows(key, part):
    return shared_keys(key).astype(jnp.bfloat16)


def draw_query_rows(key, part):
    drawn_rows = jax.random.truncated_normal(jax.random.fold_in(key, 202), -4.0, 4.0, (TOKENS, HEADS * DH), jnp.float32)
    return drawn_rows.astype(jnp.bfloat16)


def draw_reflect_rates(key, part):
    side = jax.random.randint(jax.random.fold_in(key, 301), (HEADS, TOKENS), 0, 2).astype(jnp.float32)
    offset_drawn = jax.random.uniform(jax.random.fold_in(key, 302), (HEADS, TOKENS), jnp.float32, 0.0, 1.0)
    offset_drawn = 0.1 * offset_drawn
    low_rate = 0.02 + offset_drawn
    high_rate = 1.98 - offset_drawn
    return side * high_rate + (1.0 - side) * low_rate


def shard_levels(key, shape, cuts, least, largest):
    level = 1.0
    for axis_at, blocks in cuts:
        heights = jax.random.uniform(jax.random.fold_in(jax.random.fold_in(key, 6), axis_at), (blocks,), jnp.float32, least / len(cuts), largest / len(cuts))
        level = level * jnp.repeat(jnp.exp(heights), shape[axis_at] // blocks).reshape((-1,) + (1,) * (len(shape) - 1 - axis_at))
    return level


def profile(count, total, reach, slope):
    loads = [(1 << 20) // math.isqrt(grade ** slope) + 1 for grade in range(2, count + 1)]
    spare, counts = total - reach - (count - 1), [1] * (count - 1)
    while spare > 0:
        free = [i for i in range(count - 1) if counts[i] < reach]
        mass, left = sum([loads[i] for i in free]), spare
        for i in free:
            more = min(reach - counts[i], max(1, left * loads[i] // mass), spare)
            counts[i] = counts[i] + more
            spare = spare - more
    return np.array([reach] + counts)


def ragged_sizes(rng, amount, total, limit, lean):
    if amount == 2:
        one = jax.random.randint(rng, (), max(1, total - limit), min(limit, total - 1) + 1)
        return jnp.stack([one, total - one])
    sizes = jnp.asarray(profile(amount, total, limit, lean), jnp.int32)
    pairs = (amount - 1) // 2
    source_of, sink = sizes[1:1 + 2 * pairs:2], sizes[2:2 + 2 * pairs:2]
    slack = jnp.minimum(source_of - 1, limit - sink)
    passed = jax.random.randint(jax.random.fold_in(rng, 1), (pairs,), 0, 1 << 20) % (slack + 1)
    sizes = sizes.at[1:1 + 2 * pairs:2].set(source_of - passed).at[2:2 + 2 * pairs:2].set(sink + passed)
    return sizes[jax.random.permutation(jax.random.fold_in(rng, 2), amount)]


def normal_values(key, extent, deviation, bound, split=(), kind=jnp.bfloat16):
    loudness = shard_levels(key, extent, split, -0.22, 0.18) if split else 1.0
    entries = jax.random.normal(key, extent, jnp.float32) * deviation * loudness
    return jnp.minimum(jnp.maximum(entries, -bound), bound).astype(kind)


def setup_inputs(seed: int = 0) -> dict:
    splits = jax.random.split(jax.random.key(seed), 9)
    return {
        "query_rows": draw_query_rows(jax.random.fold_in(splits[8], 71), 0),
        "key_rows": draw_key_rows(jax.random.fold_in(splits[8], 71), 0),
        "value_rows": normal_values(splits[2], (TOKENS, HEADS * DH), 1.0, 6.0, ((0, 64), (1, 8))),
        "reflect_dirs": normal_values(splits[3], (TOKENS, HEADS * DH), 1.0, 6.0, ((0, 64), (1, 8))),
        "reflect_rates": draw_reflect_rates(jax.random.fold_in(splits[8], 71), 0),
        "norm_gain": jnp.clip(1.0 + 0.1 * jax.random.normal(splits[5], (HEADS * DH,), jnp.float32), 0.5, 1.5),
        "doc_lengths": ragged_sizes(splits[6], DOCS, TOKENS, WIN * TOK_DEV, 2).astype(jnp.int32),
        "out_cotangent": normal_values(splits[7], (TOKENS, HEADS * DH), 1.0, 6.0, ((0, 64), (1, 8))),
    }


NEG_FILL = -1e+30
EPSILON = 1e-06

def exact_dot(left, right):
    return jnp.dot(left, right, precision=lax.Precision.HIGHEST)

def exact_sum(form, left, right):
    return jnp.einsum(form, left, right, precision=lax.Precision.HIGHEST)

def rounded(tensor):
    half_rounded = tensor.astype(jnp.bfloat16)
    return lax.optimization_barrier(half_rounded).astype(jnp.float32)

def unit_lower_inverse(matrix):
    length_rows = matrix.shape[0]
    padded_size = 1 << (length_rows - 1).bit_length()
    extra = padded_size - length_rows
    full = jnp.eye(padded_size, dtype=jnp.float32) + jnp.pad(matrix - jnp.eye(length_rows, dtype=jnp.float32), ((0, extra), (0, extra)))
    inverse_blocks = jnp.ones((padded_size, 1, 1), jnp.float32)
    block_width = 1
    while block_width < padded_size:
        groups = padded_size // (2 * block_width)
        diagonal_blocks = jnp.einsum('aibj,ab->aij', full.reshape(groups, 2 * block_width, groups, 2 * block_width), jnp.eye(groups, dtype=jnp.float32), precision=lax.Precision.HIGHEST)
        paired = inverse_blocks.reshape(groups, 2, block_width, block_width)
        first_inverse = paired[:, 0]
        second_inverse = paired[:, 1]
        coupling = diagonal_blocks[:, block_width:, :block_width]
        corner_block = -exact_sum('aij,ajk->aik', second_inverse, exact_sum('aij,ajk->aik', coupling, first_inverse))
        upper_rows = jnp.concatenate([first_inverse, jnp.zeros_like(first_inverse)], axis=2)
        lower_rows = jnp.concatenate([corner_block, second_inverse], axis=2)
        inverse_blocks = jnp.concatenate([upper_rows, lower_rows], axis=1)
        block_width = 2 * block_width
    return inverse_blocks[0][:length_rows, :length_rows]

def shard_prepare(query_block, key_block, mixer_block, rate_block):
    query_float = query_block.astype(jnp.float32)
    key_float = key_block.astype(jnp.float32)
    mixer_float = mixer_block.astype(jnp.float32)
    direction = mixer_float * lax.rsqrt(lax.optimization_barrier(jnp.sum(mixer_float * mixer_float, axis=1, keepdims=True)) + EPSILON)
    length = direction.shape[0]
    identity = jnp.eye(length, dtype=jnp.float32)
    gram_rates = rate_block[:, None] * exact_dot(direction, direction.T)
    lower_mat = identity + jnp.tril(gram_rates, -1)
    upper_mat = identity + jnp.triu(gram_rates, 1)
    lower_inverse = unit_lower_inverse(lower_mat)
    upper_inverse = unit_lower_inverse(upper_mat.T).T
    key_coef = exact_dot(lower_inverse, jnp.tril(rate_block[:, None] * exact_dot(direction, key_float.T), -1))
    query_dir = exact_dot(query_float, direction.T)
    intra_raw = jnp.tril(exact_dot(query_float, key_float.T) - exact_dot(jnp.tril(query_dir), key_coef))
    key_end = key_float - exact_dot(key_coef.T, direction)
    query_coef = exact_dot(upper_inverse, jnp.triu(rate_block[:, None] * query_dir.T))
    query_frame = query_float - exact_dot(query_coef.T, direction)
    applied = exact_dot(lower_inverse, rate_block[:, None] * direction)
    transform = jnp.eye(direction.shape[1], dtype=jnp.float32) - exact_dot(direction.T, applied)
    return (intra_raw, query_frame, key_end, transform)

def document_of(positions, doc_ends):
    return lax.optimization_barrier(jnp.sum((doc_ends[None, :] <= positions[:, None]).astype(jnp.int32), axis=1))

def shift_earlier(tensor, offset):
    padding = jnp.zeros((offset,) + tensor.shape[1:], tensor.dtype)
    return jnp.concatenate([padding, tensor[:-offset]], axis=0)

def shift_later(tensor, offset):
    padding = jnp.zeros((offset,) + tensor.shape[1:], tensor.dtype)
    return jnp.concatenate([tensor[offset:], padding], axis=0)

def head_state(head_pack, seen_masks):
    query_head, key_head, value_head, mixer_head, rate_head = head_pack
    prepared, prepare_back = jax.vjp(jax.vmap(shard_prepare), query_head, key_head, mixer_head, rate_head)
    intra_raw, query_frame, key_end, transform = prepared
    score_scale = DH ** (-0.5)
    left_ops = []
    right_ops = []
    current = query_frame
    for offset in range(1, WIN + 1):
        left_ops.append(current)
        right_ops.append(shift_earlier(key_end, offset))
        current = exact_sum('ntd,nde->nte', current, shift_earlier(transform, offset))
    blocks = [intra_raw] + [exact_sum('ntd,nud->ntu', left_ops[slot_index], right_ops[slot_index]) for slot_index in range(WIN)]
    scores = jnp.where(seen_masks, jnp.concatenate(blocks, axis=2) * score_scale, NEG_FILL)
    row_max = lax.optimization_barrier(jnp.max(scores, axis=2, keepdims=True))
    exp_weights = jnp.where(seen_masks, jnp.exp(scores - row_max), 0.0)
    prob_total = lax.optimization_barrier(jnp.sum(exp_weights, axis=2))
    values = jnp.concatenate([value_head] + [shift_earlier(value_head, offset) for offset in range(1, WIN + 1)], axis=1).astype(jnp.float32)
    numerator = jnp.einsum('ntu,nud->ntd', rounded(exp_weights), values)
    attended_heads = numerator / prob_total[:, :, None]
    return (attended_heads, prob_total, exp_weights, values, left_ops, right_ops, transform, prepare_back)

def head_grads(head_pack, grad_heads, seen_masks):
    attended_heads, prob_total, exp_weights, values, left_ops, right_ops, transform, prepare_back = head_state(head_pack, seen_masks)
    score_scale = DH ** (-0.5)
    grad_scaled = rounded(grad_heads / prob_total[:, :, None])
    row_delta = lax.optimization_barrier(jnp.sum(grad_heads * attended_heads, axis=2)) / prob_total
    value_slots = jnp.einsum('ntu,ntd->nud', rounded(exp_weights), grad_scaled)
    through = jnp.einsum('ntd,nud->ntu', grad_scaled, values)
    score_grad = exp_weights * (through - row_delta[:, :, None]) * score_scale
    frame_grad = jnp.zeros_like(left_ops[0])
    key_grad = jnp.zeros_like(right_ops[0])
    trans_grad = jnp.zeros_like(transform)
    for offset in range(WIN, 0, -1):
        block_grad = score_grad[:, :, offset * TOK_DEV:(offset + 1) * TOK_DEV]
        trans_grad = trans_grad + shift_later(exact_sum('ntd,nte->nde', left_ops[offset - 1], frame_grad), offset)
        key_grad = key_grad + shift_later(exact_sum('ntu,ntd->nud', block_grad, left_ops[offset - 1]), offset)
        frame_grad = exact_sum('ntu,nud->ntd', block_grad, right_ops[offset - 1]) + exact_sum('nte,nde->ntd', frame_grad, shift_earlier(transform, offset))
    value_grad = value_slots[:, :TOK_DEV]
    for offset in range(1, WIN + 1):
        value_grad = value_grad + shift_later(value_slots[:, offset * TOK_DEV:(offset + 1) * TOK_DEV], offset)
    query_grad, key_in_grad, mixer_grad, rate_grad = prepare_back((score_grad[:, :, :TOK_DEV], frame_grad, key_grad, trans_grad))
    return (query_grad, key_in_grad, mixer_grad, rate_grad, value_grad.astype(jnp.bfloat16))

def reference(query_rows, key_rows, value_rows, reflect_dirs, reflect_rates, norm_gain, doc_lengths, out_cotangent):

    def by_head(tensor):
        return tensor.reshape(N_CTX, TOK_DEV, HEADS, DH).transpose(2, 0, 1, 3)

    def from_head(tensor):
        return tensor.transpose(1, 2, 0, 3).reshape(TOKENS, HEADS * DH)
    positions = jnp.arange(TOKENS, dtype=jnp.int32).reshape(N_CTX, TOK_DEV)
    doc_ends = jnp.cumsum(doc_lengths)
    query_doc = document_of(positions.reshape(-1), doc_ends).reshape(N_CTX, TOK_DEV)
    mask_list = [(positions[:, :, None] >= positions[:, None, :]) & (query_doc[:, :, None] == query_doc[:, None, :])]
    for offset in range(1, WIN + 1):
        key_pos = positions - offset * TOK_DEV
        key_doc = document_of(key_pos.reshape(-1), doc_ends).reshape(N_CTX, TOK_DEV)
        mask_list.append((key_pos[:, None, :] >= 0) & (query_doc[:, :, None] == key_doc[:, None, :]))
    seen_masks = jnp.concatenate(mask_list, axis=2)
    packs = (by_head(query_rows), by_head(key_rows), by_head(value_rows), by_head(reflect_dirs), reflect_rates.reshape(HEADS, N_CTX, TOK_DEV))
    outputs = lax.map(lambda head_pack: head_state(head_pack, seen_masks)[0], packs)
    attended = from_head(outputs)
    square = lax.optimization_barrier(jnp.sum(attended * attended, axis=1))
    inverse_rms = lax.rsqrt(square / (HEADS * DH) + EPSILON)
    normed_out = (attended * inverse_rms[:, None] * norm_gain[None, :]).astype(jnp.bfloat16)
    cotangent = out_cotangent.astype(jnp.float32)
    weighted = cotangent * norm_gain[None, :]
    inner_sum = lax.optimization_barrier(jnp.sum(weighted * attended, axis=1))
    grad_att = weighted * inverse_rms[:, None] - attended * (inverse_rms ** 3 * inner_sum / (HEADS * DH))[:, None]
    grad_gain = lax.optimization_barrier(jnp.sum(cotangent * attended * inverse_rms[:, None], axis=0))
    grads = lax.map(lambda head_pack: head_grads(head_pack[:5], head_pack[5], seen_masks), packs + (by_head(grad_att),))
    query_grad, key_in_grad, mixer_grad, rate_grad, value_grad = grads
    return (normed_out, from_head(query_grad), from_head(key_in_grad), from_head(value_grad), from_head(mixer_grad), rate_grad.reshape(HEADS, TOKENS), grad_gain)
```

```python
import functools

import jax
import jax.numpy as jnp
from jax import lax
from jax.experimental import pallas as pl
from jax.experimental.pallas import tpu as pltpu
from jax.sharding import PartitionSpec as P

DH = 128
WIN = 4
NEG_FILL = -1e30
EPSILON = 1e-06
F32 = jnp.float32
BF16 = jnp.bfloat16
VMEM_LIMIT = 48 * 1024 * 1024


def mm(left, right, form="nn"):
    lhs = 0 if form[0] == "t" else 1
    rhs = 1 if form[1] == "t" else 0
    return lax.dot_general(
        left.astype(BF16), right.astype(BF16), (((lhs,), (rhs,)), ((), ())), preferred_element_type=F32
    )


def split(value):
    high = value.astype(BF16)
    low = (value - high.astype(F32)).astype(BF16)
    return high, low


def mm3(left, right):
    lh, ll = split(left)
    rh, rl = split(right)
    return mm(lh, rh) + (mm(lh, rl) + mm(ll, rh))


def grids(size):
    rows = lax.broadcasted_iota(jnp.int32, (size, size), 0)
    cols = lax.broadcasted_iota(jnp.int32, (size, size), 1)
    return rows, cols


def to_col(row, eye):
    return jnp.sum(jnp.where(eye, row, 0.0), axis=1, keepdims=True)


def to_row(col, eye):
    return jnp.sum(jnp.where(eye, col, 0.0), axis=0, keepdims=True)


def unit_lower_inverses(strict_list):
    size = strict_list[0].shape[0]
    rows, cols = grids(size)
    width = 1
    inverses = None
    while width < size:
        row_block = rows // width
        coupling = (row_block - cols // width == 1) & (row_block % 2 == 1)
        parts = [jnp.where(coupling, strict, 0.0) for strict in strict_list]
        if inverses is None:
            inverses = [jnp.where(rows == cols, 1.0, 0.0) - part for part in parts]
        else:
            halves = [mm3(part, inverse) for part, inverse in zip(parts, inverses)]
            inverses = [inverse - mm3(inverse, half) for inverse, half in zip(inverses, halves)]
        width = 2 * width
    return inverses


def shard_scales(dirs, rate_row, eye):
    gram = mm(dirs, dirs, "nt")
    square = jnp.where(eye, gram, 0.0)
    norm_row = lax.rsqrt(jnp.sum(square, axis=0, keepdims=True) + EPSILON)
    norm_col = lax.rsqrt(jnp.sum(square, axis=1, keepdims=True) + EPSILON)
    rate_col = to_col(rate_row, eye)
    return gram, norm_row, norm_col, rate_col


def prepare(shards):
    size = shards[0][0].shape[0]
    rows, cols = grids(size)
    eye = rows == cols
    strict = rows > cols
    grams, rights, norms = [], [], []
    for dirs, keys, rate_row in shards:
        gram, norm_row, norm_col, rate_col = shard_scales(dirs, rate_row, eye)
        scale = rate_col * norm_col
        grams.append(jnp.where(strict, gram * norm_row * scale, 0.0))
        rights.append(
            jnp.concatenate(
                [jnp.where(strict, mm(dirs, keys, "nt") * scale, 0.0), dirs.astype(F32) * scale], axis=1
            )
        )
        norms.append((norm_row, norm_col))
    inverses = unit_lower_inverses(grams)
    return [
        (inverse, mm3(inverse, right), norm) for inverse, right, norm in zip(inverses, rights, norms)
    ]


def pack_kernel(key_ref, dir_ref, value_ref, rate_ref, out_ref):
    size, width = key_ref.shape
    out_ref[0:size, 0:width] = key_ref[...]
    out_ref[0:size, width : 2 * width] = dir_ref[...]
    out_ref[0:size, 2 * width : 3 * width] = value_ref[...]
    heads = rate_ref.shape[0]
    rate = jnp.concatenate([rate_ref[h : h + 1, :] for h in range(heads)], axis=1)
    first = rate.astype(BF16).astype(F32)
    rest = rate - first
    second = rest.astype(BF16).astype(F32)
    third = rest - second
    row = lax.broadcasted_iota(jnp.int32, (16, width), 0)
    pieces = jnp.where(row == 0, first, jnp.where(row == 1, second, jnp.where(row == 2, third, 0.0)))
    out_ref[size : size + 16, 0:width] = pieces.astype(BF16)
    out_ref[size : size + 16, width : 3 * width] = jnp.zeros((16, 2 * width), BF16)


def own_kernel(query_ref, key_ref, dir_ref, rate_ref, inv_ref, kw_ref, raw_ref):
    size = query_ref.shape[0]
    heads = rate_ref.shape[0]
    rows, cols = grids(size)
    shards = []
    for h in range(heads):
        lanes = slice(h * DH, (h + 1) * DH)
        shards.append((dir_ref[:, lanes], key_ref[:, lanes], rate_ref[h : h + 1, :]))
    prepared = prepare(shards)
    for h in range(heads):
        lanes = slice(h * DH, (h + 1) * DH)
        inverse, coef, (norm_row, _) = prepared[h]
        query = query_ref[:, lanes]
        dirs, keys, _ = shards[h]
        applied = jnp.where(rows >= cols, mm(query, dirs, "nt") * norm_row, 0.0)
        base = jnp.concatenate([mm(query, keys, "nt"), query.astype(F32)], axis=1)
        raw_ref[h] = base - mm3(applied, coef)
        inv_ref[h] = inverse.astype(BF16)
        kw_ref[h] = coef.astype(BF16)


def attend_kernel(
    heads,
    raw_ref,
    value_ref,
    cot_ref,
    gain_ref,
    halo1_ref,
    halo2_ref,
    halo3_ref,
    halo4_ref,
    len_ref,
    first_ref,
    att_ref,
    tot_ref,
    prob_ref,
    frame_ref,
    kt_ref,
    sums_ref,
):
    size = value_ref.shape[0]
    width = heads * DH
    halos = (halo1_ref, halo2_ref, halo3_ref, halo4_ref)
    rows, cols = grids(size)
    eye = rows == cols
    eye_f = jnp.where(eye, 1.0, 0.0)
    first = first_ref[0]
    pos_row = first + lax.broadcasted_iota(jnp.int32, (1, size), 1)
    start_row = jnp.zeros((1, size), jnp.int32)
    end = jnp.int32(0)
    for d in range(len_ref.shape[0]):
        end = end + len_ref[d]
        start_row = jnp.where(end <= pos_row, end, start_row)
    start = to_col(start_row.astype(F32), eye).astype(jnp.int32)
    seen = [(rows >= cols) & (first + cols >= start)]
    for s in range(1, WIN + 1):
        seen.append(first - s * size + cols >= start)
    shards = []
    for s in range(WIN):
        for h in range(heads):
            keys = halos[s][0:size, h * DH : (h + 1) * DH]
            dirs = halos[s][0:size, width + h * DH : width + (h + 1) * DH]
            rate = halos[s][size : size + 16, h * DH : (h + 1) * DH].astype(F32)
            shards.append((dirs, keys, jnp.sum(rate, axis=0, keepdims=True)))
    prepared = prepare(shards)
    carry = []
    for (dirs, keys, _), (_, coef, (_, norm_col)) in zip(shards, prepared):
        base = jnp.concatenate([keys.astype(F32).T, eye_f], axis=1)
        high, low = split(coef * norm_col)
        turned = dirs.astype(F32).T.astype(BF16)
        carry.append(base - (mm(turned, high) + mm(turned, low)))
    square = jnp.zeros((size, 1), F32)
    inner = jnp.zeros((size, 1), F32)
    for h in range(heads):
        lanes = slice(h * DH, (h + 1) * DH)
        scores = [raw_ref[h, :, 0:DH]]
        frame = raw_ref[h, :, DH : 2 * DH]
        for s in range(WIN):
            matrix = carry[s * heads + h]
            kt_ref[h, s] = matrix.astype(BF16)
            frame_ref[h, s] = frame.astype(BF16)
            if s < WIN - 1:
                product = mm3(frame, matrix)
                scores.append(product[:, 0:DH])
                frame = product[:, DH : 2 * DH]
            else:
                scores.append(mm3(frame, matrix[:, 0:DH]))
        scaled = [
            jnp.where(seen[s], scores[s] * (DH ** (-0.5)), NEG_FILL) for s in range(WIN + 1)
        ]
        top = scaled[0]
        for s in range(1, WIN + 1):
            top = jnp.maximum(top, scaled[s])
        top = jnp.max(top, axis=1, keepdims=True)
        weights = [jnp.where(seen[s], jnp.exp(scaled[s] - top), 0.0) for s in range(WIN + 1)]
        total = weights[0]
        for s in range(1, WIN + 1):
            total = total + weights[s]
        total = jnp.sum(total, axis=1, keepdims=True)
        numer = None
        for s in range(WIN + 1):
            half = weights[s].astype(BF16)
            prob_ref[h, s] = half
            if s == 0:
                value = value_ref[:, lanes]
            else:
                value = halos[s - 1][0:size, 2 * width + h * DH : 2 * width + (h + 1) * DH]
            term = mm(half, value)
            numer = term if numer is None else numer + term
        att = numer / total
        att_ref[:, lanes] = att
        tot_ref[h] = jnp.broadcast_to(total, (size, 8))
        weighted = cot_ref[:, lanes].astype(F32) * gain_ref[:, lanes]
        square = square + jnp.sum(att * att, axis=1, keepdims=True)
        inner = inner + jnp.sum(weighted * att, axis=1, keepdims=True)
    sums_ref[0:1, :] = to_row(square, eye)
    sums_ref[1:2, :] = to_row(inner, eye)


def back_kernel(
    heads,
    features,
    sums_ref,
    att_ref,
    tot_ref,
    prob_ref,
    frame_ref,
    kt_ref,
    value_ref,
    cot_ref,
    gain_ref,
    halo1_ref,
    halo2_ref,
    halo3_ref,
    halo4_ref,
    normed_ref,
    part_ref,
    own_ref,
    dval_ref,
    send1_ref,
    send2_ref,
    send3_ref,
    send4_ref,
):
    size = value_ref.shape[0]
    width = heads * DH
    halos = (halo1_ref, halo2_ref, halo3_ref, halo4_ref)
    sends = (send1_ref, send2_ref, send3_ref, send4_ref)
    rows, cols = grids(size)
    eye = rows == cols
    square = to_col(sums_ref[0:1, :], eye)
    inner = to_col(sums_ref[1:2, :], eye)
    inverse = lax.rsqrt(square / features + EPSILON)
    pull = inverse * inverse * inverse * inner / features
    att_all = att_ref[...]
    cot_all = cot_ref[...].astype(F32)
    gain = gain_ref[...]
    normed = att_all * inverse
    normed_ref[...] = (normed * gain).astype(BF16)
    part_ref[...] = jnp.sum(cot_all * normed, axis=0, keepdims=True)
    grad_att = cot_all * gain * inverse - att_all * pull
    scale = DH ** (-0.5)
    for h in range(heads):
        lanes = slice(h * DH, (h + 1) * DH)
        total = tot_ref[h, :, 0:1]
        grad = grad_att[:, lanes]
        scaled = (grad / total).astype(BF16)
        delta = jnp.sum(grad * att_all[:, lanes], axis=1, keepdims=True) / total
        carried = None
        for s in range(WIN, -1, -1):
            if s == 0:
                value = value_ref[:, lanes]
            else:
                value = halos[s - 1][0:size, 2 * width + h * DH : 2 * width + (h + 1) * DH]
            prob = prob_ref[h, s]
            through = mm(scaled, value, "nt")
            dscore = (prob.astype(F32) * ((through - delta) * scale)).astype(BF16)
            dvalue = mm(prob, scaled, "tn")
            if s == 0:
                dval_ref[:, lanes] = dvalue
                own_ref[h] = jnp.concatenate([dscore, carried], axis=1)
                continue
            send = sends[s - 1]
            send[:, lanes] = dvalue.astype(BF16)
            if carried is None:
                send[:, width + h * DH : width + (h + 1) * DH] = mm(frame_ref[h, s - 1], dscore, "tn").astype(BF16)
                carried = mm(dscore, kt_ref[h, s - 1, :, 0:DH], "nt").astype(BF16)
            else:
                both = jnp.concatenate([dscore, carried], axis=1)
                grads = mm(frame_ref[h, s - 1], both, "tn").astype(BF16)
                send[:, width + h * DH : width + (h + 1) * DH] = grads[:, 0:DH]
                send[:, 2 * width + h * DH : 2 * width + (h + 1) * DH] = grads[:, DH : 2 * DH]
                carried = mm(both, kt_ref[h, s - 1], "nt").astype(BF16)


def local_kernel(heads, own_ref, kw_ref, query_ref, key_ref, dir_ref, dquery_ref, dkey_ref, ddir_ref, pulled_ref):
    size = query_ref.shape[0]
    rows, cols = grids(size)
    eye = rows == cols
    lower = rows >= cols
    for h in range(heads):
        lanes = slice(h * DH, (h + 1) * DH)
        query = query_ref[:, lanes]
        keys = key_ref[:, lanes]
        raw_dirs = dir_ref[:, lanes].astype(F32)
        norm_col = lax.rsqrt(jnp.sum(raw_dirs * raw_dirs, axis=1, keepdims=True) + EPSILON)
        unit = (raw_dirs * norm_col).astype(BF16)
        grads = own_ref[h]
        applied = jnp.where(lower, mm(query, unit, "nt"), 0.0).astype(BF16)
        dapplied = jnp.where(lower, mm(grads, kw_ref[h], "nt"), 0.0).astype(BF16)
        dquery = mm(grads[:, 0:DH], keys) + grads[:, DH : 2 * DH].astype(F32) - mm(dapplied, unit)
        dquery_ref[:, lanes] = dquery.astype(BF16)
        dkey_ref[h] = mm(grads[:, 0:DH], query, "tn")
        ddir_ref[h] = -mm(dapplied, query, "tn")
        pulled_ref[h] = mm(applied, grads, "tn")


def shard_kernel(
    heads,
    recv1_ref,
    recv2_ref,
    recv3_ref,
    recv4_ref,
    inv_ref,
    kw_ref,
    pulled_ref,
    dkey_in_ref,
    ddir_in_ref,
    dval_in_ref,
    key_ref,
    dir_ref,
    rate_ref,
    dkey_ref,
    dvalue_ref,
    ddir_ref,
    drate_ref,
):
    size = key_ref.shape[0]
    width = heads * DH
    recvs = (recv1_ref, recv2_ref, recv3_ref, recv4_ref)
    rows, cols = grids(size)
    eye = rows == cols
    strict = rows > cols
    dvalue = dval_in_ref[...]
    for s in range(WIN):
        dvalue = dvalue + recvs[s][:, 0:width].astype(F32)
    dvalue_ref[...] = dvalue.astype(BF16)
    for h in range(heads):
        lanes = slice(h * DH, (h + 1) * DH)
        keys = key_ref[:, lanes]
        raw_dirs = dir_ref[:, lanes].astype(F32)
        norm_col = lax.rsqrt(jnp.sum(raw_dirs * raw_dirs, axis=1, keepdims=True) + EPSILON)
        unit = raw_dirs * norm_col
        unit_half = unit.astype(BF16)
        rate_col = to_col(rate_ref[h : h + 1, :], eye)
        dend = recvs[0][:, width + h * DH : width + (h + 1) * DH].astype(F32)
        dtrans = recvs[0][:, 2 * width + h * DH : 2 * width + (h + 1) * DH].astype(F32)
        for s in range(1, WIN):
            dend = dend + recvs[s][:, width + h * DH : width + (h + 1) * DH].astype(F32)
            if s < WIN - 1:
                dtrans = dtrans + recvs[s][:, 2 * width + h * DH : 2 * width + (h + 1) * DH].astype(F32)
        both = jnp.concatenate([dend, dtrans], axis=1).astype(BF16)
        coef = kw_ref[h]
        dcoef = -(pulled_ref[h] + mm(unit_half, both))
        solved = mm(inv_ref[h], dcoef, "tn")
        dstrict = jnp.where(strict, -mm(solved, coef, "nt"), 0.0)
        dinner = jnp.where(strict, solved[:, 0:DH], 0.0).astype(BF16)
        local = mm(dstrict, unit_half) + mm(dinner, keys) + solved[:, DH : 2 * DH]
        dunit = (
            rate_col * local
            + mm(rate_col * dstrict, unit_half, "tn")
            + ddir_in_ref[h]
            - mm(coef, both, "nt")
        )
        drate_ref[h : h + 1, :] = to_row(jnp.sum(local * unit, axis=1, keepdims=True), eye)
        dkey_ref[:, lanes] = (
            dkey_in_ref[h] + mm(dinner, rate_col * unit, "tn") + dend.T
        ).astype(BF16)
        along = jnp.sum(unit * dunit, axis=1, keepdims=True)
        ddir_ref[:, lanes] = (norm_col * (dunit - unit * along)).astype(BF16)


def call(body, outs, flops, *operands, scalars=()):
    vmem = pl.BlockSpec(memory_space=pltpu.VMEM)
    smem = pl.BlockSpec(memory_space=pltpu.SMEM)
    moved = sum(x.size * x.dtype.itemsize for x in operands) + sum(
        jnp.dtype(d).itemsize * functools.reduce(lambda a, b: a * b, s) for s, d in outs
    )
    return pl.pallas_call(
        body,
        out_shape=[jax.ShapeDtypeStruct(s, d) for s, d in outs],
        in_specs=[vmem] * len(operands) + [smem] * len(scalars),
        out_specs=[vmem] * len(outs),
        compiler_params=pltpu.CompilerParams(vmem_limit_bytes=VMEM_LIMIT),
        cost_estimate=pl.CostEstimate(flops=flops, bytes_accessed=moved, transcendentals=0),
    )(*operands, *scalars)


def passed_along(value, steps):
    count = lax.axis_size("ctx")
    first, last = (max(0, -steps), min(count, count - steps))
    return lax.ppermute(value, "ctx", [(source, source + steps) for source in range(first, last)])


def grouped_sum(value, axis, width):
    count = lax.axis_size(axis)
    inner = [[g * width + i for i in range(width)] for g in range(count // width)]
    outer = [[g * width + i for g in range(count // width)] for i in range(width)]
    value = lax.psum(value, axis, axis_index_groups=inner)
    return lax.psum(value, axis, axis_index_groups=outer)


def per_device(query, keys, values, dirs, rates, gain, doc_lengths, cotangent):
    size, width = query.shape
    heads = width // DH
    features = width * lax.axis_size("head")
    gain_row = gain.reshape(1, width)
    first = (lax.axis_index("ctx") * size).astype(jnp.int32).reshape(1)
    unit_flops = 2 * size * size * DH
    (packed,) = call(pack_kernel, [((size + 16, 3 * width), BF16)], 0, keys, dirs, values, rates)
    halos = [passed_along(packed, s) for s in range(1, WIN + 1)]
    inverse, coef, raw = call(
        own_kernel,
        [((heads, size, size), BF16), ((heads, size, 2 * DH), BF16), ((heads, size, 2 * DH), F32)],
        heads * 60 * unit_flops,
        query,
        keys,
        dirs,
        rates,
    )
    att, total, prob, frame, carry, sums = call(
        functools.partial(attend_kernel, heads),
        [
            ((size, width), F32),
            ((heads, size, 8), F32),
            ((heads, WIN + 1, size, size), BF16),
            ((heads, WIN, size, DH), BF16),
            ((heads, WIN, DH, 2 * DH), BF16),
            ((2, size), F32),
        ],
        heads * 300 * unit_flops,
        raw,
        values,
        cotangent,
        gain_row,
        *halos,
        scalars=(doc_lengths, first),
    )
    sums = lax.psum(sums, "head")
    normed, part, own, dval, *sends = call(
        functools.partial(back_kernel, heads, features),
        [
            ((size, width), BF16),
            ((1, width), F32),
            ((heads, size, 2 * DH), BF16),
            ((size, width), F32),
            ((size, 3 * width), BF16),
            ((size, 3 * width), BF16),
            ((size, 3 * width), BF16),
            ((size, 2 * width), BF16),
        ],
        heads * 30 * unit_flops,
        sums,
        att,
        total,
        prob,
        frame,
        carry,
        values,
        cotangent,
        gain_row,
        *halos,
    )
    recvs = [passed_along(sends[s - 1], -s) for s in range(1, WIN + 1)]
    dquery, dkey_part, ddir_part, pulled = call(
        functools.partial(local_kernel, heads),
        [
            ((size, width), BF16),
            ((heads, size, DH), F32),
            ((heads, size, DH), F32),
            ((heads, size, 2 * DH), F32),
        ],
        heads * 10 * unit_flops,
        own,
        coef,
        query,
        keys,
        dirs,
    )
    grad_gain = grouped_sum(part, "ctx", 8).reshape(width)
    dkey, dvalue, ddir, drate = call(
        functools.partial(shard_kernel, heads),
        [((size, width), BF16), ((size, width), BF16), ((size, width), BF16), ((heads, size), F32)],
        heads * 20 * unit_flops,
        *recvs,
        inverse,
        coef,
        pulled,
        dkey_part,
        ddir_part,
        dval,
        keys,
        dirs,
        rates,
    )
    return normed, dquery, dkey, dvalue, ddir, drate, grad_gain


def solution(mesh):
    rows = P("ctx", "head")
    return jax.shard_map(
        per_device,
        mesh=mesh,
        in_specs=(rows, rows, rows, rows, P("head", "ctx"), P("head"), P(), rows),
        out_specs=(rows, rows, rows, rows, rows, P("head", "ctx"), P("head")),
        check_vma=False,
    )
```

```python
import functools

import jax
import jax.numpy as jnp
from jax import lax
from jax.experimental import pallas as pl
from jax.experimental.pallas import tpu as pltpu
from jax.sharding import PartitionSpec as P

DH = 128
WIN = 4
NEG_FILL = -1e30
EPSILON = 1e-06
F32 = jnp.float32
BF16 = jnp.bfloat16
VMEM_LIMIT = 48 * 1024 * 1024


def mm(left, right, form="nn"):
    lhs = 0 if form[0] == "t" else 1
    rhs = 1 if form[1] == "t" else 0
    return lax.dot_general(
        left.astype(BF16), right.astype(BF16), (((lhs,), (rhs,)), ((), ())), preferred_element_type=F32
    )


def split(value):
    high = value.astype(BF16)
    low = (value - high.astype(F32)).astype(BF16)
    return high, low


def mm3(left, right):
    lh, ll = split(left)
    rh, rl = split(right)
    return mm(lh, rh) + (mm(lh, rl) + mm(ll, rh))


def grids(size):
    rows = lax.broadcasted_iota(jnp.int32, (size, size), 0)
    cols = lax.broadcasted_iota(jnp.int32, (size, size), 1)
    return rows, cols


def to_col(row, eye):
    return jnp.sum(jnp.where(eye, row, 0.0), axis=1, keepdims=True)


def to_row(col, eye):
    return jnp.sum(jnp.where(eye, col, 0.0), axis=0, keepdims=True)


def unit_lower_inverses(strict_list):
    size = strict_list[0].shape[0]
    rows, cols = grids(size)
    width = 1
    inverses = None
    while width < size:
        row_block = rows // width
        coupling = (row_block - cols // width == 1) & (row_block % 2 == 1)
        parts = [jnp.where(coupling, strict, 0.0) for strict in strict_list]
        if inverses is None:
            inverses = [jnp.where(rows == cols, 1.0, 0.0) - part for part in parts]
        else:
            halves = [mm3(part, inverse) for part, inverse in zip(parts, inverses)]
            inverses = [inverse - mm3(inverse, half) for inverse, half in zip(inverses, halves)]
        width = 2 * width
    return inverses


def shard_scales(dirs, rate_row, eye):
    gram = mm(dirs, dirs, "nt")
    square = jnp.where(eye, gram, 0.0)
    norm_row = lax.rsqrt(jnp.sum(square, axis=0, keepdims=True) + EPSILON)
    norm_col = lax.rsqrt(jnp.sum(square, axis=1, keepdims=True) + EPSILON)
    rate_col = to_col(rate_row, eye)
    return gram, norm_row, norm_col, rate_col


def prepare(shards):
    size = shards[0][0].shape[0]
    rows, cols = grids(size)
    eye = rows == cols
    strict = rows > cols
    grams, rights, norms = [], [], []
    for dirs, keys, rate_row in shards:
        gram, norm_row, norm_col, rate_col = shard_scales(dirs, rate_row, eye)
        scale = rate_col * norm_col
        grams.append(jnp.where(strict, gram * norm_row * scale, 0.0))
        rights.append(
            jnp.concatenate(
                [jnp.where(strict, mm(dirs, keys, "nt") * scale, 0.0), dirs.astype(F32) * scale], axis=1
            )
        )
        norms.append((norm_row, norm_col))
    inverses = unit_lower_inverses(grams)
    return [
        (inverse, mm3(inverse, right), norm) for inverse, right, norm in zip(inverses, rights, norms)
    ]


def pack_kernel(key_ref, dir_ref, value_ref, rate_ref, out_ref, rate_in, rate_out, sems):
    size, width = key_ref.shape
    heads = rate_ref.shape[0]
    bring = pltpu.make_async_copy(rate_ref, rate_in, sems.at[0])
    bring.start()
    copies = [
        pltpu.make_async_copy(
            ref, out_ref.at[pl.ds(0, size), pl.ds(at * width, width)], sems.at[at + 1]
        )
        for at, ref in enumerate((key_ref, dir_ref, value_ref))
    ]
    for copy in copies:
        copy.start()
    bring.wait()
    rate = jnp.concatenate([rate_in[h : h + 1, :] for h in range(heads)], axis=1)
    first = rate.astype(BF16).astype(F32)
    rest = rate - first
    second = rest.astype(BF16).astype(F32)
    third = rest - second
    row = lax.broadcasted_iota(jnp.int32, (16, width), 0)
    pieces = jnp.where(row == 0, first, jnp.where(row == 1, second, jnp.where(row == 2, third, 0.0)))
    rate_out[:, 0:width] = pieces.astype(BF16)
    rate_out[:, width : 3 * width] = jnp.zeros((16, 2 * width), BF16)
    last = pltpu.make_async_copy(rate_out, out_ref.at[pl.ds(size, 16)], sems.at[4])
    last.start()
    for copy in copies:
        copy.wait()
    last.wait()


def pack(keys, dirs, values, rates):
    size, width = keys.shape
    anywhere = pl.BlockSpec(memory_space=pl.ANY)
    return pl.pallas_call(
        pack_kernel,
        out_shape=jax.ShapeDtypeStruct((size + 16, 3 * width), BF16),
        in_specs=[anywhere] * 4,
        out_specs=anywhere,
        scratch_shapes=[
            pltpu.VMEM(rates.shape, F32),
            pltpu.VMEM((16, 3 * width), BF16),
            pltpu.SemaphoreType.DMA((5,)),
        ],
    )(keys, dirs, values, rates)


def own_kernel(query_ref, key_ref, dir_ref, rate_ref, inv_ref, kw_ref, raw_ref):
    size = query_ref.shape[0]
    heads = rate_ref.shape[0]
    rows, cols = grids(size)
    shards = []
    for h in range(heads):
        lanes = slice(h * DH, (h + 1) * DH)
        shards.append((dir_ref[:, lanes], key_ref[:, lanes], rate_ref[h : h + 1, :]))
    prepared = prepare(shards)
    for h in range(heads):
        lanes = slice(h * DH, (h + 1) * DH)
        inverse, coef, (norm_row, _) = prepared[h]
        query = query_ref[:, lanes]
        dirs, keys, _ = shards[h]
        applied = jnp.where(rows >= cols, mm(query, dirs, "nt") * norm_row, 0.0)
        base = jnp.concatenate([mm(query, keys, "nt"), query.astype(F32)], axis=1)
        raw_ref[h] = base - mm3(applied, coef)
        inv_ref[h] = inverse.astype(BF16)
        kw_ref[h] = coef.astype(BF16)


def attend_kernel(
    heads,
    raw_ref,
    value_ref,
    cot_ref,
    gain_ref,
    halo2_ref,
    halo4_ref,
    even_ref,
    cross2_ref,
    cross4_ref,
    len_ref,
    place_ref,
    att_ref,
    tot_ref,
    prob_ref,
    frame_ref,
    kt_ref,
    sums_ref,
    far_ref,
    halo1_ref,
    halo3_ref,
):
    size = value_ref.shape[0]
    width = heads * DH

    @pl.when(place_ref[1] == 0)
    def _():
        halo1_ref[...] = cross2_ref[...]
        halo3_ref[...] = cross4_ref[...]

    @pl.when(place_ref[1] != 0)
    def _():
        halo1_ref[...] = even_ref[...]
        halo3_ref[...] = cross2_ref[...]

    halos = (halo1_ref, halo2_ref, halo3_ref, halo4_ref)
    for s in range(WIN):
        far_ref[s] = halos[s][0:size, 2 * width : 3 * width]
    rows, cols = grids(size)
    eye = rows == cols
    eye_f = jnp.where(eye, 1.0, 0.0)
    first = place_ref[0]
    pos_row = first + lax.broadcasted_iota(jnp.int32, (1, size), 1)
    start_row = jnp.zeros((1, size), jnp.int32)
    end = jnp.int32(0)
    for d in range(len_ref.shape[0]):
        end = end + len_ref[d]
        start_row = jnp.where(end <= pos_row, end, start_row)
    start = to_col(start_row.astype(F32), eye).astype(jnp.int32)
    seen = [(rows >= cols) & (first + cols >= start)]
    for s in range(1, WIN + 1):
        seen.append(first - s * size + cols >= start)
    shards = []
    for s in range(WIN):
        for h in range(heads):
            keys = halos[s][0:size, h * DH : (h + 1) * DH]
            dirs = halos[s][0:size, width + h * DH : width + (h + 1) * DH]
            rate = halos[s][size : size + 16, h * DH : (h + 1) * DH].astype(F32)
            shards.append((dirs, keys, jnp.sum(rate, axis=0, keepdims=True)))
    prepared = prepare(shards)
    carry = []
    for (dirs, keys, _), (_, coef, (_, norm_col)) in zip(shards, prepared):
        base = jnp.concatenate([keys.astype(F32).T, eye_f], axis=1)
        high, low = split(coef * norm_col)
        turned = dirs.astype(F32).T.astype(BF16)
        carry.append(base - (mm(turned, high) + mm(turned, low)))
    square = jnp.zeros((size, 1), F32)
    inner = jnp.zeros((size, 1), F32)
    for h in range(heads):
        lanes = slice(h * DH, (h + 1) * DH)
        scores = [raw_ref[h, :, 0:DH]]
        frame = raw_ref[h, :, DH : 2 * DH]
        for s in range(WIN):
            matrix = carry[s * heads + h]
            kt_ref[h, s] = matrix.astype(BF16)
            frame_ref[h, s] = frame.astype(BF16)
            if s < WIN - 1:
                product = mm3(frame, matrix)
                scores.append(product[:, 0:DH])
                frame = product[:, DH : 2 * DH]
            else:
                scores.append(mm3(frame, matrix[:, 0:DH]))
        scaled = [
            jnp.where(seen[s], scores[s] * (DH ** (-0.5)), NEG_FILL) for s in range(WIN + 1)
        ]
        top = scaled[0]
        for s in range(1, WIN + 1):
            top = jnp.maximum(top, scaled[s])
        top = jnp.max(top, axis=1, keepdims=True)
        weights = [jnp.where(seen[s], jnp.exp(scaled[s] - top), 0.0) for s in range(WIN + 1)]
        total = weights[0]
        for s in range(1, WIN + 1):
            total = total + weights[s]
        total = jnp.sum(total, axis=1, keepdims=True)
        numer = None
        for s in range(WIN + 1):
            half = weights[s].astype(BF16)
            prob_ref[h, s] = half
            if s == 0:
                value = value_ref[:, lanes]
            else:
                value = halos[s - 1][0:size, 2 * width + h * DH : 2 * width + (h + 1) * DH]
            term = mm(half, value)
            numer = term if numer is None else numer + term
        att = numer / total
        att_ref[:, lanes] = att
        tot_ref[h] = jnp.broadcast_to(total, (size, 8))
        weighted = cot_ref[:, lanes].astype(F32) * gain_ref[:, lanes]
        square = square + jnp.sum(att * att, axis=1, keepdims=True)
        inner = inner + jnp.sum(weighted * att, axis=1, keepdims=True)
    row = jnp.concatenate([to_row(square, eye), to_row(inner, eye)], axis=1)
    sums_ref[...] = jnp.broadcast_to(row, sums_ref.shape)


def back_kernel(
    heads,
    features,
    sums_ref,
    att_ref,
    tot_ref,
    prob_ref,
    frame_ref,
    kt_ref,
    value_ref,
    cot_ref,
    gain_ref,
    far_ref,
    normed_ref,
    part_ref,
    own_ref,
    dval_ref,
    send1_ref,
    send2_ref,
    send3_ref,
    send4_ref,
):
    size = value_ref.shape[0]
    width = heads * DH
    sends = (send1_ref, send2_ref, send3_ref, send4_ref)
    rows, cols = grids(size)
    eye = rows == cols
    sums = jnp.sum(sums_ref[...], axis=0, keepdims=True)
    square = to_col(sums[:, 0:size], eye)
    inner = to_col(sums[:, size : 2 * size], eye)
    inverse = lax.rsqrt(square / features + EPSILON)
    pull = inverse * inverse * inverse * inner / features
    att_all = att_ref[...]
    cot_all = cot_ref[...].astype(F32)
    gain = gain_ref[...]
    normed = att_all * inverse
    normed_ref[...] = (normed * gain).astype(BF16)
    part_ref[...] = jnp.broadcast_to(jnp.sum(cot_all * normed, axis=0, keepdims=True), part_ref.shape)
    grad_att = cot_all * gain * inverse - att_all * pull
    scale = DH ** (-0.5)
    for h in range(heads):
        lanes = slice(h * DH, (h + 1) * DH)
        total = tot_ref[h, :, 0:1]
        grad = grad_att[:, lanes]
        scaled = (grad / total).astype(BF16)
        delta = jnp.sum(grad * att_all[:, lanes], axis=1, keepdims=True) / total
        carried = None
        for s in range(WIN, -1, -1):
            if s == 0:
                value = value_ref[:, lanes]
            else:
                value = far_ref[s - 1, :, lanes]
            prob = prob_ref[h, s]
            through = mm(scaled, value, "nt")
            dscore = (prob.astype(F32) * ((through - delta) * scale)).astype(BF16)
            dvalue = mm(prob, scaled, "tn")
            if s == 0:
                dval_ref[:, lanes] = dvalue
                own_ref[h] = jnp.concatenate([dscore, carried], axis=1)
                continue
            send = sends[s - 1]
            send[:, lanes] = dvalue.astype(BF16)
            if carried is None:
                send[:, width + h * DH : width + (h + 1) * DH] = mm(frame_ref[h, s - 1], dscore, "tn").astype(BF16)
                carried = mm(dscore, kt_ref[h, s - 1, :, 0:DH], "nt").astype(BF16)
            else:
                both = jnp.concatenate([dscore, carried], axis=1)
                grads = mm(frame_ref[h, s - 1], both, "tn").astype(BF16)
                send[:, width + h * DH : width + (h + 1) * DH] = grads[:, 0:DH]
                send[:, 2 * width + h * DH : 2 * width + (h + 1) * DH] = grads[:, DH : 2 * DH]
                carried = mm(both, kt_ref[h, s - 1], "nt").astype(BF16)


def local_kernel(heads, own_ref, kw_ref, query_ref, key_ref, dir_ref, dquery_ref, dkey_ref, ddir_ref, pulled_ref):
    size = query_ref.shape[0]
    rows, cols = grids(size)
    eye = rows == cols
    lower = rows >= cols
    for h in range(heads):
        lanes = slice(h * DH, (h + 1) * DH)
        query = query_ref[:, lanes]
        keys = key_ref[:, lanes]
        raw_dirs = dir_ref[:, lanes].astype(F32)
        norm_col = lax.rsqrt(jnp.sum(raw_dirs * raw_dirs, axis=1, keepdims=True) + EPSILON)
        unit = (raw_dirs * norm_col).astype(BF16)
        grads = own_ref[h]
        applied = jnp.where(lower, mm(query, unit, "nt"), 0.0).astype(BF16)
        dapplied = jnp.where(lower, mm(grads, kw_ref[h], "nt"), 0.0).astype(BF16)
        dquery = mm(grads[:, 0:DH], keys) + grads[:, DH : 2 * DH].astype(F32) - mm(dapplied, unit)
        dquery_ref[:, lanes] = dquery.astype(BF16)
        dkey_ref[h] = mm(grads[:, 0:DH], query, "tn")
        ddir_ref[h] = -mm(dapplied, query, "tn")
        pulled_ref[h] = mm(applied, grads, "tn")


def shard_kernel(
    heads,
    recv1_ref,
    recv2_ref,
    recv3_ref,
    recv4_ref,
    inv_ref,
    kw_ref,
    pulled_ref,
    dkey_in_ref,
    ddir_in_ref,
    dval_in_ref,
    key_ref,
    dir_ref,
    rate_ref,
    parts_ref,
    dkey_ref,
    dvalue_ref,
    ddir_ref,
    drate_ref,
    dgain_ref,
):
    size = key_ref.shape[0]
    width = heads * DH
    recvs = (recv1_ref, recv2_ref, recv3_ref, recv4_ref)
    rows, cols = grids(size)
    eye = rows == cols
    strict = rows > cols
    dvalue = dval_in_ref[...]
    for s in range(WIN):
        dvalue = dvalue + recvs[s][:, 0:width].astype(F32)
    dvalue_ref[...] = dvalue.astype(BF16)
    dgain_ref[...] = jnp.sum(parts_ref[...], axis=0, keepdims=True)
    for h in range(heads):
        lanes = slice(h * DH, (h + 1) * DH)
        keys = key_ref[:, lanes]
        raw_dirs = dir_ref[:, lanes].astype(F32)
        norm_col = lax.rsqrt(jnp.sum(raw_dirs * raw_dirs, axis=1, keepdims=True) + EPSILON)
        unit = raw_dirs * norm_col
        unit_half = unit.astype(BF16)
        rate_col = to_col(rate_ref[h : h + 1, :], eye)
        dend = recvs[0][:, width + h * DH : width + (h + 1) * DH].astype(F32)
        dtrans = recvs[0][:, 2 * width + h * DH : 2 * width + (h + 1) * DH].astype(F32)
        for s in range(1, WIN):
            dend = dend + recvs[s][:, width + h * DH : width + (h + 1) * DH].astype(F32)
            if s < WIN - 1:
                dtrans = dtrans + recvs[s][:, 2 * width + h * DH : 2 * width + (h + 1) * DH].astype(F32)
        both = jnp.concatenate([dend, dtrans], axis=1).astype(BF16)
        coef = kw_ref[h]
        dcoef = -(pulled_ref[h] + mm(unit_half, both))
        solved = mm(inv_ref[h], dcoef, "tn")
        dstrict = jnp.where(strict, -mm(solved, coef, "nt"), 0.0)
        dinner = jnp.where(strict, solved[:, 0:DH], 0.0).astype(BF16)
        local = mm(dstrict, unit_half) + mm(dinner, keys) + solved[:, DH : 2 * DH]
        dunit = (
            rate_col * local
            + mm(rate_col * dstrict, unit_half, "tn")
            + ddir_in_ref[h]
            - mm(coef, both, "nt")
        )
        drate_ref[h : h + 1, :] = to_row(jnp.sum(local * unit, axis=1, keepdims=True), eye)
        dkey_ref[:, lanes] = (
            dkey_in_ref[h] + mm(dinner, rate_col * unit, "tn") + dend.T
        ).astype(BF16)
        along = jnp.sum(unit * dunit, axis=1, keepdims=True)
        ddir_ref[:, lanes] = (norm_col * (dunit - unit * along)).astype(BF16)


def call(body, outs, flops, *operands, scalars=(), scratch=()):
    vmem = pl.BlockSpec(memory_space=pltpu.VMEM)
    smem = pl.BlockSpec(memory_space=pltpu.SMEM)
    moved = sum(x.size * x.dtype.itemsize for x in operands) + sum(
        jnp.dtype(d).itemsize * functools.reduce(lambda a, b: a * b, s) for s, d in outs
    )
    return pl.pallas_call(
        body,
        out_shape=[jax.ShapeDtypeStruct(s, d) for s, d in outs],
        in_specs=[vmem] * len(operands) + [smem] * len(scalars),
        out_specs=[vmem] * len(outs),
        scratch_shapes=list(scratch),
        compiler_params=pltpu.CompilerParams(vmem_limit_bytes=VMEM_LIMIT),
        cost_estimate=pl.CostEstimate(flops=flops, bytes_accessed=moved, transcendentals=0),
    )(*operands, *scalars)


def passed_along(value, steps):
    count = lax.axis_size("ctx")
    first, last = (max(0, -steps), min(count, count - steps))
    return lax.ppermute(value, "ctx", [(source, source + steps) for source in range(first, last)])


def paired(value, first, step):
    count = lax.axis_size("ctx")
    return lax.ppermute(value, "ctx", [(source, source + step) for source in range(first, count, 2)])


def swapped(value):
    count = lax.axis_size("ctx")
    return lax.ppermute(value, "ctx", [(source, source ^ 1) for source in range(count)])


def gathered(value, axis):
    return lax.all_to_all(value, axis, 0, 0, tiled=True)


def per_device(query, keys, values, dirs, rates, gain, doc_lengths, cotangent):
    size, width = query.shape
    heads = width // DH
    features = width * lax.axis_size("head")
    gain_row = gain.reshape(1, width)
    ctx = lax.axis_index("ctx").astype(jnp.int32)
    place = jnp.stack([ctx * size, ctx % 2])
    unit_flops = 2 * size * size * DH
    packed = pack(keys, dirs, values, rates)
    halo2 = passed_along(packed, 2)
    halo4 = passed_along(packed, 4)
    halos = (halo2, halo4, paired(packed, 0, 1), swapped(halo2), paired(halo4, 1, -1))
    inverse, coef, raw = call(
        own_kernel,
        [((heads, size, size), BF16), ((heads, size, 2 * DH), BF16), ((heads, size, 2 * DH), F32)],
        heads * 60 * unit_flops,
        query,
        keys,
        dirs,
        rates,
    )
    att, total, prob, frame, carry, sums, far = call(
        functools.partial(attend_kernel, heads),
        [
            ((size, width), F32),
            ((heads, size, 8), F32),
            ((heads, WIN + 1, size, size), BF16),
            ((heads, WIN, size, DH), BF16),
            ((heads, WIN, DH, 2 * DH), BF16),
            ((lax.axis_size("head"), 2 * size), F32),
            ((WIN, size, width), BF16),
        ],
        heads * 300 * unit_flops,
        raw,
        values,
        cotangent,
        gain_row,
        *halos,
        scalars=(doc_lengths, place),
        scratch=[pltpu.VMEM((size + 16, 3 * width), BF16)] * 2,
    )
    sums = gathered(sums, "head")
    normed, part, own, dval, *sends = call(
        functools.partial(back_kernel, heads, features),
        [
            ((size, width), BF16),
            ((lax.axis_size("ctx"), width), F32),
            ((heads, size, 2 * DH), BF16),
            ((size, width), F32),
            ((size, 3 * width), BF16),
            ((size, 3 * width), BF16),
            ((size, 3 * width), BF16),
            ((size, 2 * width), BF16),
        ],
        heads * 30 * unit_flops,
        sums,
        att,
        total,
        prob,
        frame,
        carry,
        values,
        cotangent,
        gain_row,
        far,
    )
    recvs = [passed_along(sends[s - 1], -s) for s in range(1, WIN + 1)]
    dquery, dkey_part, ddir_part, pulled = call(
        functools.partial(local_kernel, heads),
        [
            ((size, width), BF16),
            ((heads, size, DH), F32),
            ((heads, size, DH), F32),
            ((heads, size, 2 * DH), F32),
        ],
        heads * 10 * unit_flops,
        own,
        coef,
        query,
        keys,
        dirs,
    )
    parts = gathered(part, "ctx")
    dkey, dvalue, ddir, drate, dgain = call(
        functools.partial(shard_kernel, heads),
        [((size, width), BF16), ((size, width), BF16), ((size, width), BF16), ((heads, size), F32), ((1, width), F32)],
        heads * 20 * unit_flops,
        *recvs,
        inverse,
        coef,
        pulled,
        dkey_part,
        ddir_part,
        dval,
        keys,
        dirs,
        rates,
        parts,
    )
    return normed, dquery, dkey, dvalue, ddir, drate, dgain.reshape(width)


def solution(mesh):
    rows = P("ctx", "head")
    return jax.shard_map(
        per_device,
        mesh=mesh,
        in_specs=(rows, rows, rows, rows, P("head", "ctx"), P("head"), P(), rows),
        out_specs=(rows, rows, rows, rows, rows, P("head", "ctx"), P("head")),
        check_vma=False,
    )
```

```python
import functools

import jax
import jax.numpy as jnp
from jax import lax
from jax.experimental import pallas as pl
from jax.experimental.pallas import tpu as pltpu
from jax.sharding import PartitionSpec as P

DH = 128
WIN = 4
NEG_FILL = -1e30
EPSILON = 1e-06
F32 = jnp.float32
BF16 = jnp.bfloat16
VMEM_LIMIT = 48 * 1024 * 1024


def mm(left, right, form="nn"):
    lhs = 0 if form[0] == "t" else 1
    rhs = 1 if form[1] == "t" else 0
    return lax.dot_general(
        left.astype(BF16), right.astype(BF16), (((lhs,), (rhs,)), ((), ())), preferred_element_type=F32
    )


def split(value):
    high = value.astype(BF16)
    low = (value - high.astype(F32)).astype(BF16)
    return high, low


def mm3(left, right):
    lh, ll = split(left)
    rh, rl = split(right)
    return mm(lh, rh) + (mm(lh, rl) + mm(ll, rh))


def grids(size):
    rows = lax.broadcasted_iota(jnp.int32, (size, size), 0)
    cols = lax.broadcasted_iota(jnp.int32, (size, size), 1)
    return rows, cols


def to_col(row, eye):
    return jnp.sum(jnp.where(eye, row, 0.0), axis=1, keepdims=True)


def to_row(col, eye):
    return jnp.sum(jnp.where(eye, col, 0.0), axis=0, keepdims=True)


def unit_lower_inverses(strict_list):
    size = strict_list[0].shape[0]
    rows, cols = grids(size)
    width = 1
    inverses = None
    while width < size:
        row_block = rows // width
        coupling = (row_block - cols // width == 1) & (row_block % 2 == 1)
        parts = [jnp.where(coupling, strict, 0.0) for strict in strict_list]
        if inverses is None:
            inverses = [jnp.where(rows == cols, 1.0, 0.0) - part for part in parts]
        else:
            halves = [mm3(part, inverse) for part, inverse in zip(parts, inverses)]
            inverses = [inverse - mm3(inverse, half) for inverse, half in zip(inverses, halves)]
        width = 2 * width
    return inverses


def shard_scales(dirs, rate_row, eye):
    gram = mm(dirs, dirs, "nt")
    square = jnp.where(eye, gram, 0.0)
    norm_row = lax.rsqrt(jnp.sum(square, axis=0, keepdims=True) + EPSILON)
    norm_col = lax.rsqrt(jnp.sum(square, axis=1, keepdims=True) + EPSILON)
    rate_col = to_col(rate_row, eye)
    return gram, norm_row, norm_col, rate_col


def prepare(shards):
    size = shards[0][0].shape[0]
    rows, cols = grids(size)
    eye = rows == cols
    strict = rows > cols
    grams, rights, norms = [], [], []
    for dirs, keys, rate_row in shards:
        gram, norm_row, norm_col, rate_col = shard_scales(dirs, rate_row, eye)
        scale = rate_col * norm_col
        grams.append(jnp.where(strict, gram * norm_row * scale, 0.0))
        rights.append(
            jnp.concatenate(
                [jnp.where(strict, mm(dirs, keys, "nt") * scale, 0.0), dirs.astype(F32) * scale], axis=1
            )
        )
        norms.append((norm_row, norm_col))
    inverses = unit_lower_inverses(grams)
    return [
        (inverse, mm3(inverse, right), norm) for inverse, right, norm in zip(inverses, rights, norms)
    ]


def rate_pieces(row, height, width):
    first = row.astype(BF16).astype(F32)
    rest = row - first
    second = rest.astype(BF16).astype(F32)
    third = rest - second
    at = lax.broadcasted_iota(jnp.int32, (height, width), 0)
    return jnp.where(at == 0, first, jnp.where(at == 1, second, jnp.where(at == 2, third, 0.0))).astype(BF16)


def pack_kernel(key_ref, dir_ref, value_ref, rate_ref, out_ref, rate_in, sems):
    size, width = key_ref.shape
    heads = rate_ref.shape[0]
    bring = pltpu.make_async_copy(rate_ref, rate_in, sems.at[3])
    bring.start()
    copies = [
        pltpu.make_async_copy(
            ref, out_ref.at[pl.ds(0, size), pl.ds(at * width, width)], sems.at[at]
        )
        for at, ref in enumerate((key_ref, dir_ref, value_ref))
    ]
    for copy in copies:
        copy.start()
    bring.wait()
    rate = jnp.concatenate([rate_in[h : h + 1, :] for h in range(heads)], axis=1)
    out_ref[size : size + 16, 0:width] = rate_pieces(rate, 16, width)
    out_ref[size : size + 16, width : 3 * width] = jnp.zeros((16, 2 * width), BF16)
    for copy in copies:
        copy.wait()


def pack(keys, dirs, values, rates):
    size, width = keys.shape
    return pl.pallas_call(
        pack_kernel,
        out_shape=jax.ShapeDtypeStruct((size + 16, 3 * width), BF16),
        in_specs=[pl.BlockSpec(memory_space=pl.ANY)] * 4,
        out_specs=pl.BlockSpec(memory_space=pltpu.VMEM),
        scratch_shapes=[pltpu.VMEM(rates.shape, F32), pltpu.SemaphoreType.DMA((4,))],
    )(keys, dirs, values, rates)


def own_kernel(query_ref, key_ref, dir_ref, rate_ref, inv_ref, kw_ref, raw_ref):
    size = query_ref.shape[0]
    heads = rate_ref.shape[0]
    rows, cols = grids(size)
    shards = []
    for h in range(heads):
        lanes = slice(h * DH, (h + 1) * DH)
        shards.append((dir_ref[:, lanes], key_ref[:, lanes], rate_ref[h : h + 1, :]))
    prepared = prepare(shards)
    for h in range(heads):
        lanes = slice(h * DH, (h + 1) * DH)
        inverse, coef, (norm_row, _) = prepared[h]
        query = query_ref[:, lanes]
        dirs, keys, _ = shards[h]
        applied = jnp.where(rows >= cols, mm(query, dirs, "nt") * norm_row, 0.0)
        base = jnp.concatenate([mm(query, keys, "nt"), query.astype(F32)], axis=1)
        raw_ref[h] = base - mm3(applied, coef)
        inv_ref[h] = inverse.astype(BF16)
        kw_ref[h] = coef.astype(BF16)


def attend_kernel(
    heads,
    raw_ref,
    value_ref,
    cot_ref,
    gain_ref,
    halo2_ref,
    halo4_ref,
    even_ref,
    cross2_ref,
    cross4_ref,
    len_ref,
    place_ref,
    att_ref,
    tot_ref,
    prob_ref,
    frame_ref,
    kt_ref,
    sums_ref,
    far_ref,
    halo1_ref,
    halo3_ref,
):
    size = value_ref.shape[0]
    width = heads * DH

    @pl.when(place_ref[1] == 0)
    def _():
        halo1_ref[...] = cross2_ref[...]
        halo3_ref[...] = cross4_ref[...]

    @pl.when(place_ref[1] != 0)
    def _():
        halo1_ref[...] = even_ref[...]
        halo3_ref[...] = cross2_ref[...]

    halos = (halo1_ref, halo2_ref, halo3_ref, halo4_ref)
    for s in range(WIN):
        far_ref[s] = halos[s][0:size, 2 * width : 3 * width]
    rows, cols = grids(size)
    eye = rows == cols
    eye_f = jnp.where(eye, 1.0, 0.0)
    first = place_ref[0]
    pos_row = first + lax.broadcasted_iota(jnp.int32, (1, size), 1)
    start_row = jnp.zeros((1, size), jnp.int32)
    end = jnp.int32(0)
    for d in range(len_ref.shape[0]):
        end = end + len_ref[d]
        start_row = jnp.where(end <= pos_row, end, start_row)
    start = to_col(start_row.astype(F32), eye).astype(jnp.int32)
    seen = [(rows >= cols) & (first + cols >= start)]
    for s in range(1, WIN + 1):
        seen.append(first - s * size + cols >= start)
    shards = []
    for s in range(WIN):
        for h in range(heads):
            keys = halos[s][0:size, h * DH : (h + 1) * DH]
            dirs = halos[s][0:size, width + h * DH : width + (h + 1) * DH]
            rate = halos[s][size : size + 16, h * DH : (h + 1) * DH].astype(F32)
            shards.append((dirs, keys, jnp.sum(rate, axis=0, keepdims=True)))
    prepared = prepare(shards)
    carry = []
    for (dirs, keys, _), (_, coef, (_, norm_col)) in zip(shards, prepared):
        base = jnp.concatenate([keys.astype(F32).T, eye_f], axis=1)
        high, low = split(coef * norm_col)
        turned = dirs.astype(F32).T.astype(BF16)
        carry.append(base - (mm(turned, high) + mm(turned, low)))
    square = jnp.zeros((size, 1), F32)
    inner = jnp.zeros((size, 1), F32)
    for h in range(heads):
        lanes = slice(h * DH, (h + 1) * DH)
        scores = [raw_ref[h, :, 0:DH]]
        frame = raw_ref[h, :, DH : 2 * DH]
        for s in range(WIN):
            matrix = carry[s * heads + h]
            kt_ref[h, s] = matrix.astype(BF16)
            frame_ref[h, s] = frame.astype(BF16)
            if s < WIN - 1:
                product = mm3(frame, matrix)
                scores.append(product[:, 0:DH])
                frame = product[:, DH : 2 * DH]
            else:
                scores.append(mm3(frame, matrix[:, 0:DH]))
        scaled = [
            jnp.where(seen[s], scores[s] * (DH ** (-0.5)), NEG_FILL) for s in range(WIN + 1)
        ]
        top = scaled[0]
        for s in range(1, WIN + 1):
            top = jnp.maximum(top, scaled[s])
        top = jnp.max(top, axis=1, keepdims=True)
        weights = [jnp.where(seen[s], jnp.exp(scaled[s] - top), 0.0) for s in range(WIN + 1)]
        total = weights[0]
        for s in range(1, WIN + 1):
            total = total + weights[s]
        total = jnp.sum(total, axis=1, keepdims=True)
        numer = None
        for s in range(WIN + 1):
            half = weights[s].astype(BF16)
            prob_ref[h, s] = half
            if s == 0:
                value = value_ref[:, lanes]
            else:
                value = halos[s - 1][0:size, 2 * width + h * DH : 2 * width + (h + 1) * DH]
            term = mm(half, value)
            numer = term if numer is None else numer + term
        att = numer / total
        att_ref[:, lanes] = att
        tot_ref[h] = jnp.broadcast_to(total, (size, 8))
        weighted = cot_ref[:, lanes].astype(F32) * gain_ref[:, lanes]
        square = square + jnp.sum(att * att, axis=1, keepdims=True)
        inner = inner + jnp.sum(weighted * att, axis=1, keepdims=True)
    row = jnp.concatenate([to_row(square, eye), to_row(inner, eye)], axis=1)
    sums_ref[...] = jnp.broadcast_to(row, sums_ref.shape)


def back_kernel(
    heads,
    features,
    sums_ref,
    att_ref,
    tot_ref,
    prob_ref,
    frame_ref,
    kt_ref,
    value_ref,
    cot_ref,
    gain_ref,
    far_ref,
    normed_ref,
    part_ref,
    own_ref,
    dval_ref,
    cross_ref,
    send2_ref,
    send4_ref,
):
    size = value_ref.shape[0]
    width = heads * DH
    block = 3 * width
    places = ((cross_ref, 0), (send2_ref, 0), (cross_ref, block), (send4_ref, 0))
    rows, cols = grids(size)
    eye = rows == cols
    sums = jnp.sum(sums_ref[...], axis=0, keepdims=True)
    square = to_col(sums[:, 0:size], eye)
    inner = to_col(sums[:, size : 2 * size], eye)
    inverse = lax.rsqrt(square / features + EPSILON)
    pull = inverse * inverse * inverse * inner / features
    att_all = att_ref[...]
    cot_all = cot_ref[...].astype(F32)
    gain = gain_ref[...]
    normed = att_all * inverse
    normed_ref[...] = (normed * gain).astype(BF16)
    part = jnp.sum(cot_all * normed, axis=0, keepdims=True)
    part_ref[...] = part
    cross_ref[size : size + 16, 0:width] = rate_pieces(part, 16, width)
    cross_ref[size : size + 16, width : 2 * block] = jnp.zeros((16, 2 * block - width), BF16)
    send4_ref[:, 2 * width : block] = jnp.zeros((size, width), BF16)
    grad_att = cot_all * gain * inverse - att_all * pull
    scale = DH ** (-0.5)
    for h in range(heads):
        lanes = slice(h * DH, (h + 1) * DH)
        total = tot_ref[h, :, 0:1]
        grad = grad_att[:, lanes]
        scaled = (grad / total).astype(BF16)
        delta = jnp.sum(grad * att_all[:, lanes], axis=1, keepdims=True) / total
        carried = None
        for s in range(WIN, -1, -1):
            if s == 0:
                value = value_ref[:, lanes]
            else:
                value = far_ref[s - 1, :, lanes]
            prob = prob_ref[h, s]
            through = mm(scaled, value, "nt")
            dscore = (prob.astype(F32) * ((through - delta) * scale)).astype(BF16)
            dvalue = mm(prob, scaled, "tn")
            if s == 0:
                dval_ref[:, lanes] = dvalue
                own_ref[h] = jnp.concatenate([dscore, carried], axis=1)
                continue
            send, base = places[s - 1]
            at_value = slice(base + h * DH, base + (h + 1) * DH)
            at_end = slice(base + width + h * DH, base + width + (h + 1) * DH)
            at_trans = slice(base + 2 * width + h * DH, base + 2 * width + (h + 1) * DH)
            send[0:size, at_value] = dvalue.astype(BF16)
            if carried is None:
                send[0:size, at_end] = mm(frame_ref[h, s - 1], dscore, "tn").astype(BF16)
                carried = mm(dscore, kt_ref[h, s - 1, :, 0:DH], "nt").astype(BF16)
            else:
                both = jnp.concatenate([dscore, carried], axis=1)
                grads = mm(frame_ref[h, s - 1], both, "tn").astype(BF16)
                send[0:size, at_end] = grads[:, 0:DH]
                send[0:size, at_trans] = grads[:, DH : 2 * DH]
                carried = mm(both, kt_ref[h, s - 1], "nt").astype(BF16)


def merge_kernel(part_ref, mine2_ref, mine4_ref, cross_ref, place_ref, parts_ref, near_ref, send2_ref, send4_ref):
    size, block = mine2_ref.shape
    width = part_ref.shape[1]
    other = jnp.sum(cross_ref[size : size + 16, 0:width].astype(F32), axis=0, keepdims=True)
    parts_ref[...] = jnp.broadcast_to(part_ref[...] + other, parts_ref.shape)

    @pl.when(place_ref[1] == 0)
    def _():
        near_ref[...] = cross_ref[0:size, 0:block]
        total = mine2_ref[...].astype(F32) + cross_ref[0:size, block : 2 * block].astype(F32)
        send2_ref[...] = total.astype(BF16)
        send4_ref[...] = mine4_ref[...]

    @pl.when(place_ref[1] != 0)
    def _():
        near_ref[...] = jnp.zeros((size, block), BF16)
        total = mine2_ref[...].astype(F32) + cross_ref[0:size, 0:block].astype(F32)
        send2_ref[...] = total.astype(BF16)
        total = mine4_ref[...].astype(F32) + cross_ref[0:size, block : 2 * block].astype(F32)
        send4_ref[...] = total.astype(BF16)


def local_kernel(heads, own_ref, kw_ref, query_ref, key_ref, dir_ref, dquery_ref, dkey_ref, ddir_ref, pulled_ref):
    size = query_ref.shape[0]
    rows, cols = grids(size)
    eye = rows == cols
    lower = rows >= cols
    for h in range(heads):
        lanes = slice(h * DH, (h + 1) * DH)
        query = query_ref[:, lanes]
        keys = key_ref[:, lanes]
        raw_dirs = dir_ref[:, lanes].astype(F32)
        norm_col = lax.rsqrt(jnp.sum(raw_dirs * raw_dirs, axis=1, keepdims=True) + EPSILON)
        unit = (raw_dirs * norm_col).astype(BF16)
        grads = own_ref[h]
        applied = jnp.where(lower, mm(query, unit, "nt"), 0.0).astype(BF16)
        dapplied = jnp.where(lower, mm(grads, kw_ref[h], "nt"), 0.0).astype(BF16)
        dquery = mm(grads[:, 0:DH], keys) + grads[:, DH : 2 * DH].astype(F32) - mm(dapplied, unit)
        dquery_ref[:, lanes] = dquery.astype(BF16)
        dkey_ref[h] = mm(grads[:, 0:DH], query, "tn")
        ddir_ref[h] = -mm(dapplied, query, "tn")
        pulled_ref[h] = mm(applied, grads, "tn")


def shard_kernel(
    heads,
    near_ref,
    recv2_ref,
    recv4_ref,
    inv_ref,
    kw_ref,
    pulled_ref,
    dkey_in_ref,
    ddir_in_ref,
    dval_in_ref,
    key_ref,
    dir_ref,
    rate_ref,
    parts_ref,
    dkey_ref,
    dvalue_ref,
    ddir_ref,
    drate_ref,
    dgain_ref,
):
    size = key_ref.shape[0]
    width = heads * DH
    recvs = (near_ref, recv2_ref, recv4_ref)
    rows, cols = grids(size)
    eye = rows == cols
    strict = rows > cols
    dvalue = dval_in_ref[...]
    for recv in recvs:
        dvalue = dvalue + recv[:, 0:width].astype(F32)
    dvalue_ref[...] = dvalue.astype(BF16)
    dgain_ref[...] = jnp.sum(parts_ref[...], axis=0, keepdims=True)
    for h in range(heads):
        lanes = slice(h * DH, (h + 1) * DH)
        keys = key_ref[:, lanes]
        raw_dirs = dir_ref[:, lanes].astype(F32)
        norm_col = lax.rsqrt(jnp.sum(raw_dirs * raw_dirs, axis=1, keepdims=True) + EPSILON)
        unit = raw_dirs * norm_col
        unit_half = unit.astype(BF16)
        rate_col = to_col(rate_ref[h : h + 1, :], eye)
        dend = jnp.zeros((size, DH), F32)
        dtrans = jnp.zeros((size, DH), F32)
        for recv in recvs:
            dend = dend + recv[:, width + h * DH : width + (h + 1) * DH].astype(F32)
            dtrans = dtrans + recv[:, 2 * width + h * DH : 2 * width + (h + 1) * DH].astype(F32)
        both = jnp.concatenate([dend, dtrans], axis=1).astype(BF16)
        coef = kw_ref[h]
        dcoef = -(pulled_ref[h] + mm(unit_half, both))
        solved = mm(inv_ref[h], dcoef, "tn")
        dstrict = jnp.where(strict, -mm(solved, coef, "nt"), 0.0)
        dinner = jnp.where(strict, solved[:, 0:DH], 0.0).astype(BF16)
        local = mm(dstrict, unit_half) + mm(dinner, keys) + solved[:, DH : 2 * DH]
        dunit = (
            rate_col * local
            + mm(rate_col * dstrict, unit_half, "tn")
            + ddir_in_ref[h]
            - mm(coef, both, "nt")
        )
        drate_ref[h : h + 1, :] = to_row(jnp.sum(local * unit, axis=1, keepdims=True), eye)
        dkey_ref[:, lanes] = (
            dkey_in_ref[h] + mm(dinner, rate_col * unit, "tn") + dend.T
        ).astype(BF16)
        along = jnp.sum(unit * dunit, axis=1, keepdims=True)
        ddir_ref[:, lanes] = (norm_col * (dunit - unit * along)).astype(BF16)


def call(body, outs, flops, *operands, scalars=(), scratch=()):
    vmem = pl.BlockSpec(memory_space=pltpu.VMEM)
    smem = pl.BlockSpec(memory_space=pltpu.SMEM)
    moved = sum(x.size * x.dtype.itemsize for x in operands) + sum(
        jnp.dtype(d).itemsize * functools.reduce(lambda a, b: a * b, s) for s, d in outs
    )
    return pl.pallas_call(
        body,
        out_shape=[jax.ShapeDtypeStruct(s, d) for s, d in outs],
        in_specs=[vmem] * len(operands) + [smem] * len(scalars),
        out_specs=[vmem] * len(outs),
        scratch_shapes=list(scratch),
        compiler_params=pltpu.CompilerParams(vmem_limit_bytes=VMEM_LIMIT),
        cost_estimate=pl.CostEstimate(flops=flops, bytes_accessed=moved, transcendentals=0),
    )(*operands, *scalars)


def passed_along(value, steps):
    count = lax.axis_size("ctx")
    first, last = (max(0, -steps), min(count, count - steps))
    return lax.ppermute(value, "ctx", [(source, source + steps) for source in range(first, last)])


def paired(value, first, step):
    count = lax.axis_size("ctx")
    return lax.ppermute(value, "ctx", [(source, source + step) for source in range(first, count, 2)])


def swapped(value):
    count = lax.axis_size("ctx")
    return lax.ppermute(value, "ctx", [(source, source ^ 1) for source in range(count)])


def gathered(value, axis, groups=None):
    return lax.all_to_all(value, axis, 0, 0, axis_index_groups=groups, tiled=True)


def per_device(query, keys, values, dirs, rates, gain, doc_lengths, cotangent):
    size, width = query.shape
    heads = width // DH
    features = width * lax.axis_size("head")
    gain_row = gain.reshape(1, width)
    ctx = lax.axis_index("ctx").astype(jnp.int32)
    place = jnp.stack([ctx * size, ctx % 2])
    unit_flops = 2 * size * size * DH
    packed = pack(keys, dirs, values, rates)
    halo2 = passed_along(packed, 2)
    halo4 = passed_along(packed, 4)
    inverse, coef, raw = call(
        own_kernel,
        [((heads, size, size), BF16), ((heads, size, 2 * DH), BF16), ((heads, size, 2 * DH), F32)],
        heads * 60 * unit_flops,
        query,
        keys,
        dirs,
        rates,
    )
    halo2, raw = lax.optimization_barrier((halo2, raw))
    halos = (halo2, halo4, paired(packed, 0, 1), swapped(halo2), paired(halo4, 1, -1))
    att, total, prob, frame, carry, sums, far = call(
        functools.partial(attend_kernel, heads),
        [
            ((size, width), F32),
            ((heads, size, 8), F32),
            ((heads, WIN + 1, size, size), BF16),
            ((heads, WIN, size, DH), BF16),
            ((heads, WIN, DH, 2 * DH), BF16),
            ((lax.axis_size("head"), 2 * size), F32),
            ((WIN, size, width), BF16),
        ],
        heads * 300 * unit_flops,
        raw,
        values,
        cotangent,
        gain_row,
        *halos,
        scalars=(doc_lengths, place),
        scratch=[pltpu.VMEM((size + 16, 3 * width), BF16)] * 2,
    )
    sums = gathered(sums, "head")
    normed, part, own, dval, cross, mine2, mine4 = call(
        functools.partial(back_kernel, heads, features),
        [
            ((size, width), BF16),
            ((1, width), F32),
            ((heads, size, 2 * DH), BF16),
            ((size, width), F32),
            ((size + 16, 6 * width), BF16),
            ((size, 3 * width), BF16),
            ((size, 3 * width), BF16),
        ],
        heads * 30 * unit_flops,
        sums,
        att,
        total,
        prob,
        frame,
        carry,
        values,
        cotangent,
        gain_row,
        far,
    )
    count = lax.axis_size("ctx")
    parts, near, send2, send4 = call(
        merge_kernel,
        [((count // 2, width), F32)] + [((size, 3 * width), BF16)] * 3,
        0,
        part,
        mine2,
        mine4,
        swapped(cross),
        scalars=(place,),
    )
    recvs = (near, passed_along(send2, -2), passed_along(send4, -4))
    dquery, dkey_part, ddir_part, pulled = call(
        functools.partial(local_kernel, heads),
        [
            ((size, width), BF16),
            ((heads, size, DH), F32),
            ((heads, size, DH), F32),
            ((heads, size, 2 * DH), F32),
        ],
        heads * 10 * unit_flops,
        own,
        coef,
        query,
        keys,
        dirs,
    )
    parts = gathered(parts, "ctx", [list(range(core, count, 2)) for core in range(2)])
    dkey, dvalue, ddir, drate, dgain = call(
        functools.partial(shard_kernel, heads),
        [((size, width), BF16), ((size, width), BF16), ((size, width), BF16), ((heads, size), F32), ((1, width), F32)],
        heads * 20 * unit_flops,
        *recvs,
        inverse,
        coef,
        pulled,
        dkey_part,
        ddir_part,
        dval,
        keys,
        dirs,
        rates,
        parts,
    )
    return normed, dquery, dkey, dvalue, ddir, drate, dgain.reshape(width)


def solution(mesh):
    rows = P("ctx", "head")
    return jax.shard_map(
        per_device,
        mesh=mesh,
        in_specs=(rows, rows, rows, rows, P("head", "ctx"), P("head"), P(), rows),
        out_specs=(rows, rows, rows, rows, rows, P("head", "ctx"), P("head")),
        check_vma=False,
    )
```

```python
import functools

import jax
import jax.numpy as jnp
from jax import lax
from jax.experimental import pallas as pl
from jax.experimental.pallas import tpu as pltpu
from jax.sharding import PartitionSpec as P

DH = 128
WIN = 4
NEG_FILL = -1e30
EPSILON = 1e-06
F32 = jnp.float32
BF16 = jnp.bfloat16
VMEM_LIMIT = 48 * 1024 * 1024


def mm(left, right, form="nn"):
    lhs = 0 if form[0] == "t" else 1
    rhs = 1 if form[1] == "t" else 0
    return lax.dot_general(
        left.astype(BF16), right.astype(BF16), (((lhs,), (rhs,)), ((), ())), preferred_element_type=F32
    )


def split(value):
    high = value.astype(BF16)
    low = (value - high.astype(F32)).astype(BF16)
    return high, low


def mm3(left, right):
    lh, ll = split(left)
    rh, rl = split(right)
    return mm(jnp.concatenate([lh, lh, ll], axis=1), jnp.concatenate([rh, rl, rh], axis=0))


def grids(size):
    rows = lax.broadcasted_iota(jnp.int32, (size, size), 0)
    cols = lax.broadcasted_iota(jnp.int32, (size, size), 1)
    return rows, cols


def to_col(row, eye):
    return jnp.sum(jnp.where(eye, row, 0.0), axis=1, keepdims=True)


def to_row(col, eye):
    return jnp.sum(jnp.where(eye, col, 0.0), axis=0, keepdims=True)


def unit_lower_inverses(strict_list):
    size = strict_list[0].shape[0]
    rows, cols = grids(size)
    eye = jnp.where(rows == cols, 1.0, 0.0)
    pair = (rows // 2 == cols // 2) & (rows > cols)
    inverses = [eye - jnp.where(pair, strict, 0.0) for strict in strict_list]
    width = 2
    while width < size:
        wide = min(4 * width, size)
        between = (rows // wide == cols // wide) & (rows // width > cols // width)
        parts = [jnp.where(between, strict, 0.0) for strict in strict_list]
        steps = [mm3(inverse, part) for inverse, part in zip(inverses, parts)]
        once = [inverse - mm3(step, inverse) for step, inverse in zip(steps, inverses)]
        if wide > 2 * width:
            twice = [mm3(step, step) for step in steps]
            inverses = [first + mm3(second, first) for first, second in zip(once, twice)]
        else:
            inverses = once
        width = wide
    return inverses


def shard_scales(dirs, rate_row, eye):
    gram = mm(dirs, dirs, "nt")
    square = jnp.where(eye, gram, 0.0)
    norm_row = lax.rsqrt(jnp.sum(square, axis=0, keepdims=True) + EPSILON)
    norm_col = lax.rsqrt(jnp.sum(square, axis=1, keepdims=True) + EPSILON)
    rate_col = to_col(rate_row, eye)
    return gram, norm_row, norm_col, rate_col


def prepare(shards):
    size = shards[0][0].shape[0]
    rows, cols = grids(size)
    eye = rows == cols
    strict = rows > cols
    grams, rights, norms = [], [], []
    for dirs, keys, rate_row in shards:
        gram, norm_row, norm_col, rate_col = shard_scales(dirs, rate_row, eye)
        scale = rate_col * norm_col
        grams.append(jnp.where(strict, gram * norm_row * scale, 0.0))
        rights.append(
            jnp.concatenate(
                [jnp.where(strict, mm(dirs, keys, "nt") * scale, 0.0), dirs.astype(F32) * scale], axis=1
            )
        )
        norms.append((norm_row, norm_col))
    inverses = unit_lower_inverses(grams)
    return [
        (inverse, mm3(inverse, right), norm) for inverse, right, norm in zip(inverses, rights, norms)
    ]


def rate_pieces(row, height, width):
    first = row.astype(BF16).astype(F32)
    rest = row - first
    second = rest.astype(BF16).astype(F32)
    third = rest - second
    at = lax.broadcasted_iota(jnp.int32, (height, width), 0)
    return jnp.where(at == 0, first, jnp.where(at == 1, second, jnp.where(at == 2, third, 0.0))).astype(BF16)


def pack_kernel(key_ref, dir_ref, value_ref, rate_ref, out_ref, rate_in, sems):
    size, width = key_ref.shape
    heads = rate_ref.shape[0]
    bring = pltpu.make_async_copy(rate_ref, rate_in, sems.at[3])
    bring.start()
    copies = [
        pltpu.make_async_copy(
            ref, out_ref.at[pl.ds(0, size), pl.ds(at * width, width)], sems.at[at]
        )
        for at, ref in enumerate((key_ref, dir_ref, value_ref))
    ]
    for copy in copies:
        copy.start()
    bring.wait()
    rate = jnp.concatenate([rate_in[h : h + 1, :] for h in range(heads)], axis=1)
    out_ref[size : size + 16, 0:width] = rate_pieces(rate, 16, width)
    out_ref[size : size + 16, width : 3 * width] = jnp.zeros((16, 2 * width), BF16)
    for copy in copies:
        copy.wait()


def pack(keys, dirs, values, rates):
    size, width = keys.shape
    return pl.pallas_call(
        pack_kernel,
        out_shape=jax.ShapeDtypeStruct((size + 16, 3 * width), BF16),
        in_specs=[pl.BlockSpec(memory_space=pl.ANY)] * 4,
        out_specs=pl.BlockSpec(memory_space=pltpu.VMEM),
        scratch_shapes=[pltpu.VMEM(rates.shape, F32), pltpu.SemaphoreType.DMA((4,))],
    )(keys, dirs, values, rates)


def own_kernel(query_ref, key_ref, dir_ref, rate_ref, inv_ref, kw_ref, raw_ref):
    size = query_ref.shape[0]
    heads = rate_ref.shape[0]
    rows, cols = grids(size)
    shards = []
    for h in range(heads):
        lanes = slice(h * DH, (h + 1) * DH)
        shards.append((dir_ref[:, lanes], key_ref[:, lanes], rate_ref[h : h + 1, :]))
    prepared = prepare(shards)
    for h in range(heads):
        lanes = slice(h * DH, (h + 1) * DH)
        inverse, coef, (norm_row, _) = prepared[h]
        query = query_ref[:, lanes]
        dirs, keys, _ = shards[h]
        applied = jnp.where(rows >= cols, mm(query, dirs, "nt") * norm_row, 0.0)
        base = jnp.concatenate([mm(query, keys, "nt"), query.astype(F32)], axis=1)
        raw_ref[h] = base - mm3(applied, coef)
        inv_ref[h] = inverse.astype(BF16)
        kw_ref[h] = coef.astype(BF16)


def attend_kernel(
    heads,
    raw_ref,
    value_ref,
    cot_ref,
    gain_ref,
    halo2_ref,
    halo4_ref,
    even_ref,
    cross2_ref,
    cross4_ref,
    len_ref,
    place_ref,
    att_ref,
    tot_ref,
    prob_ref,
    frame_ref,
    kt_ref,
    sums_ref,
    far_ref,
    halo1_ref,
    halo3_ref,
):
    size = value_ref.shape[0]
    width = heads * DH

    @pl.when(place_ref[1] == 0)
    def _():
        halo1_ref[...] = cross2_ref[...]
        halo3_ref[...] = cross4_ref[...]

    @pl.when(place_ref[1] != 0)
    def _():
        halo1_ref[...] = even_ref[...]
        halo3_ref[...] = cross2_ref[...]

    halos = (halo1_ref, halo2_ref, halo3_ref, halo4_ref)
    for s in range(WIN):
        far_ref[s] = halos[s][0:size, 2 * width : 3 * width]
    rows, cols = grids(size)
    eye = rows == cols
    eye_f = jnp.where(eye, 1.0, 0.0)
    first = place_ref[0]
    pos_row = first + lax.broadcasted_iota(jnp.int32, (1, size), 1)
    start_row = jnp.zeros((1, size), jnp.int32)
    end = jnp.int32(0)
    for d in range(len_ref.shape[0]):
        end = end + len_ref[d]
        start_row = jnp.where(end <= pos_row, end, start_row)
    start = to_col(start_row.astype(F32), eye).astype(jnp.int32)
    seen = [(rows >= cols) & (first + cols >= start)]
    for s in range(1, WIN + 1):
        seen.append(first - s * size + cols >= start)
    shards = []
    for s in range(WIN):
        for h in range(heads):
            keys = halos[s][0:size, h * DH : (h + 1) * DH]
            dirs = halos[s][0:size, width + h * DH : width + (h + 1) * DH]
            rate = halos[s][size : size + 16, h * DH : (h + 1) * DH].astype(F32)
            shards.append((dirs, keys, jnp.sum(rate, axis=0, keepdims=True)))
    prepared = prepare(shards)
    carry = []
    for (dirs, keys, _), (_, coef, (_, norm_col)) in zip(shards, prepared):
        base = jnp.concatenate([keys.astype(F32).T, eye_f], axis=1)
        high, low = split(coef * norm_col)
        turned = dirs.astype(F32).T.astype(BF16)
        carry.append(base - (mm(turned, high) + mm(turned, low)))
    square = jnp.zeros((size, 1), F32)
    inner = jnp.zeros((size, 1), F32)
    for h in range(heads):
        lanes = slice(h * DH, (h + 1) * DH)
        scores = [raw_ref[h, :, 0:DH]]
        frame = raw_ref[h, :, DH : 2 * DH]
        for s in range(WIN):
            matrix = carry[s * heads + h]
            kt_ref[h, s] = matrix.astype(BF16)
            frame_ref[h, s] = frame.astype(BF16)
            if s < WIN - 1:
                product = mm3(frame, matrix)
                scores.append(product[:, 0:DH])
                frame = product[:, DH : 2 * DH]
            else:
                scores.append(mm3(frame, matrix[:, 0:DH]))
        scaled = [
            jnp.where(seen[s], scores[s] * (DH ** (-0.5)), NEG_FILL) for s in range(WIN + 1)
        ]
        top = scaled[0]
        for s in range(1, WIN + 1):
            top = jnp.maximum(top, scaled[s])
        top = jnp.max(top, axis=1, keepdims=True)
        weights = [jnp.where(seen[s], jnp.exp(scaled[s] - top), 0.0) for s in range(WIN + 1)]
        total = weights[0]
        for s in range(1, WIN + 1):
            total = total + weights[s]
        total = jnp.sum(total, axis=1, keepdims=True)
        numer = None
        for s in range(WIN + 1):
            half = weights[s].astype(BF16)
            prob_ref[h, s] = half
            if s == 0:
                value = value_ref[:, lanes]
            else:
                value = halos[s - 1][0:size, 2 * width + h * DH : 2 * width + (h + 1) * DH]
            term = mm(half, value)
            numer = term if numer is None else numer + term
        att = numer / total
        att_ref[:, lanes] = att
        tot_ref[h] = jnp.broadcast_to(total, (size, 8))
        weighted = cot_ref[:, lanes].astype(F32) * gain_ref[:, lanes]
        square = square + jnp.sum(att * att, axis=1, keepdims=True)
        inner = inner + jnp.sum(weighted * att, axis=1, keepdims=True)
    row = jnp.concatenate([to_row(square, eye), to_row(inner, eye)], axis=1)
    sums_ref[...] = jnp.broadcast_to(row[None], sums_ref.shape)


def back_kernel(
    heads,
    features,
    sums_ref,
    att_ref,
    tot_ref,
    prob_ref,
    frame_ref,
    kt_ref,
    value_ref,
    cot_ref,
    gain_ref,
    far_ref,
    normed_ref,
    part_ref,
    own_ref,
    dval_ref,
    cross_ref,
    send2_ref,
    send4_ref,
):
    size = value_ref.shape[0]
    width = heads * DH
    block = 3 * width
    places = ((cross_ref, 0), (send2_ref, 0), (cross_ref, block), (send4_ref, 0))
    rows, cols = grids(size)
    eye = rows == cols
    sums = jnp.sum(sums_ref[...], axis=0)
    square = to_col(sums[:, 0:size], eye)
    inner = to_col(sums[:, size : 2 * size], eye)
    inverse = lax.rsqrt(square / features + EPSILON)
    pull = inverse * inverse * inverse * inner / features
    att_all = att_ref[...]
    cot_all = cot_ref[...].astype(F32)
    gain = gain_ref[...]
    normed = att_all * inverse
    normed_ref[...] = (normed * gain).astype(BF16)
    part = jnp.sum(cot_all * normed, axis=0, keepdims=True)
    part_ref[...] = part
    cross_ref[size : size + 16, 0:width] = rate_pieces(part, 16, width)
    cross_ref[size : size + 16, width : 2 * block] = jnp.zeros((16, 2 * block - width), BF16)
    send4_ref[:, 2 * width : block] = jnp.zeros((size, width), BF16)
    grad_att = cot_all * gain * inverse - att_all * pull
    scale = DH ** (-0.5)
    for h in range(heads):
        lanes = slice(h * DH, (h + 1) * DH)
        total = tot_ref[h, :, 0:1]
        grad = grad_att[:, lanes]
        scaled = (grad / total).astype(BF16)
        delta = jnp.sum(grad * att_all[:, lanes], axis=1, keepdims=True) / total
        carried = None
        for s in range(WIN, -1, -1):
            if s == 0:
                value = value_ref[:, lanes]
            else:
                value = far_ref[s - 1, :, lanes]
            prob = prob_ref[h, s]
            through = mm(scaled, value, "nt")
            dscore = (prob.astype(F32) * ((through - delta) * scale)).astype(BF16)
            dvalue = mm(prob, scaled, "tn")
            if s == 0:
                dval_ref[:, lanes] = dvalue
                own_ref[h] = jnp.concatenate([dscore, carried], axis=1)
                continue
            send, base = places[s - 1]
            at_value = slice(base + h * DH, base + (h + 1) * DH)
            at_end = slice(base + width + h * DH, base + width + (h + 1) * DH)
            at_trans = slice(base + 2 * width + h * DH, base + 2 * width + (h + 1) * DH)
            send[0:size, at_value] = dvalue.astype(BF16)
            if carried is None:
                send[0:size, at_end] = mm(frame_ref[h, s - 1], dscore, "tn").astype(BF16)
                carried = mm(dscore, kt_ref[h, s - 1, :, 0:DH], "nt").astype(BF16)
            else:
                both = jnp.concatenate([dscore, carried], axis=1)
                grads = mm(frame_ref[h, s - 1], both, "tn").astype(BF16)
                send[0:size, at_end] = grads[:, 0:DH]
                send[0:size, at_trans] = grads[:, DH : 2 * DH]
                carried = mm(both, kt_ref[h, s - 1], "nt").astype(BF16)


def merge_kernel(part_ref, mine2_ref, mine4_ref, cross_ref, place_ref, parts_ref, near_ref, send2_ref, send4_ref):
    size, block = mine2_ref.shape
    width = part_ref.shape[1]
    other = jnp.sum(cross_ref[size : size + 16, 0:width].astype(F32), axis=0, keepdims=True)
    parts_ref[...] = jnp.broadcast_to((part_ref[...] + other)[None], parts_ref.shape)

    @pl.when(place_ref[1] == 0)
    def _():
        near_ref[...] = cross_ref[0:size, 0:block]
        total = mine2_ref[...].astype(F32) + cross_ref[0:size, block : 2 * block].astype(F32)
        send2_ref[...] = total.astype(BF16)
        send4_ref[...] = mine4_ref[...]

    @pl.when(place_ref[1] != 0)
    def _():
        near_ref[...] = jnp.zeros((size, block), BF16)
        total = mine2_ref[...].astype(F32) + cross_ref[0:size, 0:block].astype(F32)
        send2_ref[...] = total.astype(BF16)
        total = mine4_ref[...].astype(F32) + cross_ref[0:size, block : 2 * block].astype(F32)
        send4_ref[...] = total.astype(BF16)


def local_kernel(heads, own_ref, kw_ref, query_ref, key_ref, dir_ref, dquery_ref, dkey_ref, ddir_ref, pulled_ref):
    size = query_ref.shape[0]
    rows, cols = grids(size)
    eye = rows == cols
    lower = rows >= cols
    for h in range(heads):
        lanes = slice(h * DH, (h + 1) * DH)
        query = query_ref[:, lanes]
        keys = key_ref[:, lanes]
        raw_dirs = dir_ref[:, lanes].astype(F32)
        norm_col = lax.rsqrt(jnp.sum(raw_dirs * raw_dirs, axis=1, keepdims=True) + EPSILON)
        unit = (raw_dirs * norm_col).astype(BF16)
        grads = own_ref[h]
        applied = jnp.where(lower, mm(query, unit, "nt"), 0.0).astype(BF16)
        dapplied = jnp.where(lower, mm(grads, kw_ref[h], "nt"), 0.0).astype(BF16)
        dquery = mm(grads[:, 0:DH], keys) + grads[:, DH : 2 * DH].astype(F32) - mm(dapplied, unit)
        dquery_ref[:, lanes] = dquery.astype(BF16)
        dkey_ref[h] = mm(grads[:, 0:DH], query, "tn")
        ddir_ref[h] = -mm(dapplied, query, "tn")
        pulled_ref[h] = mm(applied, grads, "tn")


def shard_kernel(
    heads,
    near_ref,
    recv2_ref,
    recv4_ref,
    inv_ref,
    kw_ref,
    pulled_ref,
    dkey_in_ref,
    ddir_in_ref,
    dval_in_ref,
    key_ref,
    dir_ref,
    rate_ref,
    parts_ref,
    dkey_ref,
    dvalue_ref,
    ddir_ref,
    drate_ref,
    dgain_ref,
):
    size = key_ref.shape[0]
    width = heads * DH
    recvs = (near_ref, recv2_ref, recv4_ref)
    rows, cols = grids(size)
    eye = rows == cols
    strict = rows > cols
    dvalue = dval_in_ref[...]
    for recv in recvs:
        dvalue = dvalue + recv[:, 0:width].astype(F32)
    dvalue_ref[...] = dvalue.astype(BF16)
    dgain_ref[...] = jnp.sum(parts_ref[...], axis=0)
    for h in range(heads):
        lanes = slice(h * DH, (h + 1) * DH)
        keys = key_ref[:, lanes]
        raw_dirs = dir_ref[:, lanes].astype(F32)
        norm_col = lax.rsqrt(jnp.sum(raw_dirs * raw_dirs, axis=1, keepdims=True) + EPSILON)
        unit = raw_dirs * norm_col
        unit_half = unit.astype(BF16)
        rate_col = to_col(rate_ref[h : h + 1, :], eye)
        dend = jnp.zeros((size, DH), F32)
        dtrans = jnp.zeros((size, DH), F32)
        for recv in recvs:
            dend = dend + recv[:, width + h * DH : width + (h + 1) * DH].astype(F32)
            dtrans = dtrans + recv[:, 2 * width + h * DH : 2 * width + (h + 1) * DH].astype(F32)
        both = jnp.concatenate([dend, dtrans], axis=1).astype(BF16)
        coef = kw_ref[h]
        dcoef = -(pulled_ref[h] + mm(unit_half, both))
        solved = mm(inv_ref[h], dcoef, "tn")
        dstrict = jnp.where(strict, -mm(solved, coef, "nt"), 0.0)
        dinner = jnp.where(strict, solved[:, 0:DH], 0.0).astype(BF16)
        local = mm(dstrict, unit_half) + mm(dinner, keys) + solved[:, DH : 2 * DH]
        dunit = (
            rate_col * local
            + mm(rate_col * dstrict, unit_half, "tn")
            + ddir_in_ref[h]
            - mm(coef, both, "nt")
        )
        drate_ref[h : h + 1, :] = to_row(jnp.sum(local * unit, axis=1, keepdims=True), eye)
        dkey_ref[:, lanes] = (
            dkey_in_ref[h] + mm(dinner, rate_col * unit, "tn") + dend.T
        ).astype(BF16)
        along = jnp.sum(unit * dunit, axis=1, keepdims=True)
        ddir_ref[:, lanes] = (norm_col * (dunit - unit * along)).astype(BF16)


def call(body, outs, flops, *operands, scalars=(), scratch=()):
    vmem = pl.BlockSpec(memory_space=pltpu.VMEM)
    smem = pl.BlockSpec(memory_space=pltpu.SMEM)
    moved = sum(x.size * x.dtype.itemsize for x in operands) + sum(
        jnp.dtype(d).itemsize * functools.reduce(lambda a, b: a * b, s) for s, d in outs
    )
    return pl.pallas_call(
        body,
        out_shape=[jax.ShapeDtypeStruct(s, d) for s, d in outs],
        in_specs=[vmem] * len(operands) + [smem] * len(scalars),
        out_specs=[vmem] * len(outs),
        scratch_shapes=list(scratch),
        compiler_params=pltpu.CompilerParams(vmem_limit_bytes=VMEM_LIMIT),
        cost_estimate=pl.CostEstimate(flops=flops, bytes_accessed=moved, transcendentals=0),
    )(*operands, *scalars)


def passed_along(value, steps):
    count = lax.axis_size("ctx")
    first, last = (max(0, -steps), min(count, count - steps))
    return lax.ppermute(value, "ctx", [(source, source + steps) for source in range(first, last)])


def paired(value, first, step):
    count = lax.axis_size("ctx")
    return lax.ppermute(value, "ctx", [(source, source + step) for source in range(first, count, 2)])


def swapped(value):
    count = lax.axis_size("ctx")
    return lax.ppermute(value, "ctx", [(source, source ^ 1) for source in range(count)])


def gathered(value, axis, groups=None):
    return lax.all_to_all(value, axis, 0, 0, axis_index_groups=groups, tiled=True)


def per_device(query, keys, values, dirs, rates, gain, doc_lengths, cotangent):
    size, width = query.shape
    heads = width // DH
    features = width * lax.axis_size("head")
    gain_row = gain.reshape(1, width)
    ctx = lax.axis_index("ctx").astype(jnp.int32)
    place = jnp.stack([ctx * size, ctx & 1])
    unit_flops = 2 * size * size * DH
    packed = pack(keys, dirs, values, rates)
    halo2 = passed_along(packed, 2)
    halo4 = passed_along(packed, 4)
    inverse, coef, raw = call(
        own_kernel,
        [((heads, size, size), BF16), ((heads, size, 2 * DH), BF16), ((heads, size, 2 * DH), F32)],
        heads * 60 * unit_flops,
        query,
        keys,
        dirs,
        rates,
    )
    halo2, raw = lax.optimization_barrier((halo2, raw))
    even = paired(packed, 0, 1)
    cross2 = swapped(halo2)
    cross2, halo4 = lax.optimization_barrier((cross2, halo4))
    halos = (halo2, halo4, even, cross2, paired(halo4, 1, -1))
    att, total, prob, frame, carry, sums, far = call(
        functools.partial(attend_kernel, heads),
        [
            ((size, width), F32),
            ((heads, size, 8), F32),
            ((heads, WIN + 1, size, size), BF16),
            ((heads, WIN, size, DH), BF16),
            ((heads, WIN, DH, 2 * DH), BF16),
            ((lax.axis_size("head"), 1, 2 * size), F32),
            ((WIN, size, width), BF16),
        ],
        heads * 300 * unit_flops,
        raw,
        values,
        cotangent,
        gain_row,
        *halos,
        scalars=(doc_lengths, place),
        scratch=[pltpu.VMEM((size + 16, 3 * width), BF16)] * 2,
    )
    sums = gathered(sums, "head")
    normed, part, own, dval, cross, mine2, mine4 = call(
        functools.partial(back_kernel, heads, features),
        [
            ((size, width), BF16),
            ((1, width), F32),
            ((heads, size, 2 * DH), BF16),
            ((size, width), F32),
            ((size + 16, 6 * width), BF16),
            ((size, 3 * width), BF16),
            ((size, 3 * width), BF16),
        ],
        heads * 30 * unit_flops,
        sums,
        att,
        total,
        prob,
        frame,
        carry,
        values,
        cotangent,
        gain_row,
        far,
    )
    count = lax.axis_size("ctx")
    parts, near, send2, send4 = call(
        merge_kernel,
        [((count // 2, 1, width), F32)] + [((size, 3 * width), BF16)] * 3,
        0,
        part,
        mine2,
        mine4,
        swapped(cross),
        scalars=(place,),
    )
    dquery, dkey_part, ddir_part, pulled = call(
        functools.partial(local_kernel, heads),
        [
            ((size, width), BF16),
            ((heads, size, DH), F32),
            ((heads, size, DH), F32),
            ((heads, size, 2 * DH), F32),
        ],
        heads * 10 * unit_flops,
        own,
        coef,
        query,
        keys,
        dirs,
    )
    recvs = (near, passed_along(send2, -2), passed_along(send4, -4))
    parts = gathered(parts, "ctx", [list(range(core, count, 2)) for core in range(2)])
    dkey, dvalue, ddir, drate, dgain = call(
        functools.partial(shard_kernel, heads),
        [((size, width), BF16), ((size, width), BF16), ((size, width), BF16), ((heads, size), F32), ((1, width), F32)],
        heads * 20 * unit_flops,
        *recvs,
        inverse,
        coef,
        pulled,
        dkey_part,
        ddir_part,
        dval,
        keys,
        dirs,
        rates,
        parts,
    )
    return normed, dquery, dkey, dvalue, ddir, drate, dgain.reshape(width)


def solution(mesh):
    rows = P("ctx", "head")
    return jax.shard_map(
        per_device,
        mesh=mesh,
        in_specs=(rows, rows, rows, rows, P("head", "ctx"), P("head"), P(), rows),
        out_specs=(rows, rows, rows, rows, rows, P("head", "ctx"), P("head")),
        check_vma=False,
    )
```

```python
import functools

import jax
import jax.numpy as jnp
from jax import lax
from jax.experimental import pallas as pl
from jax.experimental.pallas import tpu as pltpu
from jax.sharding import PartitionSpec as P

DH = 128
WIN = 4
NEG_FILL = -1e30
EPSILON = 1e-06
F32 = jnp.float32
BF16 = jnp.bfloat16
VMEM_LIMIT = 48 * 1024 * 1024


def mm(left, right, form="nn"):
    lhs = 0 if form[0] == "t" else 1
    rhs = 1 if form[1] == "t" else 0
    return lax.dot_general(
        left.astype(BF16), right.astype(BF16), (((lhs,), (rhs,)), ((), ())), preferred_element_type=F32
    )


def split(value):
    high = value.astype(BF16)
    low = (value - high.astype(F32)).astype(BF16)
    return high, low


def mm3(left, right):
    lh, ll = split(left)
    rh, rl = split(right)
    return mm(jnp.concatenate([lh, lh, ll], axis=1), jnp.concatenate([rh, rl, rh], axis=0))


def grids(size):
    rows = lax.broadcasted_iota(jnp.int32, (size, size), 0)
    cols = lax.broadcasted_iota(jnp.int32, (size, size), 1)
    return rows, cols


def to_col(row, eye):
    return jnp.sum(jnp.where(eye, row, 0.0), axis=1, keepdims=True)


def to_row(col, eye):
    return jnp.sum(jnp.where(eye, col, 0.0), axis=0, keepdims=True)


def unit_lower_inverses(strict_list):
    size = strict_list[0].shape[0]
    rows, cols = grids(size)
    eye = jnp.where(rows == cols, 1.0, 0.0)
    pair = (rows // 2 == cols // 2) & (rows > cols)
    inverses = [eye - jnp.where(pair, strict, 0.0) for strict in strict_list]
    width = 2
    while width < size:
        wide = min(4 * width, size)
        between = (rows // wide == cols // wide) & (rows // width > cols // width)
        parts = [jnp.where(between, strict, 0.0) for strict in strict_list]
        steps = [mm3(inverse, part) for inverse, part in zip(inverses, parts)]
        once = [inverse - mm3(step, inverse) for step, inverse in zip(steps, inverses)]
        if wide > 2 * width:
            twice = [mm3(step, step) for step in steps]
            inverses = [first + mm3(second, first) for first, second in zip(once, twice)]
        else:
            inverses = once
        width = wide
    return inverses


def shard_scales(dirs, rate_row, eye):
    gram = mm(dirs, dirs, "nt")
    square = jnp.where(eye, gram, 0.0)
    norm_row = lax.rsqrt(jnp.sum(square, axis=0, keepdims=True) + EPSILON)
    norm_col = lax.rsqrt(jnp.sum(square, axis=1, keepdims=True) + EPSILON)
    rate_col = to_col(rate_row, eye)
    return gram, norm_row, norm_col, rate_col


def prepare(shards):
    size = shards[0][0].shape[0]
    rows, cols = grids(size)
    eye = rows == cols
    strict = rows > cols
    grams, rights, norms = [], [], []
    for dirs, keys, rate_row in shards:
        gram, norm_row, norm_col, rate_col = shard_scales(dirs, rate_row, eye)
        scale = rate_col * norm_col
        grams.append(jnp.where(strict, gram * norm_row * scale, 0.0))
        rights.append(
            jnp.concatenate(
                [jnp.where(strict, mm(dirs, keys, "nt") * scale, 0.0), dirs.astype(F32) * scale], axis=1
            )
        )
        norms.append((norm_row, norm_col))
    inverses = unit_lower_inverses(grams)
    return [
        (inverse, mm3(inverse, right), norm) for inverse, right, norm in zip(inverses, rights, norms)
    ]


def rate_pieces(row, height, width):
    first = row.astype(BF16).astype(F32)
    rest = row - first
    second = rest.astype(BF16).astype(F32)
    third = rest - second
    at = lax.broadcasted_iota(jnp.int32, (height, width), 0)
    return jnp.where(at == 0, first, jnp.where(at == 1, second, jnp.where(at == 2, third, 0.0))).astype(BF16)


def pack_kernel(key_ref, dir_ref, value_ref, rate_ref, out_ref, rate_in, sems):
    size, width = key_ref.shape
    heads = rate_ref.shape[0]
    bring = pltpu.make_async_copy(rate_ref, rate_in, sems.at[3])
    bring.start()
    copies = [
        pltpu.make_async_copy(
            ref, out_ref.at[pl.ds(0, size), pl.ds(at * width, width)], sems.at[at]
        )
        for at, ref in enumerate((key_ref, dir_ref, value_ref))
    ]
    for copy in copies:
        copy.start()
    bring.wait()
    rate = jnp.concatenate([rate_in[h : h + 1, :] for h in range(heads)], axis=1)
    out_ref[size : size + 16, 0:width] = rate_pieces(rate, 16, width)
    out_ref[size : size + 16, width : 3 * width] = jnp.zeros((16, 2 * width), BF16)
    for copy in copies:
        copy.wait()


def pack(keys, dirs, values, rates):
    size, width = keys.shape
    return pl.pallas_call(
        pack_kernel,
        out_shape=jax.ShapeDtypeStruct((size + 16, 3 * width), BF16),
        in_specs=[pl.BlockSpec(memory_space=pl.ANY)] * 4,
        out_specs=pl.BlockSpec(memory_space=pltpu.VMEM),
        scratch_shapes=[pltpu.VMEM(rates.shape, F32), pltpu.SemaphoreType.DMA((4,))],
    )(keys, dirs, values, rates)


def own_kernel(query_ref, key_ref, dir_ref, rate_ref, inv_ref, kw_ref, raw_ref):
    size = query_ref.shape[0]
    heads = rate_ref.shape[0]
    rows, cols = grids(size)
    shards = []
    for h in range(heads):
        lanes = slice(h * DH, (h + 1) * DH)
        shards.append((dir_ref[:, lanes], key_ref[:, lanes], rate_ref[h : h + 1, :]))
    prepared = prepare(shards)
    for h in range(heads):
        lanes = slice(h * DH, (h + 1) * DH)
        inverse, coef, (norm_row, _) = prepared[h]
        query = query_ref[:, lanes]
        dirs, keys, _ = shards[h]
        applied = jnp.where(rows >= cols, mm(query, dirs, "nt") * norm_row, 0.0)
        base = jnp.concatenate([mm(query, keys, "nt"), query.astype(F32)], axis=1)
        raw_ref[h] = base - mm3(applied, coef)
        inv_ref[h] = inverse.astype(BF16)
        kw_ref[h] = coef.astype(BF16)


def attend_kernel(
    heads,
    raw_ref,
    value_ref,
    cot_ref,
    gain_ref,
    halo2_ref,
    halo4_ref,
    even_ref,
    cross2_ref,
    cross4_ref,
    len_ref,
    place_ref,
    att_ref,
    tot_ref,
    prob_ref,
    frame_ref,
    kt_ref,
    sums_ref,
    far_ref,
    halo1_ref,
    halo3_ref,
):
    size = value_ref.shape[0]
    width = heads * DH

    @pl.when(place_ref[1] == 0)
    def _():
        halo1_ref[...] = cross2_ref[...]
        halo3_ref[...] = cross4_ref[...]

    @pl.when(place_ref[1] != 0)
    def _():
        halo1_ref[...] = even_ref[...]
        halo3_ref[...] = cross2_ref[...]

    halos = (halo1_ref, halo2_ref, halo3_ref, halo4_ref)
    for s in range(WIN):
        far_ref[s] = halos[s][0:size, 2 * width : 3 * width]
    rows, cols = grids(size)
    eye = rows == cols
    eye_f = jnp.where(eye, 1.0, 0.0)
    first = place_ref[0]
    pos_row = first + lax.broadcasted_iota(jnp.int32, (1, size), 1)
    start_row = jnp.zeros((1, size), jnp.int32)
    end = jnp.int32(0)
    for d in range(len_ref.shape[0]):
        end = end + len_ref[d]
        start_row = jnp.where(end <= pos_row, end, start_row)
    start = to_col(start_row.astype(F32), eye).astype(jnp.int32)
    seen = [(rows >= cols) & (first + cols >= start)]
    for s in range(1, WIN + 1):
        seen.append(first - s * size + cols >= start)
    shards = []
    for s in range(WIN):
        for h in range(heads):
            keys = halos[s][0:size, h * DH : (h + 1) * DH]
            dirs = halos[s][0:size, width + h * DH : width + (h + 1) * DH]
            rate = halos[s][size : size + 16, h * DH : (h + 1) * DH].astype(F32)
            shards.append((dirs, keys, jnp.sum(rate, axis=0, keepdims=True)))
    prepared = prepare(shards)
    carry = []
    for (dirs, keys, _), (_, coef, (_, norm_col)) in zip(shards, prepared):
        base = jnp.concatenate([keys.astype(F32).T, eye_f], axis=1)
        high, low = split(coef * norm_col)
        turned = dirs.astype(F32).T.astype(BF16)
        carry.append(base - (mm(turned, high) + mm(turned, low)))
    square = jnp.zeros((size, 1), F32)
    inner = jnp.zeros((size, 1), F32)
    for h in range(heads):
        lanes = slice(h * DH, (h + 1) * DH)
        scores = [raw_ref[h, :, 0:DH]]
        frame = raw_ref[h, :, DH : 2 * DH]
        for s in range(WIN):
            matrix = carry[s * heads + h]
            kt_ref[h, s] = matrix.astype(BF16)
            frame_ref[h, s] = frame.astype(BF16)
            if s < WIN - 1:
                product = mm3(frame, matrix)
                scores.append(product[:, 0:DH])
                frame = product[:, DH : 2 * DH]
            else:
                scores.append(mm3(frame, matrix[:, 0:DH]))
        scaled = [
            jnp.where(seen[s], scores[s] * (DH ** (-0.5)), NEG_FILL) for s in range(WIN + 1)
        ]
        top = scaled[0]
        for s in range(1, WIN + 1):
            top = jnp.maximum(top, scaled[s])
        top = jnp.max(top, axis=1, keepdims=True)
        weights = [jnp.where(seen[s], jnp.exp(scaled[s] - top), 0.0) for s in range(WIN + 1)]
        total = weights[0]
        for s in range(1, WIN + 1):
            total = total + weights[s]
        total = jnp.sum(total, axis=1, keepdims=True)
        numer = None
        for s in range(WIN + 1):
            half = weights[s].astype(BF16)
            prob_ref[h, s] = half
            if s == 0:
                value = value_ref[:, lanes]
            else:
                value = halos[s - 1][0:size, 2 * width + h * DH : 2 * width + (h + 1) * DH]
            term = mm(half, value)
            numer = term if numer is None else numer + term
        att = numer / total
        att_ref[:, lanes] = att
        tot_ref[h] = jnp.broadcast_to(total, (size, 8))
        weighted = cot_ref[:, lanes].astype(F32) * gain_ref[:, lanes]
        square = square + jnp.sum(att * att, axis=1, keepdims=True)
        inner = inner + jnp.sum(weighted * att, axis=1, keepdims=True)
    row = jnp.concatenate([to_row(square, eye), to_row(inner, eye)], axis=1)
    sums_ref[...] = jnp.broadcast_to(row[None], sums_ref.shape)


def back_block(h, s, scaled, delta, prob, value, frame, matrix, carried, send):
    width = scaled.shape[1]
    lanes = slice(h * DH, (h + 1) * DH)
    through = mm(scaled[:, lanes], value, "nt")
    dscore = (prob.astype(F32) * ((through - delta) * (DH ** (-0.5)))).astype(BF16)
    send[:, lanes] = mm(prob, scaled[:, lanes], "tn").astype(send.dtype)
    if frame is None:
        return jnp.concatenate([dscore, carried], axis=1)
    at_end = slice(width + h * DH, width + (h + 1) * DH)
    at_trans = slice(2 * width + h * DH, 2 * width + (h + 1) * DH)
    if carried is None:
        send[:, at_end] = mm(frame, dscore, "tn").astype(BF16)
        return mm(dscore, matrix[:, 0:DH], "nt").astype(BF16)
    both = jnp.concatenate([dscore, carried], axis=1)
    grads = mm(frame, both, "tn").astype(BF16)
    send[:, at_end] = grads[:, 0:DH]
    send[:, at_trans] = grads[:, DH : 2 * DH]
    return mm(both, matrix, "nt").astype(BF16)


def far_back_kernel(
    heads,
    features,
    sums_ref,
    att_ref,
    tot_ref,
    prob_ref,
    frame_ref,
    kt_ref,
    cot_ref,
    gain_ref,
    far_ref,
    normed_ref,
    parts_ref,
    scaled_ref,
    delta_ref,
    carried_ref,
    send3_ref,
    send4_ref,
):
    size = att_ref.shape[0]
    rows, cols = grids(size)
    eye = rows == cols
    sums = jnp.sum(sums_ref[...], axis=0)
    square = to_col(sums[:, 0:size], eye)
    inner = to_col(sums[:, size : 2 * size], eye)
    inverse = lax.rsqrt(square / features + EPSILON)
    pull = inverse * inverse * inverse * inner / features
    att_all = att_ref[...]
    cot_all = cot_ref[...].astype(F32)
    gain = gain_ref[...]
    normed = att_all * inverse
    normed_ref[...] = (normed * gain).astype(BF16)
    part = jnp.sum(cot_all * normed, axis=0, keepdims=True)
    parts_ref[...] = jnp.broadcast_to(part[None], parts_ref.shape)
    grad_att = cot_all * gain * inverse - att_all * pull
    for h in range(heads):
        lanes = slice(h * DH, (h + 1) * DH)
        total = tot_ref[h, :, 0:1]
        grad = grad_att[:, lanes]
        scaled_ref[:, lanes] = (grad / total).astype(BF16)
        delta = jnp.sum(grad * att_all[:, lanes], axis=1, keepdims=True) / total
        delta_ref[h] = jnp.broadcast_to(delta, (size, 8))
        carried = None
        for s, send in ((4, send4_ref), (3, send3_ref)):
            carried = back_block(
                h, s, scaled_ref, delta, prob_ref[h, s], far_ref[s - 1, :, lanes], frame_ref[h, s - 1], kt_ref[h, s - 1], carried, send
            )
        carried_ref[h] = carried


def near_back_kernel(
    heads,
    scaled_ref,
    delta_ref,
    carried_ref,
    prob_ref,
    frame_ref,
    kt_ref,
    value_ref,
    far_ref,
    own_ref,
    dval_ref,
    send1_ref,
    send2_ref,
):
    for h in range(heads):
        lanes = slice(h * DH, (h + 1) * DH)
        delta = delta_ref[h, :, 0:1]
        carried = carried_ref[h]
        for s, send in ((2, send2_ref), (1, send1_ref)):
            carried = back_block(
                h, s, scaled_ref, delta, prob_ref[h, s], far_ref[s - 1, :, lanes], frame_ref[h, s - 1], kt_ref[h, s - 1], carried, send
            )
        own_ref[h] = back_block(
            h, 0, scaled_ref, delta, prob_ref[h, 0], value_ref[:, lanes], None, None, carried, dval_ref
        )


def local_kernel(heads, own_ref, kw_ref, query_ref, key_ref, dir_ref, dquery_ref, dkey_ref, ddir_ref, pulled_ref):
    size = query_ref.shape[0]
    rows, cols = grids(size)
    eye = rows == cols
    lower = rows >= cols
    for h in range(heads):
        lanes = slice(h * DH, (h + 1) * DH)
        query = query_ref[:, lanes]
        keys = key_ref[:, lanes]
        raw_dirs = dir_ref[:, lanes].astype(F32)
        norm_col = lax.rsqrt(jnp.sum(raw_dirs * raw_dirs, axis=1, keepdims=True) + EPSILON)
        unit = (raw_dirs * norm_col).astype(BF16)
        grads = own_ref[h]
        applied = jnp.where(lower, mm(query, unit, "nt"), 0.0).astype(BF16)
        dapplied = jnp.where(lower, mm(grads, kw_ref[h], "nt"), 0.0).astype(BF16)
        dquery = mm(grads[:, 0:DH], keys) + grads[:, DH : 2 * DH].astype(F32) - mm(dapplied, unit)
        dquery_ref[:, lanes] = dquery.astype(BF16)
        dkey_ref[h] = mm(grads[:, 0:DH], query, "tn")
        ddir_ref[h] = -mm(dapplied, query, "tn")
        pulled_ref[h] = mm(applied, grads, "tn")


def shard_kernel(
    heads,
    recv1_ref,
    recv2_ref,
    recv3_ref,
    recv4_ref,
    inv_ref,
    kw_ref,
    pulled_ref,
    dkey_in_ref,
    ddir_in_ref,
    dval_in_ref,
    key_ref,
    dir_ref,
    rate_ref,
    parts_ref,
    dkey_ref,
    dvalue_ref,
    ddir_ref,
    drate_ref,
    dgain_ref,
):
    size = key_ref.shape[0]
    width = heads * DH
    recvs = (recv1_ref, recv2_ref, recv3_ref, recv4_ref)
    rows, cols = grids(size)
    eye = rows == cols
    strict = rows > cols
    dvalue = dval_in_ref[...]
    for recv in recvs:
        dvalue = dvalue + recv[:, 0:width].astype(F32)
    dvalue_ref[...] = dvalue.astype(BF16)
    dgain_ref[...] = jnp.sum(parts_ref[...], axis=0)
    for h in range(heads):
        lanes = slice(h * DH, (h + 1) * DH)
        keys = key_ref[:, lanes]
        raw_dirs = dir_ref[:, lanes].astype(F32)
        norm_col = lax.rsqrt(jnp.sum(raw_dirs * raw_dirs, axis=1, keepdims=True) + EPSILON)
        unit = raw_dirs * norm_col
        unit_half = unit.astype(BF16)
        rate_col = to_col(rate_ref[h : h + 1, :], eye)
        dend = jnp.zeros((size, DH), F32)
        dtrans = jnp.zeros((size, DH), F32)
        for recv in recvs:
            dend = dend + recv[:, width + h * DH : width + (h + 1) * DH].astype(F32)
            if recv.shape[1] == 3 * width:
                dtrans = dtrans + recv[:, 2 * width + h * DH : 2 * width + (h + 1) * DH].astype(F32)
        both = jnp.concatenate([dend, dtrans], axis=1).astype(BF16)
        coef = kw_ref[h]
        dcoef = -(pulled_ref[h] + mm(unit_half, both))
        solved = mm(inv_ref[h], dcoef, "tn")
        dstrict = jnp.where(strict, -mm(solved, coef, "nt"), 0.0)
        dinner = jnp.where(strict, solved[:, 0:DH], 0.0).astype(BF16)
        local = mm(dstrict, unit_half) + mm(dinner, keys) + solved[:, DH : 2 * DH]
        dunit = (
            rate_col * local
            + mm(rate_col * dstrict, unit_half, "tn")
            + ddir_in_ref[h]
            - mm(coef, both, "nt")
        )
        drate_ref[h : h + 1, :] = to_row(jnp.sum(local * unit, axis=1, keepdims=True), eye)
        dkey_ref[:, lanes] = (
            dkey_in_ref[h] + mm(dinner, rate_col * unit, "tn") + dend.T
        ).astype(BF16)
        along = jnp.sum(unit * dunit, axis=1, keepdims=True)
        ddir_ref[:, lanes] = (norm_col * (dunit - unit * along)).astype(BF16)


def call(body, outs, flops, *operands, scalars=(), scratch=()):
    vmem = pl.BlockSpec(memory_space=pltpu.VMEM)
    smem = pl.BlockSpec(memory_space=pltpu.SMEM)
    moved = sum(x.size * x.dtype.itemsize for x in operands) + sum(
        jnp.dtype(d).itemsize * functools.reduce(lambda a, b: a * b, s) for s, d in outs
    )
    return pl.pallas_call(
        body,
        out_shape=[jax.ShapeDtypeStruct(s, d) for s, d in outs],
        in_specs=[vmem] * len(operands) + [smem] * len(scalars),
        out_specs=[vmem] * len(outs),
        scratch_shapes=list(scratch),
        compiler_params=pltpu.CompilerParams(vmem_limit_bytes=VMEM_LIMIT),
        cost_estimate=pl.CostEstimate(flops=flops, bytes_accessed=moved if flops else 0, transcendentals=0),
    )(*operands, *scalars)


def passed_along(value, steps):
    count = lax.axis_size("ctx")
    first, last = (max(0, -steps), min(count, count - steps))
    return lax.ppermute(value, "ctx", [(source, source + steps) for source in range(first, last)])


def paired(value, first, step):
    count = lax.axis_size("ctx")
    return lax.ppermute(value, "ctx", [(source, source + step) for source in range(first, count, 2)])


def swapped(value):
    count = lax.axis_size("ctx")
    return lax.ppermute(value, "ctx", [(source, source ^ 1) for source in range(count)])


def gathered(value, axis, groups=None):
    return lax.all_to_all(value, axis, 0, 0, axis_index_groups=groups, tiled=True)


def per_device(query, keys, values, dirs, rates, gain, doc_lengths, cotangent):
    size, width = query.shape
    heads = width // DH
    features = width * lax.axis_size("head")
    gain_row = gain.reshape(1, width)
    ctx = lax.axis_index("ctx").astype(jnp.int32)
    place = jnp.stack([ctx * size, ctx & 1])
    unit_flops = 2 * size * size * DH
    packed = pack(keys, dirs, values, rates)
    halo2 = passed_along(packed, 2)
    halo4 = passed_along(packed, 4)
    even = paired(packed, 0, 1)
    even, own_keys = lax.optimization_barrier((even, keys))
    inverse, coef, raw = call(
        own_kernel,
        [((heads, size, size), BF16), ((heads, size, 2 * DH), BF16), ((heads, size, 2 * DH), F32)],
        heads * 60 * unit_flops,
        query,
        own_keys,
        dirs,
        rates,
    )
    halo2, raw = lax.optimization_barrier((halo2, raw))
    cross2 = swapped(halo2)
    cross2, halo4 = lax.optimization_barrier((cross2, halo4))
    halos = (halo2, halo4, even, cross2, paired(halo4, 1, -1))
    att, total, prob, frame, carry, sums, far = call(
        functools.partial(attend_kernel, heads),
        [
            ((size, width), F32),
            ((heads, size, 8), F32),
            ((heads, WIN + 1, size, size), BF16),
            ((heads, WIN, size, DH), BF16),
            ((heads, WIN, DH, 2 * DH), BF16),
            ((lax.axis_size("head"), 1, 2 * size), F32),
            ((WIN, size, width), BF16),
        ],
        heads * 300 * unit_flops,
        raw,
        values,
        cotangent,
        gain_row,
        *halos,
        scalars=(doc_lengths, place),
        scratch=[pltpu.VMEM((size + 16, 3 * width), BF16)] * 2,
    )
    sums = gathered(sums, "head")
    count = lax.axis_size("ctx")
    normed, parts, scaled, delta, carried, send3, send4 = call(
        functools.partial(far_back_kernel, heads, features),
        [
            ((size, width), BF16),
            ((count, 1, width), F32),
            ((size, width), BF16),
            ((heads, size, 8), F32),
            ((heads, size, DH), BF16),
            ((size, 3 * width), BF16),
            ((size, 2 * width), BF16),
        ],
        heads * 15 * unit_flops,
        sums,
        att,
        total,
        prob,
        frame,
        carry,
        cotangent,
        gain_row,
        far,
    )
    recv4 = passed_along(send4, -4)
    recv3 = passed_along(send3, -3)
    parts = gathered(parts, "ctx")
    scaled, recv3, recv4 = lax.optimization_barrier((scaled, recv3, recv4))
    own, dval, send1, send2 = call(
        functools.partial(near_back_kernel, heads),
        [
            ((heads, size, 2 * DH), BF16),
            ((size, width), F32),
            ((size, 3 * width), BF16),
            ((size, 3 * width), BF16),
        ],
        heads * 3000 * unit_flops,
        scaled,
        delta,
        carried,
        prob,
        frame,
        carry,
        values,
        far,
    )
    own, parts = lax.optimization_barrier((own, parts))
    recvs = (passed_along(send1, -1), passed_along(send2, -2), recv3, recv4)
    dquery, dkey_part, ddir_part, pulled = call(
        functools.partial(local_kernel, heads),
        [
            ((size, width), BF16),
            ((heads, size, DH), F32),
            ((heads, size, DH), F32),
            ((heads, size, 2 * DH), F32),
        ],
        heads * 150 * unit_flops,
        own,
        coef,
        query,
        keys,
        dirs,
    )
    dkey, dvalue, ddir, drate, dgain = call(
        functools.partial(shard_kernel, heads),
        [((size, width), BF16), ((size, width), BF16), ((size, width), BF16), ((heads, size), F32), ((1, width), F32)],
        heads * 20 * unit_flops,
        *recvs,
        inverse,
        coef,
        pulled,
        dkey_part,
        ddir_part,
        dval,
        keys,
        dirs,
        rates,
        parts,
    )
    return normed, dquery, dkey, dvalue, ddir, drate, dgain.reshape(width)


def solution(mesh):
    rows = P("ctx", "head")
    return jax.shard_map(
        per_device,
        mesh=mesh,
        in_specs=(rows, rows, rows, rows, P("head", "ctx"), P("head"), P(), rows),
        out_specs=(rows, rows, rows, rows, rows, P("head", "ctx"), P("head")),
        check_vma=False,
    )
```

```python
import functools

import jax
import jax.numpy as jnp
from jax import lax
from jax.experimental import pallas as pl
from jax.experimental.pallas import tpu as pltpu
from jax.sharding import PartitionSpec as P

DH = 128
WIN = 4
NEG_FILL = -1e30
EPSILON = 1e-06
F32 = jnp.float32
BF16 = jnp.bfloat16
VMEM_LIMIT = 48 * 1024 * 1024


def mm(left, right, form="nn"):
    lhs = 0 if form[0] == "t" else 1
    rhs = 1 if form[1] == "t" else 0
    return lax.dot_general(
        left.astype(BF16), right.astype(BF16), (((lhs,), (rhs,)), ((), ())), preferred_element_type=F32
    )


def split(value):
    high = value.astype(BF16)
    low = (value - high.astype(F32)).astype(BF16)
    return high, low


def mm3(left, right):
    lh, ll = split(left)
    rh, rl = split(right)
    return mm(jnp.concatenate([lh, lh, ll], axis=1), jnp.concatenate([rh, rl, rh], axis=0))


def grids(size):
    rows = lax.broadcasted_iota(jnp.int32, (size, size), 0)
    cols = lax.broadcasted_iota(jnp.int32, (size, size), 1)
    return rows, cols


def to_col(row, eye):
    return jnp.sum(jnp.where(eye, row, 0.0), axis=1, keepdims=True)


def to_row(col, eye):
    return jnp.sum(jnp.where(eye, col, 0.0), axis=0, keepdims=True)


def unit_lower_inverses(strict_list):
    size = strict_list[0].shape[0]
    rows, cols = grids(size)
    eye = jnp.where(rows == cols, 1.0, 0.0)
    pair = (rows // 2 == cols // 2) & (rows > cols)
    inverses = [eye - jnp.where(pair, strict, 0.0) for strict in strict_list]
    width = 2
    while width < size:
        wide = min(4 * width, size)
        between = (rows // wide == cols // wide) & (rows // width > cols // width)
        parts = [jnp.where(between, strict, 0.0) for strict in strict_list]
        steps = [mm3(inverse, part) for inverse, part in zip(inverses, parts)]
        once = [inverse - mm3(step, inverse) for step, inverse in zip(steps, inverses)]
        if wide > 2 * width:
            twice = [mm3(step, step) for step in steps]
            inverses = [first + mm3(second, first) for first, second in zip(once, twice)]
        else:
            inverses = once
        width = wide
    return inverses


def shard_scales(dirs, rate_row, eye):
    gram = mm(dirs, dirs, "nt")
    square = jnp.where(eye, gram, 0.0)
    norm_row = lax.rsqrt(jnp.sum(square, axis=0, keepdims=True) + EPSILON)
    norm_col = lax.rsqrt(jnp.sum(square, axis=1, keepdims=True) + EPSILON)
    rate_col = to_col(rate_row, eye)
    return gram, norm_row, norm_col, rate_col


def prepare(shards):
    size = shards[0][0].shape[0]
    rows, cols = grids(size)
    eye = rows == cols
    strict = rows > cols
    grams, rights, norms = [], [], []
    for dirs, keys, rate_row in shards:
        gram, norm_row, norm_col, rate_col = shard_scales(dirs, rate_row, eye)
        scale = rate_col * norm_col
        grams.append(jnp.where(strict, gram * norm_row * scale, 0.0))
        rights.append(
            jnp.concatenate(
                [jnp.where(strict, mm(dirs, keys, "nt") * scale, 0.0), dirs.astype(F32) * scale], axis=1
            )
        )
        norms.append((norm_row, norm_col))
    inverses = unit_lower_inverses(grams)
    return [
        (inverse, mm3(inverse, right), norm) for inverse, right, norm in zip(inverses, rights, norms)
    ]


def rate_pieces(row, height, width):
    first = row.astype(BF16).astype(F32)
    rest = row - first
    second = rest.astype(BF16).astype(F32)
    third = rest - second
    at = lax.broadcasted_iota(jnp.int32, (height, width), 0)
    return jnp.where(at == 0, first, jnp.where(at == 1, second, jnp.where(at == 2, third, 0.0))).astype(BF16)


def pack_kernel(key_ref, dir_ref, value_ref, rate_ref, out_ref, rate_in, sems):
    size, width = key_ref.shape
    heads = rate_ref.shape[0]
    bring = pltpu.make_async_copy(rate_ref, rate_in, sems.at[3])
    bring.start()
    copies = [
        pltpu.make_async_copy(
            ref, out_ref.at[pl.ds(0, size), pl.ds(at * width, width)], sems.at[at]
        )
        for at, ref in enumerate((key_ref, dir_ref, value_ref))
    ]
    for copy in copies:
        copy.start()
    bring.wait()
    rate = jnp.concatenate([rate_in[h : h + 1, :] for h in range(heads)], axis=1)
    out_ref[size : size + 16, 0:width] = rate_pieces(rate, 16, width)
    out_ref[size : size + 16, width : 3 * width] = jnp.zeros((16, 2 * width), BF16)
    for copy in copies:
        copy.wait()


def pack(keys, dirs, values, rates):
    size, width = keys.shape
    return pl.pallas_call(
        pack_kernel,
        out_shape=jax.ShapeDtypeStruct((size + 16, 3 * width), BF16),
        in_specs=[pl.BlockSpec(memory_space=pl.ANY)] * 4,
        out_specs=pl.BlockSpec(memory_space=pltpu.VMEM),
        scratch_shapes=[pltpu.VMEM(rates.shape, F32), pltpu.SemaphoreType.DMA((4,))],
    )(keys, dirs, values, rates)


def own_kernel(query_ref, key_ref, dir_ref, rate_ref, inv_ref, kw_ref, raw_ref):
    size = query_ref.shape[0]
    heads = rate_ref.shape[0]
    rows, cols = grids(size)
    shards = []
    for h in range(heads):
        lanes = slice(h * DH, (h + 1) * DH)
        shards.append((dir_ref[:, lanes], key_ref[:, lanes], rate_ref[h : h + 1, :]))
    prepared = prepare(shards)
    for h in range(heads):
        lanes = slice(h * DH, (h + 1) * DH)
        inverse, coef, (norm_row, _) = prepared[h]
        query = query_ref[:, lanes]
        dirs, keys, _ = shards[h]
        applied = jnp.where(rows >= cols, mm(query, dirs, "nt") * norm_row, 0.0)
        base = jnp.concatenate([mm(query, keys, "nt"), query.astype(F32)], axis=1)
        raw_ref[h] = base - mm3(applied, coef)
        inv_ref[h] = inverse.astype(BF16)
        kw_ref[h] = coef.astype(BF16)


def attend_kernel(
    heads,
    raw_ref,
    value_ref,
    cot_ref,
    gain_ref,
    halo2_ref,
    halo4_ref,
    even_ref,
    cross2_ref,
    cross4_ref,
    len_ref,
    place_ref,
    att_ref,
    tot_ref,
    prob_ref,
    frame_ref,
    kt_ref,
    sums_ref,
    far_ref,
    halo1_ref,
    halo3_ref,
):
    size = value_ref.shape[0]
    width = heads * DH

    @pl.when(place_ref[1] == 0)
    def _():
        halo1_ref[...] = cross2_ref[...]
        halo3_ref[...] = cross4_ref[...]

    @pl.when(place_ref[1] != 0)
    def _():
        halo1_ref[...] = even_ref[...]
        halo3_ref[...] = cross2_ref[...]

    halos = (halo1_ref, halo2_ref, halo3_ref, halo4_ref)
    for s in range(WIN):
        far_ref[s] = halos[s][0:size, 2 * width : 3 * width]
    rows, cols = grids(size)
    eye = rows == cols
    eye_f = jnp.where(eye, 1.0, 0.0)
    first = place_ref[0]
    pos_row = first + lax.broadcasted_iota(jnp.int32, (1, size), 1)
    start_row = jnp.zeros((1, size), jnp.int32)
    end = jnp.int32(0)
    for d in range(len_ref.shape[0]):
        end = end + len_ref[d]
        start_row = jnp.where(end <= pos_row, end, start_row)
    start = to_col(start_row.astype(F32), eye).astype(jnp.int32)
    seen = [(rows >= cols) & (first + cols >= start)]
    for s in range(1, WIN + 1):
        seen.append(first - s * size + cols >= start)
    shards = []
    for s in range(WIN):
        for h in range(heads):
            keys = halos[s][0:size, h * DH : (h + 1) * DH]
            dirs = halos[s][0:size, width + h * DH : width + (h + 1) * DH]
            rate = halos[s][size : size + 16, h * DH : (h + 1) * DH].astype(F32)
            shards.append((dirs, keys, jnp.sum(rate, axis=0, keepdims=True)))
    prepared = prepare(shards)
    carry = []
    for (dirs, keys, _), (_, coef, (_, norm_col)) in zip(shards, prepared):
        base = jnp.concatenate([keys.astype(F32).T, eye_f], axis=1)
        high, low = split(coef * norm_col)
        turned = dirs.astype(F32).T.astype(BF16)
        carry.append(base - (mm(turned, high) + mm(turned, low)))
    square = jnp.zeros((size, 1), F32)
    inner = jnp.zeros((size, 1), F32)
    for h in range(heads):
        lanes = slice(h * DH, (h + 1) * DH)
        scores = [raw_ref[h, :, 0:DH]]
        frame = raw_ref[h, :, DH : 2 * DH]
        for s in range(WIN):
            matrix = carry[s * heads + h]
            kt_ref[h, s] = matrix.astype(BF16)
            frame_ref[h, s] = frame.astype(BF16)
            if s < WIN - 1:
                product = mm3(frame, matrix)
                scores.append(product[:, 0:DH])
                frame = product[:, DH : 2 * DH]
            else:
                scores.append(mm3(frame, matrix[:, 0:DH]))
        scaled = [
            jnp.where(seen[s], scores[s] * (DH ** (-0.5)), NEG_FILL) for s in range(WIN + 1)
        ]
        top = scaled[0]
        for s in range(1, WIN + 1):
            top = jnp.maximum(top, scaled[s])
        top = jnp.max(top, axis=1, keepdims=True)
        weights = [jnp.where(seen[s], jnp.exp(scaled[s] - top), 0.0) for s in range(WIN + 1)]
        total = weights[0]
        for s in range(1, WIN + 1):
            total = total + weights[s]
        total = jnp.sum(total, axis=1, keepdims=True)
        numer = None
        for s in range(WIN + 1):
            half = weights[s].astype(BF16)
            prob_ref[h, s] = half
            if s == 0:
                value = value_ref[:, lanes]
            else:
                value = halos[s - 1][0:size, 2 * width + h * DH : 2 * width + (h + 1) * DH]
            term = mm(half, value)
            numer = term if numer is None else numer + term
        att = numer / total
        att_ref[:, lanes] = att
        tot_ref[h] = jnp.broadcast_to(total, (size, 8))
        weighted = cot_ref[:, lanes].astype(F32) * gain_ref[:, lanes]
        square = square + jnp.sum(att * att, axis=1, keepdims=True)
        inner = inner + jnp.sum(weighted * att, axis=1, keepdims=True)
    row = jnp.concatenate([to_row(square, eye), to_row(inner, eye)], axis=1)
    sums_ref[...] = jnp.broadcast_to(row[None], sums_ref.shape)


def back_block(h, s, scaled, delta, prob, value, frame, matrix, carried, send):
    width = scaled.shape[1]
    lanes = slice(h * DH, (h + 1) * DH)
    through = mm(scaled[:, lanes], value, "nt")
    dscore = (prob.astype(F32) * ((through - delta) * (DH ** (-0.5)))).astype(BF16)
    send[:, lanes] = mm(prob, scaled[:, lanes], "tn").astype(send.dtype)
    if frame is None:
        return jnp.concatenate([dscore, carried], axis=1)
    at_end = slice(width + h * DH, width + (h + 1) * DH)
    at_trans = slice(2 * width + h * DH, 2 * width + (h + 1) * DH)
    if carried is None:
        send[:, at_end] = mm(frame, dscore, "tn").astype(BF16)
        return mm(dscore, matrix[:, 0:DH], "nt").astype(BF16)
    both = jnp.concatenate([dscore, carried], axis=1)
    grads = mm(frame, both, "tn").astype(BF16)
    send[:, at_end] = grads[:, 0:DH]
    send[:, at_trans] = grads[:, DH : 2 * DH]
    return mm(both, matrix, "nt").astype(BF16)


def far_back_kernel(
    heads,
    features,
    sums_ref,
    att_ref,
    tot_ref,
    prob_ref,
    frame_ref,
    kt_ref,
    cot_ref,
    gain_ref,
    far_ref,
    normed_ref,
    parts_ref,
    scaled_ref,
    delta_ref,
    carried_ref,
    send3_ref,
    send4_ref,
):
    size = att_ref.shape[0]
    rows, cols = grids(size)
    eye = rows == cols
    sums = jnp.sum(sums_ref[...], axis=0)
    square = to_col(sums[:, 0:size], eye)
    inner = to_col(sums[:, size : 2 * size], eye)
    inverse = lax.rsqrt(square / features + EPSILON)
    pull = inverse * inverse * inverse * inner / features
    att_all = att_ref[...]
    cot_all = cot_ref[...].astype(F32)
    gain = gain_ref[...]
    normed = att_all * inverse
    normed_ref[...] = (normed * gain).astype(BF16)
    part = jnp.sum(cot_all * normed, axis=0, keepdims=True)
    parts_ref[...] = jnp.broadcast_to(part[None], parts_ref.shape)
    grad_att = cot_all * gain * inverse - att_all * pull
    for h in range(heads):
        lanes = slice(h * DH, (h + 1) * DH)
        total = tot_ref[h, :, 0:1]
        grad = grad_att[:, lanes]
        scaled_ref[:, lanes] = (grad / total).astype(BF16)
        delta = jnp.sum(grad * att_all[:, lanes], axis=1, keepdims=True) / total
        delta_ref[h] = jnp.broadcast_to(delta, (size, 8))
        carried = None
        for s, send in ((4, send4_ref), (3, send3_ref)):
            carried = back_block(
                h, s, scaled_ref, delta, prob_ref[h, s], far_ref[s - 1, :, lanes], frame_ref[h, s - 1], kt_ref[h, s - 1], carried, send
            )
        carried_ref[h] = carried


def near_back_kernel(
    heads,
    scaled_ref,
    delta_ref,
    carried_ref,
    prob_ref,
    frame_ref,
    kt_ref,
    value_ref,
    far_ref,
    own_ref,
    dval_ref,
    send1_ref,
    send2_ref,
):
    for h in range(heads):
        lanes = slice(h * DH, (h + 1) * DH)
        delta = delta_ref[h, :, 0:1]
        carried = carried_ref[h]
        for s, send in ((2, send2_ref), (1, send1_ref)):
            carried = back_block(
                h, s, scaled_ref, delta, prob_ref[h, s], far_ref[s - 1, :, lanes], frame_ref[h, s - 1], kt_ref[h, s - 1], carried, send
            )
        own_ref[h] = back_block(
            h, 0, scaled_ref, delta, prob_ref[h, 0], value_ref[:, lanes], None, None, carried, dval_ref
        )


def local_kernel(heads, own_ref, kw_ref, query_ref, key_ref, dir_ref, dquery_ref, dkey_ref, ddir_ref, pulled_ref):
    size = query_ref.shape[0]
    rows, cols = grids(size)
    eye = rows == cols
    lower = rows >= cols
    for h in range(heads):
        lanes = slice(h * DH, (h + 1) * DH)
        query = query_ref[:, lanes]
        keys = key_ref[:, lanes]
        raw_dirs = dir_ref[:, lanes].astype(F32)
        norm_col = lax.rsqrt(jnp.sum(raw_dirs * raw_dirs, axis=1, keepdims=True) + EPSILON)
        unit = (raw_dirs * norm_col).astype(BF16)
        grads = own_ref[h]
        applied = jnp.where(lower, mm(query, unit, "nt"), 0.0).astype(BF16)
        dapplied = jnp.where(lower, mm(grads, kw_ref[h], "nt"), 0.0).astype(BF16)
        dquery = mm(grads[:, 0:DH], keys) + grads[:, DH : 2 * DH].astype(F32) - mm(dapplied, unit)
        dquery_ref[:, lanes] = dquery.astype(BF16)
        dkey_ref[h] = mm(grads[:, 0:DH], query, "tn")
        ddir_ref[h] = -mm(dapplied, query, "tn")
        pulled_ref[h] = mm(applied, grads, "tn")


def shard_kernel(
    heads,
    recv1_ref,
    recv2_ref,
    recv3_ref,
    recv4_ref,
    inv_ref,
    kw_ref,
    pulled_ref,
    dkey_in_ref,
    ddir_in_ref,
    dval_in_ref,
    key_ref,
    dir_ref,
    rate_ref,
    parts_ref,
    dkey_ref,
    dvalue_ref,
    ddir_ref,
    drate_ref,
    dgain_ref,
):
    size = key_ref.shape[0]
    width = heads * DH
    recvs = (recv1_ref, recv2_ref, recv3_ref, recv4_ref)
    rows, cols = grids(size)
    eye = rows == cols
    strict = rows > cols
    dvalue = dval_in_ref[...]
    for recv in recvs:
        dvalue = dvalue + recv[:, 0:width].astype(F32)
    dvalue_ref[...] = dvalue.astype(BF16)
    dgain_ref[...] = jnp.sum(parts_ref[...], axis=0)
    for h in range(heads):
        lanes = slice(h * DH, (h + 1) * DH)
        keys = key_ref[:, lanes]
        raw_dirs = dir_ref[:, lanes].astype(F32)
        norm_col = lax.rsqrt(jnp.sum(raw_dirs * raw_dirs, axis=1, keepdims=True) + EPSILON)
        unit = raw_dirs * norm_col
        unit_half = unit.astype(BF16)
        rate_col = to_col(rate_ref[h : h + 1, :], eye)
        dend = jnp.zeros((size, DH), F32)
        dtrans = jnp.zeros((size, DH), F32)
        for recv in recvs:
            dend = dend + recv[:, width + h * DH : width + (h + 1) * DH].astype(F32)
            if recv.shape[1] == 3 * width:
                dtrans = dtrans + recv[:, 2 * width + h * DH : 2 * width + (h + 1) * DH].astype(F32)
        both = jnp.concatenate([dend, dtrans], axis=1).astype(BF16)
        coef = kw_ref[h]
        dcoef = -(pulled_ref[h] + mm(unit_half, both))
        solved = mm(inv_ref[h], dcoef, "tn")
        dstrict = jnp.where(strict, -mm(solved, coef, "nt"), 0.0)
        dinner = jnp.where(strict, solved[:, 0:DH], 0.0).astype(BF16)
        local = mm(dstrict, unit_half) + mm(dinner, keys) + solved[:, DH : 2 * DH]
        dunit = (
            rate_col * local
            + mm(rate_col * dstrict, unit_half, "tn")
            + ddir_in_ref[h]
            - mm(coef, both, "nt")
        )
        drate_ref[h : h + 1, :] = to_row(jnp.sum(local * unit, axis=1, keepdims=True), eye)
        dkey_ref[:, lanes] = (
            dkey_in_ref[h] + mm(dinner, rate_col * unit, "tn") + dend.T
        ).astype(BF16)
        along = jnp.sum(unit * dunit, axis=1, keepdims=True)
        ddir_ref[:, lanes] = (norm_col * (dunit - unit * along)).astype(BF16)


def call(body, outs, flops, *operands, scalars=(), scratch=()):
    vmem = pl.BlockSpec(memory_space=pltpu.VMEM)
    smem = pl.BlockSpec(memory_space=pltpu.SMEM)
    moved = sum(x.size * x.dtype.itemsize for x in operands) + sum(
        jnp.dtype(d).itemsize * functools.reduce(lambda a, b: a * b, s) for s, d in outs
    )
    return pl.pallas_call(
        body,
        out_shape=[jax.ShapeDtypeStruct(s, d) for s, d in outs],
        in_specs=[vmem] * len(operands) + [smem] * len(scalars),
        out_specs=[vmem] * len(outs),
        scratch_shapes=list(scratch),
        compiler_params=pltpu.CompilerParams(vmem_limit_bytes=VMEM_LIMIT),
        cost_estimate=pl.CostEstimate(flops=flops, bytes_accessed=moved if flops else 0, transcendentals=0),
    )(*operands, *scalars)


def passed_along(value, steps):
    count = lax.axis_size("ctx")
    first, last = (max(0, -steps), min(count, count - steps))
    return lax.ppermute(value, "ctx", [(source, source + steps) for source in range(first, last)])


def paired(value, first, step):
    count = lax.axis_size("ctx")
    return lax.ppermute(value, "ctx", [(source, source + step) for source in range(first, count, 2)])


def swapped(value):
    count = lax.axis_size("ctx")
    return lax.ppermute(value, "ctx", [(source, source ^ 1) for source in range(count)])


def gathered(value, axis, groups=None):
    return lax.all_to_all(value, axis, 0, 0, axis_index_groups=groups, tiled=True)


def per_device(query, keys, values, dirs, rates, gain, doc_lengths, cotangent):
    size, width = query.shape
    heads = width // DH
    features = width * lax.axis_size("head")
    gain_row = gain.reshape(1, width)
    ctx = lax.axis_index("ctx").astype(jnp.int32)
    place = jnp.stack([ctx * size, ctx & 1])
    unit_flops = 2 * size * size * DH
    packed = pack(keys, dirs, values, rates)
    halo2 = passed_along(packed, 2)
    even = paired(packed, 0, 1)
    inverse, coef, raw = call(
        own_kernel,
        [((heads, size, size), BF16), ((heads, size, 2 * DH), BF16), ((heads, size, 2 * DH), F32)],
        heads * 60 * unit_flops,
        query,
        keys,
        dirs,
        rates,
    )
    halo2, raw = lax.optimization_barrier((halo2, raw))
    halo4 = passed_along(halo2, 2)
    cross2 = swapped(halo2)
    cross2, halo4 = lax.optimization_barrier((cross2, halo4))
    halos = (halo2, halo4, even, cross2, paired(halo4, 1, -1))
    att, total, prob, frame, carry, sums, far = call(
        functools.partial(attend_kernel, heads),
        [
            ((size, width), F32),
            ((heads, size, 8), F32),
            ((heads, WIN + 1, size, size), BF16),
            ((heads, WIN, size, DH), BF16),
            ((heads, WIN, DH, 2 * DH), BF16),
            ((lax.axis_size("head"), 1, 2 * size), F32),
            ((WIN, size, width), BF16),
        ],
        heads * 300 * unit_flops,
        raw,
        values,
        cotangent,
        gain_row,
        *halos,
        scalars=(doc_lengths, place),
        scratch=[pltpu.VMEM((size + 16, 3 * width), BF16)] * 2,
    )
    sums = gathered(sums, "head")
    count = lax.axis_size("ctx")
    normed, parts, scaled, delta, carried, send3, send4 = call(
        functools.partial(far_back_kernel, heads, features),
        [
            ((size, width), BF16),
            ((count, 1, width), F32),
            ((size, width), BF16),
            ((heads, size, 8), F32),
            ((heads, size, DH), BF16),
            ((size, 3 * width), BF16),
            ((size, 2 * width), BF16),
        ],
        heads * 15 * unit_flops,
        sums,
        att,
        total,
        prob,
        frame,
        carry,
        cotangent,
        gain_row,
        far,
    )
    recv4 = passed_along(send4, -4)
    recv3 = passed_along(send3, -3)
    parts = gathered(parts, "ctx")
    scaled, recv3, recv4 = lax.optimization_barrier((scaled, recv3, recv4))
    own, dval, send1, send2 = call(
        functools.partial(near_back_kernel, heads),
        [
            ((heads, size, 2 * DH), BF16),
            ((size, width), F32),
            ((size, 3 * width), BF16),
            ((size, 3 * width), BF16),
        ],
        heads * 3000 * unit_flops,
        scaled,
        delta,
        carried,
        prob,
        frame,
        carry,
        values,
        far,
    )
    own, parts = lax.optimization_barrier((own, parts))
    recvs = (passed_along(send1, -1), passed_along(send2, -2), recv3, recv4)
    dquery, dkey_part, ddir_part, pulled = call(
        functools.partial(local_kernel, heads),
        [
            ((size, width), BF16),
            ((heads, size, DH), F32),
            ((heads, size, DH), F32),
            ((heads, size, 2 * DH), F32),
        ],
        heads * 150 * unit_flops,
        own,
        coef,
        query,
        keys,
        dirs,
    )
    dkey, dvalue, ddir, drate, dgain = call(
        functools.partial(shard_kernel, heads),
        [((size, width), BF16), ((size, width), BF16), ((size, width), BF16), ((heads, size), F32), ((1, width), F32)],
        heads * 20 * unit_flops,
        *recvs,
        inverse,
        coef,
        pulled,
        dkey_part,
        ddir_part,
        dval,
        keys,
        dirs,
        rates,
        parts,
    )
    return normed, dquery, dkey, dvalue, ddir, drate, dgain.reshape(width)


def solution(mesh):
    rows = P("ctx", "head")
    return jax.shard_map(
        per_device,
        mesh=mesh,
        in_specs=(rows, rows, rows, rows, P("head", "ctx"), P("head"), P(), rows),
        out_specs=(rows, rows, rows, rows, rows, P("head", "ctx"), P("head")),
        check_vma=False,
    )
```

```python
import functools

import jax
import jax.numpy as jnp
from jax import lax
from jax.experimental import pallas as pl
from jax.experimental.pallas import tpu as pltpu
from jax.sharding import PartitionSpec as P

DH = 128
WIN = 4
NEG_FILL = -1e30
EPSILON = 1e-06
F32 = jnp.float32
BF16 = jnp.bfloat16
VMEM_LIMIT = 48 * 1024 * 1024


def mm(left, right, form="nn"):
    lhs = 0 if form[0] == "t" else 1
    rhs = 1 if form[1] == "t" else 0
    return lax.dot_general(
        left.astype(BF16), right.astype(BF16), (((lhs,), (rhs,)), ((), ())), preferred_element_type=F32
    )


def split(value):
    high = value.astype(BF16)
    low = (value - high.astype(F32)).astype(BF16)
    return high, low


def mm3(left, right):
    lh, ll = split(left)
    rh, rl = split(right)
    return mm(jnp.concatenate([lh, lh, ll], axis=1), jnp.concatenate([rh, rl, rh], axis=0))


def grids(size):
    rows = lax.broadcasted_iota(jnp.int32, (size, size), 0)
    cols = lax.broadcasted_iota(jnp.int32, (size, size), 1)
    return rows, cols


def to_col(row, eye):
    return jnp.sum(jnp.where(eye, row, 0.0), axis=1, keepdims=True)


def to_row(col, eye):
    return jnp.sum(jnp.where(eye, col, 0.0), axis=0, keepdims=True)


def unit_lower_inverses(strict_list):
    size = strict_list[0].shape[0]
    rows, cols = grids(size)
    eye = jnp.where(rows == cols, 1.0, 0.0)
    pair = (rows // 2 == cols // 2) & (rows > cols)
    inverses = [eye - jnp.where(pair, strict, 0.0) for strict in strict_list]
    width = 2
    while width < size:
        wide = min(4 * width, size)
        between = (rows // wide == cols // wide) & (rows // width > cols // width)
        parts = [jnp.where(between, strict, 0.0) for strict in strict_list]
        steps = [mm3(inverse, part) for inverse, part in zip(inverses, parts)]
        once = [inverse - mm3(step, inverse) for step, inverse in zip(steps, inverses)]
        if wide > 2 * width:
            twice = [mm3(step, step) for step in steps]
            inverses = [first + mm3(second, first) for first, second in zip(once, twice)]
        else:
            inverses = once
        width = wide
    return inverses


def shard_scales(dirs, rate_row, eye):
    gram = mm(dirs, dirs, "nt")
    square = jnp.where(eye, gram, 0.0)
    norm_row = lax.rsqrt(jnp.sum(square, axis=0, keepdims=True) + EPSILON)
    norm_col = lax.rsqrt(jnp.sum(square, axis=1, keepdims=True) + EPSILON)
    rate_col = to_col(rate_row, eye)
    return gram, norm_row, norm_col, rate_col


def prepare(shards):
    size = shards[0][0].shape[0]
    rows, cols = grids(size)
    eye = rows == cols
    strict = rows > cols
    grams, rights, norms = [], [], []
    for dirs, keys, rate_row in shards:
        gram, norm_row, norm_col, rate_col = shard_scales(dirs, rate_row, eye)
        scale = rate_col * norm_col
        grams.append(jnp.where(strict, gram * norm_row * scale, 0.0))
        rights.append(
            jnp.concatenate(
                [jnp.where(strict, mm(dirs, keys, "nt") * scale, 0.0), dirs.astype(F32) * scale], axis=1
            )
        )
        norms.append((norm_row, norm_col))
    inverses = unit_lower_inverses(grams)
    return [
        (inverse, mm3(inverse, right), norm) for inverse, right, norm in zip(inverses, rights, norms)
    ]


def rate_pieces(row, height, width):
    first = row.astype(BF16).astype(F32)
    rest = row - first
    second = rest.astype(BF16).astype(F32)
    third = rest - second
    at = lax.broadcasted_iota(jnp.int32, (height, width), 0)
    return jnp.where(at == 0, first, jnp.where(at == 1, second, jnp.where(at == 2, third, 0.0))).astype(BF16)


def pack_kernel(key_ref, dir_ref, value_ref, rate_ref, out_ref, rate_in, sems):
    size, width = key_ref.shape
    heads = rate_ref.shape[0]
    bring = pltpu.make_async_copy(rate_ref, rate_in, sems.at[3])
    bring.start()
    copies = [
        pltpu.make_async_copy(
            ref, out_ref.at[pl.ds(0, size), pl.ds(at * width, width)], sems.at[at]
        )
        for at, ref in enumerate((key_ref, dir_ref, value_ref))
    ]
    for copy in copies:
        copy.start()
    bring.wait()
    rate = jnp.concatenate([rate_in[h : h + 1, :] for h in range(heads)], axis=1)
    out_ref[size : size + 16, 0:width] = rate_pieces(rate, 16, width)
    out_ref[size : size + 16, width : 3 * width] = jnp.zeros((16, 2 * width), BF16)
    for copy in copies:
        copy.wait()


def pack(keys, dirs, values, rates):
    size, width = keys.shape
    return pl.pallas_call(
        pack_kernel,
        out_shape=jax.ShapeDtypeStruct((size + 16, 3 * width), BF16),
        in_specs=[pl.BlockSpec(memory_space=pl.ANY)] * 4,
        out_specs=pl.BlockSpec(memory_space=pltpu.VMEM),
        scratch_shapes=[pltpu.VMEM(rates.shape, F32), pltpu.SemaphoreType.DMA((4,))],
    )(keys, dirs, values, rates)


def own_kernel(query_ref, key_ref, dir_ref, rate_ref, inv_ref, kw_ref, raw_ref):
    size = query_ref.shape[0]
    heads = rate_ref.shape[0]
    rows, cols = grids(size)
    shards = []
    for h in range(heads):
        lanes = slice(h * DH, (h + 1) * DH)
        shards.append((dir_ref[:, lanes], key_ref[:, lanes], rate_ref[h : h + 1, :]))
    prepared = prepare(shards)
    for h in range(heads):
        lanes = slice(h * DH, (h + 1) * DH)
        inverse, coef, (norm_row, _) = prepared[h]
        query = query_ref[:, lanes]
        dirs, keys, _ = shards[h]
        applied = jnp.where(rows >= cols, mm(query, dirs, "nt") * norm_row, 0.0)
        base = jnp.concatenate([mm(query, keys, "nt"), query.astype(F32)], axis=1)
        raw_ref[h] = base - mm3(applied, coef)
        inv_ref[h] = inverse.astype(BF16)
        kw_ref[h] = coef.astype(BF16)


def carries(blocks, heads):
    shards = []
    for block in blocks:
        size, width = block.shape[0] - 16, heads * DH
        for h in range(heads):
            lanes = slice(h * DH, (h + 1) * DH)
            keys = block[0:size, lanes]
            dirs = block[0:size, width + h * DH : width + (h + 1) * DH]
            rate = block[size : size + 16, lanes].astype(F32)
            shards.append((dirs, keys, jnp.sum(rate, axis=0, keepdims=True)))
    rows, cols = grids(DH)
    eye = jnp.where(rows == cols, 1.0, 0.0)
    matrices = []
    for (dirs, keys, _), (_, coef, (_, norm_col)) in zip(shards, prepare(shards)):
        base = jnp.concatenate([keys.astype(F32).T, eye], axis=1)
        high, low = split(coef * norm_col)
        turned = dirs.astype(F32).T.astype(BF16)
        matrices.append(base - (mm(turned, high) + mm(turned, low)))
    return matrices


def far_prepare_kernel(heads, halo2_ref, halo4_ref, out_ref):
    for at, matrix in enumerate(carries((halo2_ref, halo4_ref), heads)):
        out_ref[at] = matrix


def attend_kernel(
    heads,
    raw_ref,
    value_ref,
    cot_ref,
    gain_ref,
    halo2_ref,
    halo4_ref,
    even_ref,
    cross2_ref,
    cross4_ref,
    far_carry_ref,
    len_ref,
    place_ref,
    att_ref,
    tot_ref,
    prob_ref,
    frame_ref,
    kt_ref,
    sums_ref,
    far_ref,
    halo1_ref,
    halo3_ref,
):
    size = value_ref.shape[0]
    width = heads * DH

    @pl.when(place_ref[1] == 0)
    def _():
        halo1_ref[...] = cross2_ref[...]
        halo3_ref[...] = cross4_ref[...]

    @pl.when(place_ref[1] != 0)
    def _():
        halo1_ref[...] = even_ref[...]
        halo3_ref[...] = cross2_ref[...]

    halos = (halo1_ref, halo2_ref, halo3_ref, halo4_ref)
    for s in range(WIN):
        far_ref[s] = halos[s][0:size, 2 * width : 3 * width]
    rows, cols = grids(size)
    eye = rows == cols
    first = place_ref[0]
    pos_row = first + lax.broadcasted_iota(jnp.int32, (1, size), 1)
    start_row = jnp.zeros((1, size), jnp.int32)
    end = jnp.int32(0)
    for d in range(len_ref.shape[0]):
        end = end + len_ref[d]
        start_row = jnp.where(end <= pos_row, end, start_row)
    start = to_col(start_row.astype(F32), eye).astype(jnp.int32)
    seen = [(rows >= cols) & (first + cols >= start)]
    for s in range(1, WIN + 1):
        seen.append(first - s * size + cols >= start)
    near = carries((halo1_ref, halo3_ref), heads)
    carry = near[0:heads] + [far_carry_ref[h] for h in range(heads)]
    carry = carry + near[heads : 2 * heads] + [far_carry_ref[heads + h] for h in range(heads)]
    square = jnp.zeros((size, 1), F32)
    inner = jnp.zeros((size, 1), F32)
    for h in range(heads):
        lanes = slice(h * DH, (h + 1) * DH)
        scores = [raw_ref[h, :, 0:DH]]
        frame = raw_ref[h, :, DH : 2 * DH]
        for s in range(WIN):
            matrix = carry[s * heads + h]
            kt_ref[h, s] = matrix.astype(BF16)
            frame_ref[h, s] = frame.astype(BF16)
            if s < WIN - 1:
                product = mm3(frame, matrix)
                scores.append(product[:, 0:DH])
                frame = product[:, DH : 2 * DH]
            else:
                scores.append(mm3(frame, matrix[:, 0:DH]))
        scaled = [
            jnp.where(seen[s], scores[s] * (DH ** (-0.5)), NEG_FILL) for s in range(WIN + 1)
        ]
        top = scaled[0]
        for s in range(1, WIN + 1):
            top = jnp.maximum(top, scaled[s])
        top = jnp.max(top, axis=1, keepdims=True)
        weights = [jnp.where(seen[s], jnp.exp(scaled[s] - top), 0.0) for s in range(WIN + 1)]
        total = weights[0]
        for s in range(1, WIN + 1):
            total = total + weights[s]
        total = jnp.sum(total, axis=1, keepdims=True)
        numer = None
        for s in range(WIN + 1):
            half = weights[s].astype(BF16)
            prob_ref[h, s] = half
            if s == 0:
                value = value_ref[:, lanes]
            else:
                value = halos[s - 1][0:size, 2 * width + h * DH : 2 * width + (h + 1) * DH]
            term = mm(half, value)
            numer = term if numer is None else numer + term
        att = numer / total
        att_ref[:, lanes] = att
        tot_ref[h] = jnp.broadcast_to(total, (size, 8))
        weighted = cot_ref[:, lanes].astype(F32) * gain_ref[:, lanes]
        square = square + jnp.sum(att * att, axis=1, keepdims=True)
        inner = inner + jnp.sum(weighted * att, axis=1, keepdims=True)
    row = jnp.concatenate([to_row(square, eye), to_row(inner, eye)], axis=1)
    sums_ref[...] = jnp.broadcast_to(row[None], sums_ref.shape)


def back_block(h, s, scaled, delta, prob, value, frame, matrix, carried, send):
    width = scaled.shape[1]
    lanes = slice(h * DH, (h + 1) * DH)
    through = mm(scaled[:, lanes], value, "nt")
    dscore = (prob.astype(F32) * ((through - delta) * (DH ** (-0.5)))).astype(BF16)
    send[:, lanes] = mm(prob, scaled[:, lanes], "tn").astype(send.dtype)
    if frame is None:
        return jnp.concatenate([dscore, carried], axis=1)
    at_end = slice(width + h * DH, width + (h + 1) * DH)
    at_trans = slice(2 * width + h * DH, 2 * width + (h + 1) * DH)
    if carried is None:
        send[:, at_end] = mm(frame, dscore, "tn").astype(BF16)
        return mm(dscore, matrix[:, 0:DH], "nt").astype(BF16)
    both = jnp.concatenate([dscore, carried], axis=1)
    grads = mm(frame, both, "tn").astype(BF16)
    send[:, at_end] = grads[:, 0:DH]
    send[:, at_trans] = grads[:, DH : 2 * DH]
    return mm(both, matrix, "nt").astype(BF16)


def far_back_kernel(
    heads,
    features,
    sums_ref,
    att_ref,
    tot_ref,
    prob_ref,
    frame_ref,
    kt_ref,
    cot_ref,
    gain_ref,
    far_ref,
    normed_ref,
    parts_ref,
    scaled_ref,
    delta_ref,
    carried_ref,
    send3_ref,
    send4_ref,
):
    size = att_ref.shape[0]
    rows, cols = grids(size)
    eye = rows == cols
    sums = jnp.sum(sums_ref[...], axis=0)
    square = to_col(sums[:, 0:size], eye)
    inner = to_col(sums[:, size : 2 * size], eye)
    inverse = lax.rsqrt(square / features + EPSILON)
    pull = inverse * inverse * inverse * inner / features
    att_all = att_ref[...]
    cot_all = cot_ref[...].astype(F32)
    gain = gain_ref[...]
    normed = att_all * inverse
    normed_ref[...] = (normed * gain).astype(BF16)
    part = jnp.sum(cot_all * normed, axis=0, keepdims=True)
    parts_ref[...] = jnp.broadcast_to(part[None], parts_ref.shape)
    grad_att = cot_all * gain * inverse - att_all * pull
    for h in range(heads):
        lanes = slice(h * DH, (h + 1) * DH)
        total = tot_ref[h, :, 0:1]
        grad = grad_att[:, lanes]
        scaled_ref[:, lanes] = (grad / total).astype(BF16)
        delta = jnp.sum(grad * att_all[:, lanes], axis=1, keepdims=True) / total
        delta_ref[h] = jnp.broadcast_to(delta, (size, 8))
        carried = None
        for s, send in ((4, send4_ref), (3, send3_ref)):
            carried = back_block(
                h, s, scaled_ref, delta, prob_ref[h, s], far_ref[s - 1, :, lanes], frame_ref[h, s - 1], kt_ref[h, s - 1], carried, send
            )
        carried_ref[h] = carried


def near_back_kernel(
    heads,
    scaled_ref,
    delta_ref,
    carried_ref,
    prob_ref,
    frame_ref,
    kt_ref,
    value_ref,
    far_ref,
    own_ref,
    dval_ref,
    send1_ref,
    send2_ref,
):
    for h in range(heads):
        lanes = slice(h * DH, (h + 1) * DH)
        delta = delta_ref[h, :, 0:1]
        carried = carried_ref[h]
        for s, send in ((2, send2_ref), (1, send1_ref)):
            carried = back_block(
                h, s, scaled_ref, delta, prob_ref[h, s], far_ref[s - 1, :, lanes], frame_ref[h, s - 1], kt_ref[h, s - 1], carried, send
            )
        own_ref[h] = back_block(
            h, 0, scaled_ref, delta, prob_ref[h, 0], value_ref[:, lanes], None, None, carried, dval_ref
        )


def local_kernel(heads, own_ref, kw_ref, query_ref, key_ref, dir_ref, dquery_ref, dkey_ref, ddir_ref, pulled_ref):
    size = query_ref.shape[0]
    rows, cols = grids(size)
    eye = rows == cols
    lower = rows >= cols
    for h in range(heads):
        lanes = slice(h * DH, (h + 1) * DH)
        query = query_ref[:, lanes]
        keys = key_ref[:, lanes]
        raw_dirs = dir_ref[:, lanes].astype(F32)
        norm_col = lax.rsqrt(jnp.sum(raw_dirs * raw_dirs, axis=1, keepdims=True) + EPSILON)
        unit = (raw_dirs * norm_col).astype(BF16)
        grads = own_ref[h]
        applied = jnp.where(lower, mm(query, unit, "nt"), 0.0).astype(BF16)
        dapplied = jnp.where(lower, mm(grads, kw_ref[h], "nt"), 0.0).astype(BF16)
        dquery = mm(grads[:, 0:DH], keys) + grads[:, DH : 2 * DH].astype(F32) - mm(dapplied, unit)
        dquery_ref[:, lanes] = dquery.astype(BF16)
        dkey_ref[h] = mm(grads[:, 0:DH], query, "tn")
        ddir_ref[h] = -mm(dapplied, query, "tn")
        pulled_ref[h] = mm(applied, grads, "tn")


def shard_kernel(
    heads,
    recv1_ref,
    recv2_ref,
    recv3_ref,
    recv4_ref,
    inv_ref,
    kw_ref,
    pulled_ref,
    dkey_in_ref,
    ddir_in_ref,
    dval_in_ref,
    key_ref,
    dir_ref,
    rate_ref,
    parts_ref,
    dkey_ref,
    dvalue_ref,
    ddir_ref,
    drate_ref,
    dgain_ref,
):
    size = key_ref.shape[0]
    width = heads * DH
    recvs = (recv1_ref, recv2_ref, recv3_ref, recv4_ref)
    rows, cols = grids(size)
    eye = rows == cols
    strict = rows > cols
    dvalue = dval_in_ref[...]
    for recv in recvs:
        dvalue = dvalue + recv[:, 0:width].astype(F32)
    dvalue_ref[...] = dvalue.astype(BF16)
    dgain_ref[...] = jnp.sum(parts_ref[...], axis=0)
    for h in range(heads):
        lanes = slice(h * DH, (h + 1) * DH)
        keys = key_ref[:, lanes]
        raw_dirs = dir_ref[:, lanes].astype(F32)
        norm_col = lax.rsqrt(jnp.sum(raw_dirs * raw_dirs, axis=1, keepdims=True) + EPSILON)
        unit = raw_dirs * norm_col
        unit_half = unit.astype(BF16)
        rate_col = to_col(rate_ref[h : h + 1, :], eye)
        dend = jnp.zeros((size, DH), F32)
        dtrans = jnp.zeros((size, DH), F32)
        for recv in recvs:
            dend = dend + recv[:, width + h * DH : width + (h + 1) * DH].astype(F32)
            if recv.shape[1] == 3 * width:
                dtrans = dtrans + recv[:, 2 * width + h * DH : 2 * width + (h + 1) * DH].astype(F32)
        both = jnp.concatenate([dend, dtrans], axis=1).astype(BF16)
        coef = kw_ref[h]
        dcoef = -(pulled_ref[h] + mm(unit_half, both))
        solved = mm(inv_ref[h], dcoef, "tn")
        dstrict = jnp.where(strict, -mm(solved, coef, "nt"), 0.0)
        dinner = jnp.where(strict, solved[:, 0:DH], 0.0).astype(BF16)
        local = mm(dstrict, unit_half) + mm(dinner, keys) + solved[:, DH : 2 * DH]
        dunit = (
            rate_col * local
            + mm(rate_col * dstrict, unit_half, "tn")
            + ddir_in_ref[h]
            - mm(coef, both, "nt")
        )
        drate_ref[h : h + 1, :] = to_row(jnp.sum(local * unit, axis=1, keepdims=True), eye)
        dkey_ref[:, lanes] = (
            dkey_in_ref[h] + mm(dinner, rate_col * unit, "tn") + dend.T
        ).astype(BF16)
        along = jnp.sum(unit * dunit, axis=1, keepdims=True)
        ddir_ref[:, lanes] = (norm_col * (dunit - unit * along)).astype(BF16)


def call(body, outs, flops, *operands, scalars=(), scratch=()):
    vmem = pl.BlockSpec(memory_space=pltpu.VMEM)
    smem = pl.BlockSpec(memory_space=pltpu.SMEM)
    moved = sum(x.size * x.dtype.itemsize for x in operands) + sum(
        jnp.dtype(d).itemsize * functools.reduce(lambda a, b: a * b, s) for s, d in outs
    )
    return pl.pallas_call(
        body,
        out_shape=[jax.ShapeDtypeStruct(s, d) for s, d in outs],
        in_specs=[vmem] * len(operands) + [smem] * len(scalars),
        out_specs=[vmem] * len(outs),
        scratch_shapes=list(scratch),
        compiler_params=pltpu.CompilerParams(vmem_limit_bytes=VMEM_LIMIT),
        cost_estimate=pl.CostEstimate(flops=flops, bytes_accessed=moved if flops else 0, transcendentals=0),
    )(*operands, *scalars)


def passed_along(value, steps):
    count = lax.axis_size("ctx")
    first, last = (max(0, -steps), min(count, count - steps))
    return lax.ppermute(value, "ctx", [(source, source + steps) for source in range(first, last)])


def paired(value, first, step):
    count = lax.axis_size("ctx")
    return lax.ppermute(value, "ctx", [(source, source + step) for source in range(first, count, 2)])


def swapped(value):
    count = lax.axis_size("ctx")
    return lax.ppermute(value, "ctx", [(source, source ^ 1) for source in range(count)])


def gathered(value, axis, groups=None):
    return lax.all_to_all(value, axis, 0, 0, axis_index_groups=groups, tiled=True)


def per_device(query, keys, values, dirs, rates, gain, doc_lengths, cotangent):
    size, width = query.shape
    heads = width // DH
    features = width * lax.axis_size("head")
    gain_row = gain.reshape(1, width)
    ctx = lax.axis_index("ctx").astype(jnp.int32)
    place = jnp.stack([ctx * size, ctx & 1])
    unit_flops = 2 * size * size * DH
    packed = pack(keys, dirs, values, rates)
    halo2 = passed_along(packed, 2)
    halo4 = passed_along(packed, 4)
    inverse, coef, raw = call(
        own_kernel,
        [((heads, size, size), BF16), ((heads, size, 2 * DH), BF16), ((heads, size, 2 * DH), F32)],
        heads * 60 * unit_flops,
        query,
        keys,
        dirs,
        rates,
    )
    own_packed, raw = lax.optimization_barrier((packed, raw))
    even = paired(own_packed, 0, 1)
    halo2, raw = lax.optimization_barrier((halo2, raw))
    cross2 = swapped(halo2)
    cross2, halo4 = lax.optimization_barrier((cross2, halo4))
    (far_carry,) = call(
        functools.partial(far_prepare_kernel, heads),
        [((2 * heads, DH, 2 * DH), F32)],
        heads * 150 * unit_flops,
        halo2,
        halo4,
    )
    halos = (halo2, halo4, even, cross2, paired(halo4, 1, -1), far_carry)
    att, total, prob, frame, carry, sums, far = call(
        functools.partial(attend_kernel, heads),
        [
            ((size, width), F32),
            ((heads, size, 8), F32),
            ((heads, WIN + 1, size, size), BF16),
            ((heads, WIN, size, DH), BF16),
            ((heads, WIN, DH, 2 * DH), BF16),
            ((lax.axis_size("head"), 1, 2 * size), F32),
            ((WIN, size, width), BF16),
        ],
        heads * 300 * unit_flops,
        raw,
        values,
        cotangent,
        gain_row,
        *halos,
        scalars=(doc_lengths, place),
        scratch=[pltpu.VMEM((size + 16, 3 * width), BF16)] * 2,
    )
    sums = gathered(sums, "head")
    count = lax.axis_size("ctx")
    normed, parts, scaled, delta, carried, send3, send4 = call(
        functools.partial(far_back_kernel, heads, features),
        [
            ((size, width), BF16),
            ((count, 1, width), F32),
            ((size, width), BF16),
            ((heads, size, 8), F32),
            ((heads, size, DH), BF16),
            ((size, 3 * width), BF16),
            ((size, 2 * width), BF16),
        ],
        heads * 15 * unit_flops,
        sums,
        att,
        total,
        prob,
        frame,
        carry,
        cotangent,
        gain_row,
        far,
    )
    recv4 = passed_along(send4, -4)
    recv3 = passed_along(send3, -3)
    parts = gathered(parts, "ctx")
    scaled, recv3, recv4 = lax.optimization_barrier((scaled, recv3, recv4))
    own, dval, send1, send2 = call(
        functools.partial(near_back_kernel, heads),
        [
            ((heads, size, 2 * DH), BF16),
            ((size, width), F32),
            ((size, 3 * width), BF16),
            ((size, 3 * width), BF16),
        ],
        heads * 3000 * unit_flops,
        scaled,
        delta,
        carried,
        prob,
        frame,
        carry,
        values,
        far,
    )
    own, parts = lax.optimization_barrier((own, parts))
    recvs = (passed_along(send1, -1), passed_along(send2, -2), recv3, recv4)
    dquery, dkey_part, ddir_part, pulled = call(
        functools.partial(local_kernel, heads),
        [
            ((size, width), BF16),
            ((heads, size, DH), F32),
            ((heads, size, DH), F32),
            ((heads, size, 2 * DH), F32),
        ],
        heads * 150 * unit_flops,
        own,
        coef,
        query,
        keys,
        dirs,
    )
    dkey, dvalue, ddir, drate, dgain = call(
        functools.partial(shard_kernel, heads),
        [((size, width), BF16), ((size, width), BF16), ((size, width), BF16), ((heads, size), F32), ((1, width), F32)],
        heads * 20 * unit_flops,
        *recvs,
        inverse,
        coef,
        pulled,
        dkey_part,
        ddir_part,
        dval,
        keys,
        dirs,
        rates,
        parts,
    )
    return normed, dquery, dkey, dvalue, ddir, drate, dgain.reshape(width)


def solution(mesh):
    rows = P("ctx", "head")
    return jax.shard_map(
        per_device,
        mesh=mesh,
        in_specs=(rows, rows, rows, rows, P("head", "ctx"), P("head"), P(), rows),
        out_specs=(rows, rows, rows, rows, rows, P("head", "ctx"), P("head")),
        check_vma=False,
    )
```

```python
import functools

import jax
import jax.numpy as jnp
from jax import lax
from jax.experimental import pallas as pl
from jax.experimental.pallas import tpu as pltpu
from jax.sharding import PartitionSpec as P

DH = 128
WIN = 4
NEG_FILL = -1e30
EPSILON = 1e-06
F32 = jnp.float32
BF16 = jnp.bfloat16
VMEM_LIMIT = 48 * 1024 * 1024


def mm(left, right, form="nn"):
    lhs = 0 if form[0] == "t" else 1
    rhs = 1 if form[1] == "t" else 0
    return lax.dot_general(
        left.astype(BF16), right.astype(BF16), (((lhs,), (rhs,)), ((), ())), preferred_element_type=F32
    )


def split(value):
    high = value.astype(BF16)
    low = (value - high.astype(F32)).astype(BF16)
    return high, low


def mm3(left, right):
    lh, ll = split(left)
    rh, rl = split(right)
    return mm(jnp.concatenate([lh, lh, ll], axis=1), jnp.concatenate([rh, rl, rh], axis=0))


def grids(size):
    rows = lax.broadcasted_iota(jnp.int32, (size, size), 0)
    cols = lax.broadcasted_iota(jnp.int32, (size, size), 1)
    return rows, cols


def to_col(row, eye):
    return jnp.sum(jnp.where(eye, row, 0.0), axis=1, keepdims=True)


def to_row(col, eye):
    return jnp.sum(jnp.where(eye, col, 0.0), axis=0, keepdims=True)


def unit_lower_inverses(strict_list):
    size = strict_list[0].shape[0]
    rows, cols = grids(size)
    eye = jnp.where(rows == cols, 1.0, 0.0)
    pair = (rows // 2 == cols // 2) & (rows > cols)
    inverses = [eye - jnp.where(pair, strict, 0.0) for strict in strict_list]
    width = 2
    while width < size:
        wide = min(4 * width, size)
        between = (rows // wide == cols // wide) & (rows // width > cols // width)
        parts = [jnp.where(between, strict, 0.0) for strict in strict_list]
        steps = [mm3(inverse, part) for inverse, part in zip(inverses, parts)]
        once = [inverse - mm3(step, inverse) for step, inverse in zip(steps, inverses)]
        if wide > 2 * width:
            twice = [mm3(step, step) for step in steps]
            inverses = [first + mm3(second, first) for first, second in zip(once, twice)]
        else:
            inverses = once
        width = wide
    return inverses


def shard_scales(dirs, rate_row, eye):
    gram = mm(dirs, dirs, "nt")
    square = jnp.where(eye, gram, 0.0)
    norm_row = lax.rsqrt(jnp.sum(square, axis=0, keepdims=True) + EPSILON)
    norm_col = lax.rsqrt(jnp.sum(square, axis=1, keepdims=True) + EPSILON)
    rate_col = to_col(rate_row, eye)
    return gram, norm_row, norm_col, rate_col


def prepare(shards):
    size = shards[0][0].shape[0]
    rows, cols = grids(size)
    eye = rows == cols
    strict = rows > cols
    grams, rights, norms = [], [], []
    for dirs, keys, rate_row in shards:
        gram, norm_row, norm_col, rate_col = shard_scales(dirs, rate_row, eye)
        scale = rate_col * norm_col
        grams.append(jnp.where(strict, gram * norm_row * scale, 0.0))
        rights.append(
            jnp.concatenate(
                [jnp.where(strict, mm(dirs, keys, "nt") * scale, 0.0), dirs.astype(F32) * scale], axis=1
            )
        )
        norms.append((norm_row, norm_col))
    inverses = unit_lower_inverses(grams)
    return [
        (inverse, mm3(inverse, right), norm) for inverse, right, norm in zip(inverses, rights, norms)
    ]


def rate_pieces(row, height, width):
    first = row.astype(BF16).astype(F32)
    rest = row - first
    second = rest.astype(BF16).astype(F32)
    third = rest - second
    at = lax.broadcasted_iota(jnp.int32, (height, width), 0)
    return jnp.where(at == 0, first, jnp.where(at == 1, second, jnp.where(at == 2, third, 0.0))).astype(BF16)


def pack_kernel(key_ref, dir_ref, value_ref, rate_ref, out_ref, rate_in, sems):
    size, width = key_ref.shape
    heads = rate_ref.shape[0]
    bring = pltpu.make_async_copy(rate_ref, rate_in, sems.at[3])
    bring.start()
    copies = [
        pltpu.make_async_copy(
            ref, out_ref.at[pl.ds(0, size), pl.ds(at * width, width)], sems.at[at]
        )
        for at, ref in enumerate((key_ref, dir_ref, value_ref))
    ]
    for copy in copies:
        copy.start()
    bring.wait()
    rate = jnp.concatenate([rate_in[h : h + 1, :] for h in range(heads)], axis=1)
    out_ref[size : size + 16, 0:width] = rate_pieces(rate, 16, width)
    out_ref[size : size + 16, width : 3 * width] = jnp.zeros((16, 2 * width), BF16)
    for copy in copies:
        copy.wait()


def pack(keys, dirs, values, rates):
    size, width = keys.shape
    return pl.pallas_call(
        pack_kernel,
        out_shape=jax.ShapeDtypeStruct((size + 16, 3 * width), BF16),
        in_specs=[pl.BlockSpec(memory_space=pl.ANY)] * 4,
        out_specs=pl.BlockSpec(memory_space=pltpu.VMEM),
        scratch_shapes=[pltpu.VMEM(rates.shape, F32), pltpu.SemaphoreType.DMA((4,))],
    )(keys, dirs, values, rates)


def own_kernel(
    query_ref, key_ref, dir_ref, rate_ref, gain_ref, len_ref, place_ref, inv_ref, kw_ref, raw_ref, gain_out_ref, start_ref
):
    size = query_ref.shape[0]
    heads = rate_ref.shape[0]
    rows, cols = grids(size)
    gain_out_ref[...] = gain_ref[...]
    pos_row = place_ref[0] + lax.broadcasted_iota(jnp.int32, (1, size), 1)
    start_row = jnp.zeros((1, size), jnp.int32)
    end = jnp.int32(0)
    for d in range(len_ref.shape[0]):
        end = end + len_ref[d]
        start_row = jnp.where(end <= pos_row, end, start_row)
    start_ref[...] = start_row.astype(F32)
    shards = []
    for h in range(heads):
        lanes = slice(h * DH, (h + 1) * DH)
        shards.append((dir_ref[:, lanes], key_ref[:, lanes], rate_ref[h : h + 1, :]))
    prepared = prepare(shards)
    for h in range(heads):
        lanes = slice(h * DH, (h + 1) * DH)
        inverse, coef, (norm_row, _) = prepared[h]
        query = query_ref[:, lanes]
        dirs, keys, _ = shards[h]
        applied = jnp.where(rows >= cols, mm(query, dirs, "nt") * norm_row, 0.0)
        base = jnp.concatenate([mm(query, keys, "nt"), query.astype(F32)], axis=1)
        raw_ref[h] = base - mm3(applied, coef)
        inv_ref[h] = inverse.astype(BF16)
        kw_ref[h] = coef.astype(BF16)


def carries(blocks, heads):
    shards = []
    for block in blocks:
        size, width = block.shape[0] - 16, heads * DH
        for h in range(heads):
            lanes = slice(h * DH, (h + 1) * DH)
            keys = block[0:size, lanes]
            dirs = block[0:size, width + h * DH : width + (h + 1) * DH]
            rate = block[size : size + 16, lanes].astype(F32)
            shards.append((dirs, keys, jnp.sum(rate, axis=0, keepdims=True)))
    rows, cols = grids(DH)
    eye = jnp.where(rows == cols, 1.0, 0.0)
    matrices = []
    for (dirs, keys, _), (_, coef, (_, norm_col)) in zip(shards, prepare(shards)):
        base = jnp.concatenate([keys.astype(F32).T, eye], axis=1)
        high, low = split(coef * norm_col)
        turned = dirs.astype(F32).T.astype(BF16)
        matrices.append(base - (mm(turned, high) + mm(turned, low)))
    return matrices


def far_prepare_kernel(heads, halo2_ref, halo4_ref, out_ref):
    for at, matrix in enumerate(carries((halo2_ref, halo4_ref), heads)):
        out_ref[at] = matrix


def attend_kernel(
    heads,
    raw_ref,
    value_ref,
    cot_ref,
    gain_ref,
    halo2_ref,
    halo4_ref,
    even_ref,
    cross2_ref,
    cross4_ref,
    far_carry_ref,
    start_ref,
    place_ref,
    att_ref,
    tot_ref,
    prob_ref,
    frame_ref,
    kt_ref,
    sums_ref,
    far_ref,
    halo1_ref,
    halo3_ref,
):
    size = value_ref.shape[0]
    width = heads * DH

    @pl.when(place_ref[1] == 0)
    def _():
        halo1_ref[...] = cross2_ref[...]
        halo3_ref[...] = cross4_ref[...]

    @pl.when(place_ref[1] != 0)
    def _():
        halo1_ref[...] = even_ref[...]
        halo3_ref[...] = cross2_ref[...]

    halos = (halo1_ref, halo2_ref, halo3_ref, halo4_ref)
    for s in range(WIN):
        far_ref[s] = halos[s][0:size, 2 * width : 3 * width]
    rows, cols = grids(size)
    eye = rows == cols
    first = place_ref[0]
    start = to_col(start_ref[...], eye).astype(jnp.int32)
    seen = [(rows >= cols) & (first + cols >= start)]
    for s in range(1, WIN + 1):
        seen.append(first - s * size + cols >= start)
    near = carries((halo1_ref, halo3_ref), heads)
    carry = near[0:heads] + [far_carry_ref[h] for h in range(heads)]
    carry = carry + near[heads : 2 * heads] + [far_carry_ref[heads + h] for h in range(heads)]
    square = jnp.zeros((size, 1), F32)
    inner = jnp.zeros((size, 1), F32)
    for h in range(heads):
        lanes = slice(h * DH, (h + 1) * DH)
        scores = [raw_ref[h, :, 0:DH]]
        frame = raw_ref[h, :, DH : 2 * DH]
        for s in range(WIN):
            matrix = carry[s * heads + h]
            kt_ref[h, s] = matrix.astype(BF16)
            frame_ref[h, s] = frame.astype(BF16)
            if s < WIN - 1:
                product = mm3(frame, matrix)
                scores.append(product[:, 0:DH])
                frame = product[:, DH : 2 * DH]
            else:
                scores.append(mm3(frame, matrix[:, 0:DH]))
        scaled = [
            jnp.where(seen[s], scores[s] * (DH ** (-0.5)), NEG_FILL) for s in range(WIN + 1)
        ]
        top = scaled[0]
        for s in range(1, WIN + 1):
            top = jnp.maximum(top, scaled[s])
        top = jnp.max(top, axis=1, keepdims=True)
        weights = [jnp.where(seen[s], jnp.exp(scaled[s] - top), 0.0) for s in range(WIN + 1)]
        total = weights[0]
        for s in range(1, WIN + 1):
            total = total + weights[s]
        total = jnp.sum(total, axis=1, keepdims=True)
        numer = None
        for s in range(WIN + 1):
            half = weights[s].astype(BF16)
            prob_ref[h, s] = half
            if s == 0:
                value = value_ref[:, lanes]
            else:
                value = halos[s - 1][0:size, 2 * width + h * DH : 2 * width + (h + 1) * DH]
            term = mm(half, value)
            numer = term if numer is None else numer + term
        att = numer / total
        att_ref[:, lanes] = att
        tot_ref[h] = jnp.broadcast_to(total, (size, 8))
        weighted = cot_ref[:, lanes].astype(F32) * gain_ref[:, lanes]
        square = square + jnp.sum(att * att, axis=1, keepdims=True)
        inner = inner + jnp.sum(weighted * att, axis=1, keepdims=True)
    row = jnp.concatenate([to_row(square, eye), to_row(inner, eye)], axis=1)
    sums_ref[...] = jnp.broadcast_to(row[None], sums_ref.shape)


def back_block(h, s, scaled, delta, prob, value, frame, matrix, carried, send):
    width = scaled.shape[1]
    lanes = slice(h * DH, (h + 1) * DH)
    through = mm(scaled[:, lanes], value, "nt")
    dscore = (prob.astype(F32) * ((through - delta) * (DH ** (-0.5)))).astype(BF16)
    send[:, lanes] = mm(prob, scaled[:, lanes], "tn").astype(send.dtype)
    if frame is None:
        return jnp.concatenate([dscore, carried], axis=1)
    at_end = slice(width + h * DH, width + (h + 1) * DH)
    at_trans = slice(2 * width + h * DH, 2 * width + (h + 1) * DH)
    if carried is None:
        send[:, at_end] = mm(frame, dscore, "tn").astype(BF16)
        return mm(dscore, matrix[:, 0:DH], "nt").astype(BF16)
    both = jnp.concatenate([dscore, carried], axis=1)
    grads = mm(frame, both, "tn").astype(BF16)
    send[:, at_end] = grads[:, 0:DH]
    send[:, at_trans] = grads[:, DH : 2 * DH]
    return mm(both, matrix, "nt").astype(BF16)


def far_back_kernel(
    heads,
    features,
    sums_ref,
    att_ref,
    tot_ref,
    prob_ref,
    frame_ref,
    kt_ref,
    cot_ref,
    gain_ref,
    far_ref,
    normed_ref,
    parts_ref,
    scaled_ref,
    delta_ref,
    carried_ref,
    send3_ref,
    send4_ref,
):
    size = att_ref.shape[0]
    rows, cols = grids(size)
    eye = rows == cols
    sums = jnp.sum(sums_ref[...], axis=0)
    square = to_col(sums[:, 0:size], eye)
    inner = to_col(sums[:, size : 2 * size], eye)
    inverse = lax.rsqrt(square / features + EPSILON)
    pull = inverse * inverse * inverse * inner / features
    att_all = att_ref[...]
    cot_all = cot_ref[...].astype(F32)
    gain = gain_ref[...]
    normed = att_all * inverse
    normed_ref[...] = (normed * gain).astype(BF16)
    part = jnp.sum(cot_all * normed, axis=0, keepdims=True)
    parts_ref[...] = jnp.broadcast_to(part[None], parts_ref.shape)
    grad_att = cot_all * gain * inverse - att_all * pull
    for h in range(heads):
        lanes = slice(h * DH, (h + 1) * DH)
        total = tot_ref[h, :, 0:1]
        grad = grad_att[:, lanes]
        scaled_ref[:, lanes] = (grad / total).astype(BF16)
        delta = jnp.sum(grad * att_all[:, lanes], axis=1, keepdims=True) / total
        delta_ref[h] = jnp.broadcast_to(delta, (size, 8))
        carried = None
        for s, send in ((4, send4_ref), (3, send3_ref)):
            carried = back_block(
                h, s, scaled_ref, delta, prob_ref[h, s], far_ref[s - 1, :, lanes], frame_ref[h, s - 1], kt_ref[h, s - 1], carried, send
            )
        carried_ref[h] = carried


def near_back_kernel(
    heads,
    scaled_ref,
    delta_ref,
    carried_ref,
    prob_ref,
    frame_ref,
    kt_ref,
    value_ref,
    far_ref,
    own_ref,
    dval_ref,
    send1_ref,
    send2_ref,
):
    for h in range(heads):
        lanes = slice(h * DH, (h + 1) * DH)
        delta = delta_ref[h, :, 0:1]
        carried = carried_ref[h]
        for s, send in ((2, send2_ref), (1, send1_ref)):
            carried = back_block(
                h, s, scaled_ref, delta, prob_ref[h, s], far_ref[s - 1, :, lanes], frame_ref[h, s - 1], kt_ref[h, s - 1], carried, send
            )
        own_ref[h] = back_block(
            h, 0, scaled_ref, delta, prob_ref[h, 0], value_ref[:, lanes], None, None, carried, dval_ref
        )


def local_kernel(heads, own_ref, kw_ref, query_ref, key_ref, dir_ref, dquery_ref, dkey_ref, ddir_ref, pulled_ref):
    size = query_ref.shape[0]
    rows, cols = grids(size)
    eye = rows == cols
    lower = rows >= cols
    for h in range(heads):
        lanes = slice(h * DH, (h + 1) * DH)
        query = query_ref[:, lanes]
        keys = key_ref[:, lanes]
        raw_dirs = dir_ref[:, lanes].astype(F32)
        norm_col = lax.rsqrt(jnp.sum(raw_dirs * raw_dirs, axis=1, keepdims=True) + EPSILON)
        unit = (raw_dirs * norm_col).astype(BF16)
        grads = own_ref[h]
        applied = jnp.where(lower, mm(query, unit, "nt"), 0.0).astype(BF16)
        dapplied = jnp.where(lower, mm(grads, kw_ref[h], "nt"), 0.0).astype(BF16)
        dquery = mm(grads[:, 0:DH], keys) + grads[:, DH : 2 * DH].astype(F32) - mm(dapplied, unit)
        dquery_ref[:, lanes] = dquery.astype(BF16)
        dkey_ref[h] = mm(grads[:, 0:DH], query, "tn")
        ddir_ref[h] = -mm(dapplied, query, "tn")
        pulled_ref[h] = mm(applied, grads, "tn")


def shard_kernel(
    heads,
    recv1_ref,
    recv2_ref,
    recv3_ref,
    recv4_ref,
    inv_ref,
    kw_ref,
    pulled_ref,
    dkey_in_ref,
    ddir_in_ref,
    dval_in_ref,
    key_ref,
    dir_ref,
    rate_ref,
    parts_ref,
    dkey_ref,
    dvalue_ref,
    ddir_ref,
    drate_ref,
    dgain_ref,
):
    size = key_ref.shape[0]
    width = heads * DH
    recvs = (recv1_ref, recv2_ref, recv3_ref, recv4_ref)
    rows, cols = grids(size)
    eye = rows == cols
    strict = rows > cols
    dvalue = dval_in_ref[...]
    for recv in recvs:
        dvalue = dvalue + recv[:, 0:width].astype(F32)
    dvalue_ref[...] = dvalue.astype(BF16)
    dgain_ref[...] = jnp.sum(parts_ref[...], axis=0)
    for h in range(heads):
        lanes = slice(h * DH, (h + 1) * DH)
        keys = key_ref[:, lanes]
        raw_dirs = dir_ref[:, lanes].astype(F32)
        norm_col = lax.rsqrt(jnp.sum(raw_dirs * raw_dirs, axis=1, keepdims=True) + EPSILON)
        unit = raw_dirs * norm_col
        unit_half = unit.astype(BF16)
        rate_col = to_col(rate_ref[h : h + 1, :], eye)
        dend = jnp.zeros((size, DH), F32)
        dtrans = jnp.zeros((size, DH), F32)
        for recv in recvs:
            dend = dend + recv[:, width + h * DH : width + (h + 1) * DH].astype(F32)
            if recv.shape[1] == 3 * width:
                dtrans = dtrans + recv[:, 2 * width + h * DH : 2 * width + (h + 1) * DH].astype(F32)
        both = jnp.concatenate([dend, dtrans], axis=1).astype(BF16)
        coef = kw_ref[h]
        dcoef = -(pulled_ref[h] + mm(unit_half, both))
        solved = mm(inv_ref[h], dcoef, "tn")
        dstrict = jnp.where(strict, -mm(solved, coef, "nt"), 0.0)
        dinner = jnp.where(strict, solved[:, 0:DH], 0.0).astype(BF16)
        local = mm(dstrict, unit_half) + mm(dinner, keys) + solved[:, DH : 2 * DH]
        dunit = (
            rate_col * local
            + mm(rate_col * dstrict, unit_half, "tn")
            + ddir_in_ref[h]
            - mm(coef, both, "nt")
        )
        drate_ref[h : h + 1, :] = to_row(jnp.sum(local * unit, axis=1, keepdims=True), eye)
        dkey_ref[:, lanes] = (
            dkey_in_ref[h] + mm(dinner, rate_col * unit, "tn") + dend.T
        ).astype(BF16)
        along = jnp.sum(unit * dunit, axis=1, keepdims=True)
        ddir_ref[:, lanes] = (norm_col * (dunit - unit * along)).astype(BF16)


def call(body, outs, flops, *operands, scalars=(), scratch=()):
    vmem = pl.BlockSpec(memory_space=pltpu.VMEM)
    smem = pl.BlockSpec(memory_space=pltpu.SMEM)
    moved = sum(x.size * x.dtype.itemsize for x in operands) + sum(
        jnp.dtype(d).itemsize * functools.reduce(lambda a, b: a * b, s) for s, d in outs
    )
    return pl.pallas_call(
        body,
        out_shape=[jax.ShapeDtypeStruct(s, d) for s, d in outs],
        in_specs=[vmem] * len(operands) + [smem] * len(scalars),
        out_specs=[vmem] * len(outs),
        scratch_shapes=list(scratch),
        compiler_params=pltpu.CompilerParams(vmem_limit_bytes=VMEM_LIMIT),
        cost_estimate=pl.CostEstimate(flops=flops, bytes_accessed=moved if flops else 0, transcendentals=0),
    )(*operands, *scalars)


def passed_along(value, steps):
    count = lax.axis_size("ctx")
    first, last = (max(0, -steps), min(count, count - steps))
    return lax.ppermute(value, "ctx", [(source, source + steps) for source in range(first, last)])


def paired(value, first, step):
    count = lax.axis_size("ctx")
    return lax.ppermute(value, "ctx", [(source, source + step) for source in range(first, count, 2)])


def swapped(value):
    count = lax.axis_size("ctx")
    return lax.ppermute(value, "ctx", [(source, source ^ 1) for source in range(count)])


def gathered(value, axis, groups=None):
    return lax.all_to_all(value, axis, 0, 0, axis_index_groups=groups, tiled=True)


def per_device(query, keys, values, dirs, rates, gain, doc_lengths, cotangent):
    size, width = query.shape
    heads = width // DH
    features = width * lax.axis_size("head")
    gain_row = gain.reshape(1, width)
    ctx = lax.axis_index("ctx").astype(jnp.int32)
    place = jnp.stack([ctx * size, ctx & 1])
    unit_flops = 2 * size * size * DH
    packed = pack(keys, dirs, values, rates)
    halo2 = passed_along(packed, 2)
    halo4 = passed_along(packed, 4)
    inverse, coef, raw, gain_row, start_row = call(
        own_kernel,
        [((heads, size, size), BF16), ((heads, size, 2 * DH), BF16), ((heads, size, 2 * DH), F32), ((1, width), F32), ((1, size), F32)],
        heads * 60 * unit_flops,
        query,
        keys,
        dirs,
        rates,
        gain_row,
        scalars=(doc_lengths, place),
    )
    own_packed, raw = lax.optimization_barrier((packed, raw))
    even = paired(own_packed, 0, 1)
    halo2, raw = lax.optimization_barrier((halo2, raw))
    cross2 = swapped(halo2)
    cross2, halo4 = lax.optimization_barrier((cross2, halo4))
    (far_carry,) = call(
        functools.partial(far_prepare_kernel, heads),
        [((2 * heads, DH, 2 * DH), F32)],
        heads * 150 * unit_flops,
        halo2,
        halo4,
    )
    halos = (halo2, halo4, even, cross2, paired(halo4, 1, -1), far_carry, start_row)
    att, total, prob, frame, carry, sums, far = call(
        functools.partial(attend_kernel, heads),
        [
            ((size, width), F32),
            ((heads, size, 8), F32),
            ((heads, WIN + 1, size, size), BF16),
            ((heads, WIN, size, DH), BF16),
            ((heads, WIN, DH, 2 * DH), BF16),
            ((lax.axis_size("head"), 1, 2 * size), F32),
            ((WIN, size, width), BF16),
        ],
        heads * 300 * unit_flops,
        raw,
        values,
        cotangent,
        gain_row,
        *halos,
        scalars=(place,),
        scratch=[pltpu.VMEM((size + 16, 3 * width), BF16)] * 2,
    )
    sums = gathered(sums, "head")
    count = lax.axis_size("ctx")
    normed, parts, scaled, delta, carried, send3, send4 = call(
        functools.partial(far_back_kernel, heads, features),
        [
            ((size, width), BF16),
            ((count, 1, width), F32),
            ((size, width), BF16),
            ((heads, size, 8), F32),
            ((heads, size, DH), BF16),
            ((size, 3 * width), BF16),
            ((size, 2 * width), BF16),
        ],
        heads * 15 * unit_flops,
        sums,
        att,
        total,
        prob,
        frame,
        carry,
        cotangent,
        gain_row,
        far,
    )
    recv4 = passed_along(send4, -4)
    recv3 = passed_along(send3, -3)
    parts = gathered(parts, "ctx")
    scaled, recv3, recv4 = lax.optimization_barrier((scaled, recv3, recv4))
    own, dval, send1, send2 = call(
        functools.partial(near_back_kernel, heads),
        [
            ((heads, size, 2 * DH), BF16),
            ((size, width), F32),
            ((size, 3 * width), BF16),
            ((size, 3 * width), BF16),
        ],
        heads * 3000 * unit_flops,
        scaled,
        delta,
        carried,
        prob,
        frame,
        carry,
        values,
        far,
    )
    own, parts = lax.optimization_barrier((own, parts))
    recv2 = passed_along(send2, -2)
    recvs = (passed_along(send1, -1), recv2, recv3, recv4)
    dquery, dkey_part, ddir_part, pulled = call(
        functools.partial(local_kernel, heads),
        [
            ((size, width), BF16),
            ((heads, size, DH), F32),
            ((heads, size, DH), F32),
            ((heads, size, 2 * DH), F32),
        ],
        heads * 150 * unit_flops,
        own,
        coef,
        query,
        keys,
        dirs,
    )
    dkey, dvalue, ddir, drate, dgain = call(
        functools.partial(shard_kernel, heads),
        [((size, width), BF16), ((size, width), BF16), ((size, width), BF16), ((heads, size), F32), ((1, width), F32)],
        heads * 20 * unit_flops,
        *recvs,
        inverse,
        coef,
        pulled,
        dkey_part,
        ddir_part,
        dval,
        keys,
        dirs,
        rates,
        parts,
    )
    return normed, dquery, dkey, dvalue, ddir, drate, dgain.reshape(width)


def solution(mesh):
    rows = P("ctx", "head")
    return jax.shard_map(
        per_device,
        mesh=mesh,
        in_specs=(rows, rows, rows, rows, P("head", "ctx"), P("head"), P(), rows),
        out_specs=(rows, rows, rows, rows, rows, P("head", "ctx"), P("head")),
        check_vma=False,
    )
```
